32 devices in a mesh: rows: 4 (over y, x), seq: 8 (over z, core).
Axes of the slice: x: 2, y: 2, z: 4, core: 2. Of those that a mesh axis runs over, the one named last changes fastest.
Arguments:
- inputs: bfloat16 [8, 2048, 768], P('rows', 'seq'), may hold values from -6 to 6
- doc_lengths: int32 [8, 2], P('rows'), may hold values from 0 to 2048, as said below
- w_query: bfloat16 [768, 768], replicated, may hold values from -0.0546875 to 0.0546875
- w_key: bfloat16 [768, 768], replicated, may hold values from -0.21875 to 0.21875
- w_value: bfloat16 [768, 768], replicated, may hold values from -0.21875 to 0.21875
- w_out: bfloat16 [768, 768], replicated, may hold values from -1.25 to 1.25
- w_in: bfloat16 [768, 3072], replicated, may hold values from -0.21875 to 0.21875
- w_ffout: bfloat16 [3072, 768], replicated, may hold values from -0.109375 to 0.109375
- rel_table: float32 [32, 12], replicated, may hold values from -4 to 4
- gain_attn: float32 [768], replicated, may hold values from 0.25 to 1.75
- gain_ffn: float32 [768], replicated, may hold values from 0.25 to 1.75
- phm_rule: float32 [4, 4, 4], replicated, may hold values from -4 to 4
- down_left: float32 [4, 192], replicated, may hold values from -0.109375 to 0.109375
- down_right: float32 [4, 12], replicated, may hold values from -4 to 4
- up_left: float32 [4, 12], replicated, may hold values from -4 to 4
- up_right: float32 [4, 192], replicated, may hold values from -0.4375 to 0.4375
- down_bias: float32 [48], replicated, may hold values from -3 to 3
- up_bias: float32 [768], replicated, may hold values from -2 to 2
- cotangent: bfloat16 [8, 2048, 768], P('rows', 'seq'), may hold values from -10 to 10
Outputs:
- output: bfloat16 [8, 2048, 768], P('rows', 'seq')
- input_grad: bfloat16 [8, 2048, 768], P('rows', 'seq')
- rule_grad: float32 [4, 4, 4], replicated
- down_left_grad: float32 [4, 192], replicated
- down_right_grad: float32 [4, 12], replicated
- up_left_grad: float32 [4, 12], replicated
- up_right_grad: float32 [4, 192], replicated
- down_bias_grad: float32 [48], replicated
- up_bias_grad: float32 [768], replicated
The draws below stay inside these ranges and needn't reach their ends.
Inputs may be any that keep to these rules, and one draw needn't show every extreme that they name: `doc_lengths`: each row's nonzero lengths come first, are at least 1024 and add up to 2048; the rest are 0. In each aligned block of 2 rows that one index of rows holds, exactly one row is a single document; every other row holds two documents or more.
All inputs are finite; a program needn't handle non-finite values.
Results may differ from the reference program's by a relative error of at most 0.035.
Values may be sent and summed in bfloat16 or wider, within the bound.
A program may use at most 256 MiB of HBM per device.

```python
import jax
import jax.numpy as jnp
from jax import lax

MODEL_DIM = 768
H = 12
DH = 64
FF = 3072
BUCKETS = 32
ADAPT = 48
PHM = 4
SHORTEST_DOC = 1024
ROWS_DEV = 2
ROW_TOKENS = 2048
PACKED_ROWS = 8
NDOC = 2


def draw_doc_lengths(key, part):
    key = jax.random.fold_in(key, 5)
    count_key, cut_key, full_key = jax.random.split(key, 3)
    document_count_list = jax.random.randint(count_key, (PACKED_ROWS,), 2, NDOC + 1)
    chosen = jax.random.randint(full_key, (PACKED_ROWS // ROWS_DEV,), 0, ROWS_DEV)
    row_index = jnp.arange(PACKED_ROWS)
    document_count_list = jnp.where(row_index % ROWS_DEV == jnp.repeat(chosen, ROWS_DEV), 1, document_count_list)
    remaining_tokens = ROW_TOKENS - document_count_list * SHORTEST_DOC
    cut_points = jax.random.randint(cut_key, (PACKED_ROWS, NDOC - 1), 0, remaining_tokens[:, None] + 1)
    slot_index = jnp.arange(NDOC - 1)
    cut_points = jnp.where(slot_index[None, :] < document_count_list[:, None] - 1, cut_points, remaining_tokens[:, None])
    cut_points = jnp.sort(cut_points, axis=1)
    boundary = jnp.concatenate([jnp.zeros((PACKED_ROWS, 1), jnp.int32), cut_points.astype(jnp.int32), remaining_tokens[:, None].astype(jnp.int32)], axis=1)
    doc_spans = boundary[:, 1:] - boundary[:, :-1]
    return jnp.where(jnp.arange(NDOC)[None, :] < document_count_list[:, None], doc_spans + SHORTEST_DOC, 0).astype(jnp.int32)


def draw_cotangent(key, part):
    key = jax.random.fold_in(key, 9)
    root_random_key = jax.random.fold_in(key, 0)
    running_offset = jnp.arange(ROW_TOKENS, dtype=jnp.float32) / ROW_TOKENS
    across = jnp.arange(PACKED_ROWS, dtype=jnp.float32) / PACKED_ROWS
    random_jitter = jax.random.truncated_normal(root_random_key, -4.0, 4.0, (PACKED_ROWS, ROW_TOKENS, MODEL_DIM), jnp.float32)
    factor = (0.5 + running_offset)[None, :, None] * (0.5 + across)[:, None, None]
    return (random_jitter * factor).astype(jnp.bfloat16)


def block_levels(key, extent, cuts, least, top_value):
    level, own = 1.0, jax.random.fold_in(key, 6)
    for position, parts in cuts:
        draws = jnp.exp(jax.random.uniform(jax.random.fold_in(own, position), (parts,), jnp.float32, least / len(cuts), top_value / len(cuts)))
        level = level * jnp.repeat(draws, extent[position] // parts).reshape([-1 if axis == position else 1 for axis in range(len(extent))])
    return level


def gaussian(rng, dims, scale, most, shards=(), kind=jnp.bfloat16):
    level = block_levels(rng, dims, shards, -0.22, 0.18) if shards else 1.0
    values = jax.random.normal(rng, dims, jnp.float32) * scale * level
    return jnp.minimum(jnp.maximum(values, -most), most).astype(kind)


def setup_inputs(seed: int = 0) -> dict:
    streams_of = jax.random.split(jax.random.key(seed), 20)
    return {
        "inputs": gaussian(streams_of[0], (PACKED_ROWS, ROW_TOKENS, MODEL_DIM), 1.0, 6.0, ((0, 4), (1, 8))),
        "doc_lengths": draw_doc_lengths(jax.random.fold_in(streams_of[19], 71), 0),
        "w_query": gaussian(streams_of[2], (MODEL_DIM, MODEL_DIM), (16 * MODEL_DIM) ** -0.5, 0.0546875),
        "w_key": gaussian(streams_of[3], (MODEL_DIM, MODEL_DIM), MODEL_DIM ** -0.5, 0.21875),
        "w_value": gaussian(streams_of[4], (MODEL_DIM, MODEL_DIM), MODEL_DIM ** -0.5, 0.21875),
        "w_out": gaussian(streams_of[5], (MODEL_DIM, MODEL_DIM), (MODEL_DIM // 32) ** -0.5, 1.25),
        "w_in": gaussian(streams_of[6], (MODEL_DIM, FF), MODEL_DIM ** -0.5, 0.21875),
        "w_ffout": gaussian(streams_of[7], (FF, MODEL_DIM), FF ** -0.5, 0.109375),
        "rel_table": gaussian(streams_of[8], (BUCKETS, H), 1.0, 4.0, (), jnp.float32),
        "gain_attn": jnp.clip(1.0 + 0.15 * jax.random.normal(streams_of[9], (MODEL_DIM,), jnp.float32), 0.25, 1.75),
        "gain_ffn": jnp.clip(1.0 + 0.15 * jax.random.normal(streams_of[10], (MODEL_DIM,), jnp.float32), 0.25, 1.75),
        "phm_rule": gaussian(streams_of[11], (PHM, PHM, PHM), 1.0, 4.0, (), jnp.float32),
        "down_left": gaussian(streams_of[12], (PHM, MODEL_DIM // PHM), (PHM * MODEL_DIM) ** -0.5, 0.109375, (), jnp.float32),
        "down_right": gaussian(streams_of[13], (PHM, ADAPT // PHM), 1.0, 4.0, (), jnp.float32),
        "up_left": gaussian(streams_of[14], (PHM, ADAPT // PHM), 1.0, 4.0, (), jnp.float32),
        "up_right": gaussian(streams_of[15], (PHM, MODEL_DIM // PHM), (PHM * ADAPT) ** -0.5, 0.4375, (), jnp.float32),
        "down_bias": gaussian(streams_of[16], (ADAPT,), 0.5, 3.0, (), jnp.float32),
        "up_bias": gaussian(streams_of[17], (MODEL_DIM,), 0.3, 2.0, (), jnp.float32),
        "cotangent": draw_cotangent(jax.random.fold_in(streams_of[19], 71), 0),
    }


@jax.custom_vjp
def low(v):
    return lax.optimization_barrier(v.astype(jnp.bfloat16)).astype(jnp.float32)

@jax.custom_vjp
def low_back(v):
    return v

def low_keep(v):
    return (low(v), None)

def low_pass(kept, grad):
    return (grad,)

def back_keep(v):
    return (v, None)

def back_low(kept, grad):
    return (low(grad),)
low.defvjp(low_keep, low_pass)
low_back.defvjp(back_keep, back_low)
epsilon = 1e-06
highest = lax.Precision.HIGHEST
bucket_edges = (12, 16, 23, 32, 46, 64, 91)

def smooth_gelu(values):
    return 0.5 * values * (1.0 + jnp.tanh(0.7978845608028654 * (values + 0.044715 * values * values * values)))

def rms_norm(values, gain):
    return values * lax.rsqrt(lax.optimization_barrier(jnp.mean(values * values, axis=-1, keepdims=True)) + epsilon) * gain

def bucket_of(offset):
    magnitude = jnp.abs(offset)
    larger = jnp.full(offset.shape, 8, jnp.int32)
    for edge in bucket_edges:
        larger = larger + (magnitude >= edge).astype(jnp.int32)
    inside = jnp.where(magnitude < 8, magnitude, larger)
    return inside + jnp.where(offset > 0, 16, 0).astype(jnp.int32)

def segment_ids(lengths, token_positions):
    doc_ends = jnp.cumsum(lengths, axis=-1, dtype=jnp.int32)
    return lax.optimization_barrier(jnp.sum((token_positions[..., :, None] >= doc_ends[..., None, :]).astype(jnp.int32), axis=-1, dtype=jnp.int32))

def kron_sum(rule_part, left_part, right_part):
    blocks = jnp.einsum('iab,ip,iq->apbq', rule_part, left_part, right_part, precision=highest)
    return blocks.reshape(rule_part.shape[1] * left_part.shape[1], rule_part.shape[2] * right_part.shape[1])

def attend_row(queries, key_rows, value_rows, row_segments, rel_table):
    total_len = queries.shape[0]
    block_len = min(512, total_len)
    token_positions = jnp.arange(total_len, dtype=jnp.int32)

    @jax.checkpoint
    def one_block(block_index):
        first_row = block_index * block_len
        query_block = lax.dynamic_slice_in_dim(queries, first_row, block_len, 0)
        query_pos = first_row + jnp.arange(block_len, dtype=jnp.int32)
        query_seg = lax.dynamic_slice_in_dim(row_segments, first_row, block_len, 0)
        scores = jnp.einsum('qhd,khd->hqk', query_block, key_rows, precision=highest)
        buckets = bucket_of(token_positions[None, :] - query_pos[:, None])
        scores = low_back(scores + jnp.transpose(rel_table[buckets], (2, 0, 1)))
        allowed = (query_seg[:, None] == row_segments[None, :])[None]
        scores = jnp.where(allowed, scores, -1e+30)
        row_peak = lax.optimization_barrier(jnp.max(scores, axis=-1, keepdims=True))
        exponent = jnp.exp(scores - row_peak)
        weights = exponent / lax.optimization_barrier(jnp.sum(exponent, axis=-1, keepdims=True))
        return jnp.einsum('hqk,khd->qhd', low(weights), value_rows, precision=highest)
    blocks = lax.map(one_block, jnp.arange(total_len // block_len, dtype=jnp.int32))
    return blocks.reshape(queries.shape)

def dense(left_part, right_part):
    return jnp.dot(left_part, right_part, precision=highest)

def layer(inputs, phm_rule, down_left, down_right, up_left, up_right, down_bias, up_bias, frozen, segments):
    w_query, w_key, w_value, w_out, w_in, w_ffout, rel_table, gain_attn, gain_ffn = frozen
    down_matrix = low(kron_sum(phm_rule, down_left, down_right))
    up_matrix = low(kron_sum(phm_rule, up_left, up_right))

    def one_row(row_pair):
        row_input, row_segments = row_pair
        total_len = row_input.shape[0]
        normed = low(rms_norm(row_input, gain_attn))
        queries = low_back(low(dense(normed, w_query)))
        key_rows = low_back(low(dense(normed, w_key)))
        value_rows = low_back(low(dense(normed, w_value)))
        attended = attend_row(queries.reshape(total_len, H, DH), key_rows.reshape(total_len, H, DH), value_rows.reshape(total_len, H, DH), row_segments, rel_table)
        attended = low_back(low(attended.reshape(total_len, MODEL_DIM)))
        hidden = row_input + low_back(dense(attended, w_out))
        normed_ffn = low(rms_norm(hidden, gain_ffn))
        inner = low_back(dense(normed_ffn, w_in))
        ff_out = low(low_back(dense(low(smooth_gelu(inner)), w_ffout)))
        squeezed = low_back(dense(ff_out, down_matrix)) + down_bias
        expanded = low_back(dense(low(smooth_gelu(squeezed)), up_matrix)) + up_bias
        return hidden + ff_out + expanded
    return lax.map(one_row, (inputs, segments))

def reference(inputs, doc_lengths, w_query, w_key, w_value, w_out, w_in, w_ffout, rel_table, gain_attn, gain_ffn, phm_rule, down_left, down_right, up_left, up_right, down_bias, up_bias, cotangent):
    token_positions = jnp.arange(ROW_TOKENS, dtype=jnp.int32)
    segments = segment_ids(doc_lengths, token_positions[None, :])
    frozen = (w_query.astype(jnp.float32), w_key.astype(jnp.float32), w_value.astype(jnp.float32), w_out.astype(jnp.float32), w_in.astype(jnp.float32), w_ffout.astype(jnp.float32), rel_table.astype(jnp.float32), gain_attn.astype(jnp.float32), gain_ffn.astype(jnp.float32))

    def wrapped(inputs_f, rule_part, dl_part, dr_part, ul_part, ur_part, db_part, ub_part):
        return layer(inputs_f, rule_part, dl_part, dr_part, ul_part, ur_part, db_part, ub_part, frozen, segments)
    result, pullback = jax.vjp(wrapped, inputs.astype(jnp.float32), phm_rule, down_left, down_right, up_left, up_right, down_bias, up_bias)
    grads = pullback(cotangent.astype(jnp.float32))
    return (result.astype(jnp.bfloat16), grads[0].astype(jnp.bfloat16), grads[1], grads[2], grads[3], grads[4], grads[5], grads[6], grads[7])
```

```python
import functools
import math

import jax
import jax.numpy as jnp
from jax import lax
from jax.experimental import pallas as pl
from jax.experimental.pallas import tpu as pltpu
from jax.sharding import PartitionSpec as P

epsilon = 1e-06
highest = lax.Precision.HIGHEST
bucket_edges = (12, 16, 23, 32, 46, 64, 91)


def smooth_gelu(values):
    return (
        0.5
        * values
        * (1.0 + jnp.tanh(0.7978845608028654 * (values + 0.044715 * values * values * values)))
    )


def rms_norm(values, gain):
    return values * lax.rsqrt(jnp.mean(values * values, axis=-1, keepdims=True) + epsilon) * gain


def bucket_of(offset):
    magnitude = jnp.abs(offset)
    larger = jnp.full(offset.shape, 8, jnp.int32)
    for edge in bucket_edges:
        larger = larger + (magnitude >= edge).astype(jnp.int32)
    inside = jnp.where(magnitude < 8, magnitude, larger)
    return inside + jnp.where(offset > 0, 16, 0).astype(jnp.int32)


def segment_ids(lengths, token_positions):
    doc_ends = jnp.cumsum(lengths, axis=-1, dtype=jnp.int32)
    return jnp.sum(
        (token_positions[..., :, None] >= doc_ends[..., None, :]).astype(jnp.int32),
        axis=-1,
        dtype=jnp.int32,
    )


def kron_sum(rule_part, left_part, right_part):
    blocks = jnp.einsum("iab,ip,iq->apbq", rule_part, left_part, right_part, precision=highest)
    return blocks.reshape(
        rule_part.shape[1] * left_part.shape[1], rule_part.shape[2] * right_part.shape[1]
    )


def pair_bias(query_pos, key_pos, rel_table):
    buckets = bucket_of(key_pos[None, :] - query_pos[:, None])
    onehot = (buckets[:, :, None] == jnp.arange(rel_table.shape[0], dtype=jnp.int32)).astype(
        jnp.bfloat16
    )
    table_high = rel_table.astype(jnp.bfloat16)
    table_rest = (rel_table - table_high.astype(jnp.float32)).astype(jnp.bfloat16)
    high_part = jnp.einsum("qkb,bh->qhk", onehot, table_high, preferred_element_type=jnp.float32)
    rest_part = jnp.einsum("qkb,bh->qhk", onehot, table_rest, preferred_element_type=jnp.float32)
    return high_part + rest_part


def over_blocks(carried, pieces, blockwise):
    total_len = pieces[0].shape[1]
    block_len = math.gcd(total_len, 512)

    def one_step(block_index, inner_state):
        begin_row = block_index * block_len
        sliced = tuple(
            (lax.dynamic_slice_in_dim(member, begin_row, block_len, 1) for member in pieces)
        )
        return blockwise(inner_state, sliced, begin_row)

    return lax.fori_loop(0, total_len // block_len, one_step, carried)


def local(
    inputs,
    doc_lengths,
    w_query,
    w_key,
    w_value,
    w_out,
    w_in,
    w_ffout,
    rel_table,
    gain_attn,
    gain_ffn,
    phm_rule,
    down_left,
    down_right,
    up_left,
    up_right,
    down_bias,
    up_bias,
    cotangent,
):
    row_count, length, model_width = inputs.shape
    head_count = rel_table.shape[1]
    head_dim = model_width // head_count
    seq_place = lax.axis_index("seq")
    token_count = row_count * length
    local_pos = seq_place * length + jnp.arange(length, dtype=jnp.int32)
    local_seg = segment_ids(doc_lengths, local_pos[None, :])
    bf16 = jnp.bfloat16
    f32 = jnp.float32

    def heads_of(matrix, block_len):
        return matrix.reshape(row_count, block_len, head_count, head_dim)

    def norm_attn(values):
        return rms_norm(values, gain_attn)

    def norm_ffn(values):
        return rms_norm(values, gain_ffn)

    source = inputs.astype(f32).reshape(token_count, model_width)
    normed, norm_attn_back = jax.vjp(norm_attn, source)
    normed_b = normed.astype(bf16)
    queries = (
        jnp.dot(normed_b, w_query, preferred_element_type=f32)
        .astype(bf16)
        .reshape(row_count, length, model_width)
    )
    key_rows = (
        jnp.dot(normed_b, w_key, preferred_element_type=f32)
        .astype(bf16)
        .reshape(row_count, length, model_width)
    )
    value_rows = (
        jnp.dot(normed_b, w_value, preferred_element_type=f32)
        .astype(bf16)
        .reshape(row_count, length, model_width)
    )
    queries_h = heads_of(queries, length)
    keys_h = heads_of(key_rows, length)
    values_h = heads_of(value_rows, length)

    def scores_for(query_h, query_pos, query_seg, key_h, key_pos, key_seg):
        scores = jnp.einsum("rqhd,rkhd->rqhk", query_h, key_h, preferred_element_type=f32)
        scores = scores + pair_bias(query_pos, key_pos, rel_table)[None]
        allowed = (query_seg[:, :, None] == key_seg[:, None, :])[:, :, None, :]
        return (scores, allowed)

    def forward_piece(carried, pieces, first_row):
        weighted, running, mass_sum = carried
        key_part, value_part = pieces
        block_len = key_part.shape[1]
        key_pos = first_row + jnp.arange(block_len, dtype=jnp.int32)
        key_seg = segment_ids(doc_lengths, key_pos[None, :])
        scores, allowed = scores_for(
            queries_h, local_pos, local_seg, heads_of(key_part, block_len), key_pos, key_seg
        )
        scores = jnp.where(allowed, scores, -1e30)
        raised = jnp.maximum(running, jnp.max(scores, axis=-1))
        weights = jnp.where(allowed, jnp.exp(scores - raised[..., None]), 0.0)
        rescale = jnp.exp(running - raised)
        mass_sum = mass_sum * rescale + jnp.sum(weights, axis=-1)
        weighted = weighted * rescale[..., None] + jnp.einsum(
            "rqhk,rkhd->rqhd",
            weights.astype(bf16),
            heads_of(value_part, block_len),
            preferred_element_type=f32,
        )
        return (weighted, raised, mass_sum)

    start_state = (
        jnp.zeros((row_count, length, head_count, head_dim), f32),
        jnp.full((row_count, length, head_count), -1e30, f32),
        jnp.zeros((row_count, length, head_count), f32),
    )
    weighted, running, mass_sum = over_blocks(
        start_state,
        (
            lax.all_gather(key_rows, "seq", axis=1, tiled=True),
            lax.all_gather(value_rows, "seq", axis=1, tiled=True),
        ),
        forward_piece,
    )
    attended = weighted / mass_sum[..., None]
    log_mass = running + jnp.log(mass_sum)
    attended_b = attended.astype(bf16).reshape(token_count, model_width)
    hidden = source + jnp.dot(attended_b, w_out, preferred_element_type=f32)
    normed_ffn, norm_ffn_back = jax.vjp(norm_ffn, hidden)
    inner = jnp.dot(normed_ffn.astype(bf16), w_in, preferred_element_type=f32)
    activated, gelu_back = jax.vjp(smooth_gelu, inner)
    activated_b = activated.astype(bf16)
    ff_out = jnp.dot(activated_b, w_ffout, preferred_element_type=f32).astype(bf16)
    down_full, down_back = jax.vjp(kron_sum, phm_rule, down_left, down_right)
    up_full, up_back = jax.vjp(kron_sum, phm_rule, up_left, up_right)
    down_b = down_full.astype(bf16)
    up_b = up_full.astype(bf16)
    squeezed = jnp.dot(ff_out, down_b, preferred_element_type=f32) + down_bias
    squeezed_act, squeeze_back = jax.vjp(smooth_gelu, squeezed)
    squeezed_act_b = squeezed_act.astype(bf16)
    expanded = jnp.dot(squeezed_act_b, up_b, preferred_element_type=f32) + up_bias
    result = hidden + ff_out.astype(f32) + expanded
    output = result.astype(bf16).reshape(row_count, length, model_width)
    upstream = cotangent.astype(f32).reshape(token_count, model_width)
    up_bias_grad = jnp.sum(upstream, axis=0)
    upstream_b = upstream.astype(bf16)
    up_matrix_grad = jnp.einsum("ta,td->ad", squeezed_act_b, upstream_b, preferred_element_type=f32)
    squeezed_grad = squeeze_back(
        jnp.einsum("td,ad->ta", upstream_b, up_b, preferred_element_type=f32)
    )[0]
    down_bias_grad = jnp.sum(squeezed_grad, axis=0)
    squeezed_low = squeezed_grad.astype(bf16)
    down_matrix_grad = jnp.einsum("td,ta->da", ff_out, squeezed_low, preferred_element_type=f32)
    rule_down, down_left_grad, down_right_grad = down_back(down_matrix_grad)
    rule_up, up_left_grad, up_right_grad = up_back(up_matrix_grad)
    summed = lax.psum(
        (
            rule_down + rule_up,
            down_left_grad,
            down_right_grad,
            up_left_grad,
            up_right_grad,
            down_bias_grad,
            up_bias_grad,
        ),
        ("rows", "seq"),
    )
    ff_grad = upstream + jnp.einsum("ta,da->td", squeezed_low, down_b, preferred_element_type=f32)
    ff_grad_b = ff_grad.astype(bf16)
    inner_grad = gelu_back(jnp.einsum("td,fd->tf", ff_grad_b, w_ffout, preferred_element_type=f32))[
        0
    ]
    inner_grad_b = inner_grad.astype(bf16)
    hidden_grad = (
        upstream
        + norm_ffn_back(jnp.einsum("tf,df->td", inner_grad_b, w_in, preferred_element_type=f32))[0]
    )
    hidden_grad_b = hidden_grad.astype(bf16)
    attended_grad = jnp.einsum(
        "te,de->td", hidden_grad_b, w_out, preferred_element_type=f32
    ).astype(bf16)
    attended_grad = attended_grad.reshape(row_count, length, model_width)
    attended_grad_h = heads_of(attended_grad, length)
    row_delta = jnp.sum(attended_grad_h.astype(f32) * attended, axis=-1)

    def gradient_terms(
        query_h,
        query_pos,
        query_seg,
        grad_h,
        mass_part,
        delta_part,
        key_h,
        value_h,
        key_pos,
        key_seg,
    ):
        scores, allowed = scores_for(query_h, query_pos, query_seg, key_h, key_pos, key_seg)
        weights = jnp.exp(jnp.where(allowed, scores - mass_part[..., None], -1e30))
        weights_grad = jnp.einsum("rqhd,rkhd->rqhk", grad_h, value_h, preferred_element_type=f32)
        score_grad = (weights * (weights_grad - delta_part[..., None])).astype(bf16)
        return (weights.astype(bf16), score_grad)

    zero_grad = jnp.zeros((row_count, length, head_count, head_dim), f32)

    def query_side(carried, pieces, first_row):
        key_part, value_part = pieces
        block_len = key_part.shape[1]
        key_pos = first_row + jnp.arange(block_len, dtype=jnp.int32)
        key_seg = segment_ids(doc_lengths, key_pos[None, :])
        key_h = heads_of(key_part, block_len)
        weights_b, score_grad = gradient_terms(
            queries_h,
            local_pos,
            local_seg,
            attended_grad_h,
            log_mass,
            row_delta,
            key_h,
            heads_of(value_part, block_len),
            key_pos,
            key_seg,
        )
        return carried + jnp.einsum(
            "rqhk,rkhd->rqhd", score_grad, key_h, preferred_element_type=f32
        )

    query_grad = over_blocks(
        zero_grad,
        (
            lax.all_gather(key_rows, "seq", axis=1, tiled=True),
            lax.all_gather(value_rows, "seq", axis=1, tiled=True),
        ),
        query_side,
    )
    mass_all, delta_all = (
        lax.all_gather(log_mass, "seq", axis=1, tiled=True),
        lax.all_gather(row_delta, "seq", axis=1, tiled=True),
    )

    def key_side(carried, pieces, first_row):
        key_acc, value_acc = carried
        query_part, grad_part = pieces
        block_len = query_part.shape[1]
        query_pos = first_row + jnp.arange(block_len, dtype=jnp.int32)
        query_seg = segment_ids(doc_lengths, query_pos[None, :])
        mass_part = lax.dynamic_slice_in_dim(mass_all, first_row, block_len, 1)
        delta_part = lax.dynamic_slice_in_dim(delta_all, first_row, block_len, 1)
        query_h = heads_of(query_part, block_len)
        grad_h = heads_of(grad_part, block_len)
        weights_b, score_grad = gradient_terms(
            query_h,
            query_pos,
            query_seg,
            grad_h,
            mass_part,
            delta_part,
            keys_h,
            values_h,
            local_pos,
            local_seg,
        )
        key_acc = key_acc + jnp.einsum(
            "rqhk,rqhd->rkhd", score_grad, query_h, preferred_element_type=f32
        )
        value_acc = value_acc + jnp.einsum(
            "rqhk,rqhd->rkhd", weights_b, grad_h, preferred_element_type=f32
        )
        return (key_acc, value_acc)

    key_grad, value_grad = over_blocks(
        (zero_grad, zero_grad),
        (
            lax.all_gather(queries, "seq", axis=1, tiled=True),
            lax.all_gather(attended_grad, "seq", axis=1, tiled=True),
        ),
        key_side,
    )
    query_grad_b = query_grad.astype(bf16).reshape(token_count, model_width)
    key_grad_b = key_grad.astype(bf16).reshape(token_count, model_width)
    value_grad_b = value_grad.astype(bf16).reshape(token_count, model_width)
    normed_grad = jnp.einsum("te,de->td", query_grad_b, w_query, preferred_element_type=f32)
    normed_grad = normed_grad + jnp.einsum(
        "te,de->td", key_grad_b, w_key, preferred_element_type=f32
    )
    normed_grad = normed_grad + jnp.einsum(
        "te,de->td", value_grad_b, w_value, preferred_element_type=f32
    )
    input_grad = hidden_grad + norm_attn_back(normed_grad)[0]
    input_grad = input_grad.astype(bf16).reshape(row_count, length, model_width)
    return (
        output,
        input_grad,
        summed[0],
        summed[1],
        summed[2],
        summed[3],
        summed[4],
        summed[5],
        summed[6],
    )


MESH = pl.DeviceIdType.MESH
LANES = 256


def dot_nn(left, right, precision=None):
    return lax.dot_general(
        left, right, (((1,), (0,)), ((), ())), precision=precision, preferred_element_type=jnp.float32
    )


def dot_nt(left, right, precision=None):
    return lax.dot_general(
        left, right, (((1,), (1,)), ((), ())), precision=precision, preferred_element_type=jnp.float32
    )


def gelu_pair(values):
    square = values * values
    tanh = jnp.tanh(0.7978845608028654 * values * (1.0 + 0.044715 * square))
    half = 0.5 * (1.0 + tanh)
    slope = half + 0.5 * values * (1.0 - tanh * tanh) * (
        0.7978845608028654 * (1.0 + 3.0 * 0.044715 * square)
    )
    return values * half, slope


def inverse_rms(values):
    return lax.rsqrt(jnp.mean(values * values, axis=-1, keepdims=True) + epsilon)


def norm_back(values, gain, grad):
    inverse = inverse_rms(values)
    scaled = grad * gain
    return inverse * scaled - values * (
        inverse * inverse * inverse * jnp.mean(values * scaled, axis=-1, keepdims=True)
    )


def layer_kernel(
    rows_size,
    doc_lengths,
    rel_table,
    phm_rule,
    gain_attn,
    gain_ffn,
    down_left,
    down_right,
    up_left,
    up_right,
    down_bias,
    up_bias,
    x_hbm,
    ct_hbm,
    w_query_hbm,
    w_key_hbm,
    w_value_hbm,
    w_out_hbm,
    w_in_hbm,
    w_ffout_hbm,
    out_hbm,
    igrad_hbm,
    stats_out,
    w_query,
    w_key,
    w_value,
    w_out,
    w_in,
    w_ffout,
    x_rows,
    ct_rows,
    normed,
    qkv_send,
    slots_a,
    slots_b,
    key_value,
    wide,
    bias,
    att_a,
    att_b,
    mass_a,
    mass_b,
    o_send_a,
    o_send_b,
    att_recv,
    hidden,
    act,
    ff_out,
    down_b,
    up_b,
    hidden_grad,
    do_a,
    do_b,
    dk_acc,
    dv_acc,
    dq_acc,
    stats,
    stats_rows,
    stats_core,
    stats_z,
    out_stage,
    load_sem,
    qkv_send_sem,
    slot_a_sem,
    slot_b_sem,
    o_send_a_sem,
    o_send_b_sem,
    att_sem,
    do_send_sem,
    do_a_sem,
    do_b_sem,
    g_send_a_sem,
    g_send_b_sem,
    g_sem,
    st_rows_send,
    st_rows_recv,
    st_core_send,
    st_core_recv,
    st_z_send,
    st_z_recv,
    st_last_send,
    st_last_recv,
    out_sem,
):
    f32 = jnp.float32
    bf16 = jnp.bfloat16
    highest_p = lax.Precision.HIGHEST
    row_place = lax.axis_index("rows")
    place = lax.axis_index("seq")
    chip = place // 2
    core = lax.rem(place, 2)
    half = chip // 2
    parity = lax.rem(chip, 2)

    gain_attn = gain_attn[...].reshape(1, 768)
    gain_ffn = gain_ffn[...].reshape(1, 768)
    down_bias = down_bias[...].reshape(1, 48)
    up_bias = up_bias[...].reshape(1, 768)

    x_raw = out_stage.at[0]
    ct_raw = out_stage.at[1]
    do_send = att_recv
    g_recv = qkv_send

    loads = [
        pltpu.make_async_copy(src, dst, load_sem.at[index])
        for index, (src, dst) in enumerate(
            (
                (x_hbm, x_raw),
                (w_query_hbm, w_query),
                (w_key_hbm, w_key),
                (w_value_hbm, w_value),
                (ct_hbm, ct_raw),
                (w_out_hbm, w_out),
                (w_in_hbm, w_in),
                (w_ffout_hbm, w_ffout),
            )
        )
    ]
    for load in loads:
        load.start()
    barrier = pltpu.get_barrier_semaphore()
    for offset in range(1, 8):
        pl.semaphore_signal(
            barrier,
            inc=1,
            device_id=(row_place, lax.rem(place + offset, 8)),
            device_id_type=MESH,
        )
    for offset in range(1, rows_size):
        pl.semaphore_signal(
            barrier,
            inc=1,
            device_id=(lax.rem(row_place + offset, rows_size), place),
            device_id_type=MESH,
        )

    first_single = doc_lengths[0, 1] == 0
    loads[0].wait()
    x_rows[0] = jnp.where(first_single, x_raw[0], x_raw[1])
    x_rows[1] = jnp.where(first_single, x_raw[1], x_raw[0])

    def norm_row(row, _):
        values = x_rows[row].astype(f32)
        normed[pl.ds(pl.multiple_of(row * LANES, LANES), LANES), :] = (
            values * inverse_rms(values) * gain_attn
        ).astype(bf16)
        return 0

    lax.fori_loop(0, 2, norm_row, 0)
    for load in loads[1:4]:
        load.wait()

    for part, weight in enumerate((w_query, w_key, w_value)):
        for group in range(3):
            made = dot_nn(normed[...], weight[:, group * 256 : (group + 1) * 256]).astype(bf16)
            turned = made.T
            for inside in range(4):
                for row in range(2):
                    qkv_send[row, group * 4 + inside, part * 64 : (part + 1) * 64, :] = turned[
                        inside * 64 : (inside + 1) * 64, row * LANES : (row + 1) * LANES
                    ]

    pl.semaphore_wait(barrier, 7 + rows_size - 1)

    def send_heads(visit):
        def head_a(offset, inside):
            to_chip = lax.rem(chip + offset, 4)
            owner = to_chip * 2 + inside // 2
            visit(0, 3 * to_chip + inside, owner, inside % 2, offset == 0)

        def head_b(to_parity, inside):
            to_chip = half * 2 + to_parity
            owner = to_chip * 2 + min(inside, 1)
            visit(1, 6 * to_parity + inside, owner, max(inside - 1, 0), True)

        for inside in (0, 2, 1):
            for offset in (2, 1, 3, 0):
                head_a(offset, inside)
            for block in ((0, 1), (2, 3), (4, 5))[(0, 2, 1).index(inside)]:
                for to_parity in range(2):
                    head_b(to_parity, block)

    def exchange(source, to_a, to_b, send_sem, a_sem, b_sem):
        def visit(start):
            def go(row, head, owner, slot, maybe_mine):
                src = source.at[row, head]
                if row == 0:
                    dst, sem = to_a.at[slot, place], a_sem.at[slot]
                else:
                    dst, sem = to_b.at[slot, lax.rem(place, 4)], b_sem.at[slot]

                def remote():
                    copy = pltpu.make_async_remote_copy(
                        src_ref=src,
                        dst_ref=dst,
                        send_sem=send_sem.at[row, head],
                        recv_sem=sem,
                        device_id=(row_place, owner),
                        device_id_type=MESH,
                    )
                    if start:
                        copy.start()
                    else:
                        copy.wait_send()

                if not maybe_mine:
                    remote()
                    return
                pl.when(owner != place)(remote)
                if start:

                    @pl.when(owner == place)
                    def _():
                        pltpu.make_async_copy(src, dst, sem).start()

            return go

        return (lambda: send_heads(visit(True))), (lambda: send_heads(visit(False)))

    start_qkv, end_qkv = exchange(qkv_send, slots_a, slots_b, qkv_send_sem, slot_a_sem, slot_b_sem)
    start_qkv()

    def back_to_sources(row, source, head, to, send_sem, sem, start):
        count = 8 if row == 0 else 4
        for offset in (4, 5, 3, 6, 2, 7, 1, 0) if row == 0 else (2, 3, 1, 0):
            if row == 0:
                index = lax.rem(place + offset, 8)
                owner = index
            else:
                index = lax.rem(lax.rem(place, 4) + offset, 4)
                owner = half * 4 + index
            if offset:
                copy = pltpu.make_async_remote_copy(
                    src_ref=source.at[index],
                    dst_ref=to.at[row, head],
                    send_sem=send_sem.at[offset],
                    recv_sem=sem.at[row],
                    device_id=(row_place, owner),
                    device_id_type=MESH,
                )
                if start:
                    copy.start()
                else:
                    copy.wait_send()
            elif start:
                pltpu.make_async_copy(source.at[index], to.at[row, head], sem.at[row]).start()

    head_of_a = lambda item: 3 * chip + item + 2 * core
    head_of_b = lambda item: 6 * parity + item + core
    count_a = 2 - core
    count_b = 1 + 4 * core

    def make_bias(slot, head):
        offset = 256 - lax.broadcasted_iota(jnp.int32, (8, 512), 1)
        bucket = bucket_of(offset)
        line = jnp.zeros((8, 512), f32)
        for number in range(32):
            line = jnp.where(bucket == number, rel_table[head, number], line)
        spread = pltpu.roll(
            jnp.broadcast_to(line[:1], (128, 512)), 0, 1, stride=1, stride_axis=0
        )
        bias[slot, 0] = jnp.full((128, 128), rel_table[head, 15], f32)
        bias[slot, 1] = spread[:, 384:512]
        bias[slot, 2] = spread[:, 256:384]
        bias[slot, 3] = spread[:, 128:256]
        bias[slot, 4] = jnp.full((128, 128), rel_table[head, 31], f32)

    def bias_a(item, _):
        make_bias(item, head_of_a(item))
        return 0

    def bias_b(item, _):
        make_bias(2 + item, head_of_b(item))
        return 0

    lax.fori_loop(0, count_a, bias_a, 0)
    lax.fori_loop(0, count_b, bias_b, 0)

    lane48 = lax.broadcasted_iota(jnp.int32, (4, 48), 1)
    term = lax.broadcasted_iota(jnp.int32, (4, 48), 0)
    fold12 = (
        lax.rem(lax.broadcasted_iota(jnp.int32, (12, 48), 1), 12)
        == lax.broadcasted_iota(jnp.int32, (12, 48), 0)
    ).astype(f32)

    def rule_lines(transposed, outer):
        made = jnp.zeros((4, 48), f32)
        for number in range(4):
            for inner in range(4):
                value = (
                    phm_rule[number, inner, outer] if transposed else phm_rule[number, outer, inner]
                )
                made = jnp.where((term == number) & (lane48 // 12 == inner), value, made)
        return made

    down_rules = [rule_lines(False, outer) for outer in range(4)]
    up_rules = [rule_lines(True, outer) for outer in range(4)]
    down_right_wide = dot_nn(down_right[...], fold12, highest_p)
    up_left_wide = dot_nn(up_left[...], fold12, highest_p)
    down_left_t = down_left[...].T
    up_right_t = up_right[...].T
    for outer in range(4):
        down_b[outer * 192 : (outer + 1) * 192, :] = dot_nn(
            down_left_t, down_rules[outer] * down_right_wide, highest_p
        ).astype(bf16)
        up_b[outer * 192 : (outer + 1) * 192, :] = dot_nn(
            up_right_t, up_rules[outer] * up_left_wide, highest_p
        ).astype(bf16)

    loads[4].wait()
    ct_rows[0:LANES, :] = jnp.where(first_single, ct_raw[0], ct_raw[1])
    ct_rows[LANES:, :] = jnp.where(first_single, ct_raw[1], ct_raw[0])

    zero64 = jnp.zeros((64, 1024), bf16)

    def turn_keys(slot, blocks):
        for block in range(blocks):
            key_value[block * 256 : (block + 1) * 256, :] = slot[block, 64:192, :].T

    def joined(slot, tile, low, high):
        return jnp.concatenate([slot[4 * tile + u, low:high, :] for u in range(4)], axis=1)

    def with_bias(scores, number, block, tile):
        lines = []
        for upper in range(2):
            pieces = []
            for lane in range(8):
                distance = 2 * block + upper - (8 * tile + lane)
                if isinstance(distance, int):
                    distance = max(-2, min(2, distance)) + 2
                else:
                    distance = jnp.clip(distance, -2, 2) + 2
                pieces.append(
                    scores[upper * 128 : (upper + 1) * 128, lane * 128 : (lane + 1) * 128]
                    + bias[number, distance]
                )
            lines.append(jnp.concatenate(pieces, axis=1))
        return jnp.concatenate(lines, axis=0)

    def attend(slot, number, blocks, att, mass, o_send):
        turn_keys(slot, blocks)

        def one_tile(tile, _):
            lanes = pl.ds(pl.multiple_of(tile * 1024, 1024), 1024)
            query = jnp.concatenate([joined(slot, tile, 0, 64), zero64], axis=0)
            peak = jnp.full((8, 1024), -1e30, f32)
            for block in range(blocks):
                scores = dot_nn(key_value[block * 256 : (block + 1) * 256, :], query)
                scores = with_bias(scores, number, block, tile)
                wide[block * 256 : (block + 1) * 256, :] = scores
                peak = jnp.maximum(peak, jnp.max(scores.reshape(32, 8, 1024), axis=0))
            peak = jnp.max(peak, axis=0, keepdims=True)
            total = jnp.zeros((64, 1024), f32)
            mass_sum = jnp.zeros((8, 1024), f32)
            for block in range(blocks):
                weights = jnp.exp(wide[block * 256 : (block + 1) * 256, :] - peak)
                mass_sum = mass_sum + jnp.sum(weights.reshape(32, 8, 1024), axis=0)
                total = total + dot_nn(slot[block, 128:192, :], weights.astype(bf16))
            mass_sum = jnp.sum(mass_sum, axis=0, keepdims=True)
            total = total / mass_sum
            att[:, lanes] = total
            mass[:, lanes] = peak + jnp.log(mass_sum)
            for u in range(4):
                o_send[4 * tile + u] = total[:, u * 256 : (u + 1) * 256].astype(bf16)
            return 0

        if blocks == 4:
            one_tile(0, 0)
        else:
            lax.fori_loop(0, blocks // 4, one_tile, 0)

    def forward_a(item, _):
        pltpu.make_async_copy(slots_a.at[item], slots_a.at[item], slot_a_sem.at[item]).wait()
        attend(slots_a.at[item], item, 8, att_a.at[item], mass_a.at[item], o_send_a.at[item])
        back_to_sources(
            0, o_send_a.at[item], head_of_a(item), att_recv, o_send_a_sem.at[item], att_sem, True
        )
        return 0

    def forward_b(item, _):
        pltpu.make_async_copy(slots_b.at[item], slots_b.at[item], slot_b_sem.at[item]).wait()
        attend(slots_b.at[item], 2 + item, 4, att_b.at[item], mass_b.at[item], o_send_b.at[item])
        back_to_sources(
            1, o_send_b.at[item], head_of_b(item), att_recv, o_send_b_sem.at[item], att_sem, True
        )
        return 0

    lax.fori_loop(0, count_a, forward_a, 0)
    lax.fori_loop(0, count_b, forward_b, 0)

    loads[5].wait()
    for row in range(2):
        pltpu.make_async_copy(att_recv.at[row], att_recv.at[row], att_sem.at[row]).wait()
        lines = slice(row * LANES, (row + 1) * LANES)
        attended = att_recv[row].reshape(768, LANES).T
        values = x_rows[row].astype(f32) + dot_nn(attended, w_out[...])
        hidden[lines, :] = values
        normed[lines, :] = (values * inverse_rms(values) * gain_ffn).astype(bf16)

    def wide_place(chunk):
        return (
            pl.ds(pl.multiple_of((chunk // 2) * 512, 512), 512),
            pl.ds(pl.multiple_of(lax.rem(chunk, 2) * 512, 512), 512),
        )

    loads[6].wait()

    def inner_chunk(chunk, _):
        columns = pl.ds(pl.multiple_of(chunk * 512, 512), 512)
        value, slope = gelu_pair(dot_nn(normed[...], w_in[:, columns]))
        act[:, columns] = value.astype(bf16)
        at_rows, at_lanes = wide_place(chunk)
        wide[at_rows, at_lanes] = slope
        return 0

    lax.fori_loop(0, 6, inner_chunk, 0)
    loads[7].wait()
    ff_out[...] = dot_nn(act[...], w_ffout[...]).astype(bf16)
    squeezed_act, squeezed_slope = gelu_pair(dot_nn(ff_out[...], down_b[...]) + down_bias)
    squeezed_act = squeezed_act.astype(bf16)
    squeezed_grad = dot_nn(ct_rows[...], up_b[...]) * squeezed_slope
    squeezed_low = squeezed_grad.astype(bf16)
    result_rows = []
    for row in range(2):
        lines = slice(row * LANES, (row + 1) * LANES)
        result_rows.append(
            (
                hidden[lines, :]
                + ff_out[lines, :].astype(f32)
                + dot_nt(squeezed_act[lines, :], up_b[...])
                + up_bias
            ).astype(bf16)
        )
    out_stage[0, 0] = jnp.where(first_single, result_rows[0], result_rows[1])
    out_stage[0, 1] = jnp.where(first_single, result_rows[1], result_rows[0])
    write_out = pltpu.make_async_copy(out_stage.at[0], out_hbm, out_sem.at[0])
    write_out.start()

    ff_grad = (ct_rows[...].astype(f32) + dot_nt(squeezed_low, down_b[...])).astype(bf16)

    normed[...] = ff_grad

    def inner_back(chunk, _):
        columns = pl.ds(pl.multiple_of(chunk * 512, 512), 512)
        at_rows, at_lanes = wide_place(chunk)
        act[:, columns] = (
            dot_nt(normed[...], w_ffout[columns, :]) * wide[at_rows, at_lanes]
        ).astype(bf16)
        return 0

    lax.fori_loop(0, 6, inner_back, 0)
    normed_grad = dot_nt(act[...], w_in[...])
    for row in range(2):
        lines = slice(row * LANES, (row + 1) * LANES)
        values = ct_rows[lines, :].astype(f32) + norm_back(
            hidden[lines, :], gain_ffn, normed_grad[lines, :]
        )
        hidden_grad[lines, :] = values
        turned = dot_nt(values.astype(bf16), w_out[...]).astype(bf16).T
        do_send[row] = turned.reshape(12, 64, LANES)

    end_qkv()
    start_do, end_do = exchange(do_send, do_a, do_b, do_send_sem, do_a_sem, do_b_sem)
    start_do()

    up_grad = dot_nn(ct_rows[...].T, squeezed_act)
    down_grad = dot_nn(ff_out[...].T, squeezed_low)
    column48 = lax.broadcasted_iota(jnp.int32, (48, 16), 0) // 12
    lane16 = lax.broadcasted_iota(jnp.int32, (48, 16), 1)

    def kron_back(grad, left, right_wide, rules, transposed):
        left_grad = jnp.zeros((4, 192), f32)
        right_grad = jnp.zeros((4, 48), f32)
        rule_grad = jnp.zeros((4, 16), f32)
        for outer in range(4):
            block = grad[outer * 192 : (outer + 1) * 192, :]
            left_grad = left_grad + dot_nt(rules[outer] * right_wide, block, highest_p)
            contracted = dot_nn(left, block, highest_p)
            right_grad = right_grad + contracted * rules[outer]
            target = column48 * 4 + outer if transposed else outer * 4 + column48
            rule_grad = rule_grad + dot_nn(
                contracted * right_wide, (target == lane16).astype(f32), highest_p
            )
        return left_grad, dot_nt(right_grad, fold12, highest_p), rule_grad

    dl_grad, dr_grad, rule_down = kron_back(
        down_grad, down_left[...], down_right_wide, down_rules, False
    )
    ur_grad, ul_grad, rule_up = kron_back(up_grad, up_right[...], up_left_wide, up_rules, True)
    stats[...] = jnp.zeros_like(stats)
    stats[0:4, 0:192] = dl_grad
    stats[4:8, 0:192] = ur_grad
    stats[8:12, 0:12] = dr_grad
    stats[8:12, 128:140] = ul_grad
    stats[12:16, 0:16] = rule_down + rule_up
    stats[16:17, 0:48] = jnp.sum(squeezed_grad, axis=0, keepdims=True)
    up_bias_grad = jnp.sum(ct_rows[...].astype(f32), axis=0, keepdims=True)
    for third in range(3):
        stats[17 + third : 18 + third, :] = up_bias_grad[:, third * 256 : (third + 1) * 256]

    def rows_copy(offset):
        return pltpu.make_async_remote_copy(
            src_ref=stats,
            dst_ref=stats_rows.at[row_place],
            send_sem=st_rows_send.at[offset - 1],
            recv_sem=st_rows_recv.at[offset - 1],
            device_id=(lax.rem(row_place + offset, rows_size), place),
            device_id_type=MESH,
        )

    for offset in range(1, rows_size):
        rows_copy(offset).start()

    def attend_back(slot, do_slot, number, blocks, att, mass, g_send):
        turn_keys(slot, blocks)

        def one_tile(tile, first):
            lanes = pl.ds(pl.multiple_of(tile * 1024, 1024), 1024)
            query = joined(slot, tile, 0, 64)
            grad = joined(do_slot, tile, 0, 64)
            query_z = jnp.concatenate([query, zero64], axis=0)
            grad_z = jnp.concatenate([zero64, grad], axis=0)
            delta = jnp.sum(grad.astype(f32) * att[:, lanes], axis=0, keepdims=True)
            log_mass = mass[:, lanes]
            for block in range(blocks):
                keys = slice(block * 256, (block + 1) * 256)
                scores = with_bias(dot_nn(key_value[keys, :], query_z), number, block, tile)
                probs = jnp.exp(scores - log_mass)
                probs_grad = dot_nn(key_value[keys, :], grad_z)
                score_grad = (probs * (probs_grad - delta)).astype(bf16)
                dq_part = dot_nn(slot[block, 64:128, :], score_grad)
                if block == 0:
                    dq_acc[...] = dq_part
                else:
                    dq_acc[...] += dq_part
                dv_part = dot_nt(grad, probs.astype(bf16))
                dk_part = dot_nt(query, score_grad)
                if first:
                    dv_acc[:, keys] = dv_part
                    dk_acc[:, keys] = dk_part
                else:
                    dv_acc[:, keys] += dv_part
                    dk_acc[:, keys] += dk_part
            for u in range(4):
                g_send[4 * tile + u, 0:64, :] = dq_acc[:, u * 256 : (u + 1) * 256].astype(bf16)

        for tile in range(blocks // 4):
            one_tile(tile, tile == 0)
        for block in range(blocks):
            keys = slice(block * 256, (block + 1) * 256)
            g_send[block, 64:128, :] = dk_acc[:, keys].astype(bf16)
            g_send[block, 128:192, :] = dv_acc[:, keys].astype(bf16)

    def backward_a(item, _):
        pltpu.make_async_copy(do_a.at[item], do_a.at[item], do_a_sem.at[item]).wait()
        attend_back(
            slots_a.at[item],
            do_a.at[item],
            item,
            8,
            att_a.at[item],
            mass_a.at[item],
            slots_a.at[item],
        )
        back_to_sources(
            0, slots_a.at[item], head_of_a(item), g_recv, g_send_a_sem.at[item], g_sem, True
        )
        return 0

    def backward_b(item, _):
        pltpu.make_async_copy(do_b.at[item], do_b.at[item], do_b_sem.at[item]).wait()
        attend_back(
            slots_b.at[item],
            do_b.at[item],
            2 + item,
            4,
            att_b.at[item],
            mass_b.at[item],
            slots_b.at[item],
        )
        back_to_sources(
            1, slots_b.at[item], head_of_b(item), g_recv, g_send_b_sem.at[item], g_sem, True
        )
        return 0

    lax.fori_loop(0, count_a, backward_a, 0)

    my_lanes = pl.ds(pl.multiple_of(core * 128, 128), 128)
    other_lanes = pl.ds(pl.multiple_of((1 - core) * 128, 128), 128)
    sibling = chip * 2 + 1 - core
    stats_rows[row_place] = stats[...]
    for offset in range(1, rows_size):
        rows_copy(offset).wait()
    summed = stats_rows[0]
    for number in range(1, rows_size):
        summed = summed + stats_rows[number]
    stats_core[0] = summed
    core_copy = pltpu.make_async_remote_copy(
        src_ref=stats_core.at[0, :, other_lanes],
        dst_ref=stats_core.at[1, :, other_lanes],
        send_sem=st_core_send,
        recv_sem=st_core_recv,
        device_id=(row_place, sibling),
        device_id_type=MESH,
    )
    core_copy.start()
    core_copy.wait_send()
    pltpu.make_async_copy(
        stats_core.at[1, :, my_lanes], stats_core.at[1, :, my_lanes], st_core_recv
    ).wait()
    stats_z[chip] = stats_core[0, :, my_lanes] + stats_core[1, :, my_lanes]

    def z_copy(offset):
        return pltpu.make_async_remote_copy(
            src_ref=stats_z.at[chip],
            dst_ref=stats_z.at[chip],
            send_sem=st_z_send.at[offset - 1],
            recv_sem=st_z_recv.at[offset - 1],
            device_id=(row_place, lax.rem(chip + offset, 4) * 2 + core),
            device_id_type=MESH,
        )

    for offset in range(1, 4):
        z_copy(offset).start()

    lax.fori_loop(0, count_b, backward_b, 0)

    for offset in range(1, 4):
        z_copy(offset).wait()
    stats_core[2, :, my_lanes] = (stats_z[0] + stats_z[1]) + (stats_z[2] + stats_z[3])
    last_copy = pltpu.make_async_remote_copy(
        src_ref=stats_core.at[2, :, my_lanes],
        dst_ref=stats_core.at[2, :, my_lanes],
        send_sem=st_last_send,
        recv_sem=st_last_recv,
        device_id=(row_place, sibling),
        device_id_type=MESH,
    )
    last_copy.start()

    turned_grad = jnp.zeros((768, 512), f32)
    for row in range(2):
        pltpu.make_async_copy(g_recv.at[row], g_recv.at[row], g_sem.at[row]).wait()
    for part, weight in enumerate((w_query, w_key, w_value)):
        grads = jnp.concatenate(
            [
                g_recv[row, :, part * 64 : (part + 1) * 64, :].reshape(768, LANES)
                for row in range(2)
            ],
            axis=1,
        )
        turned_grad = turned_grad + dot_nn(weight[...], grads)
    final_rows = []
    for row in range(2):
        lines = slice(row * LANES, (row + 1) * LANES)
        final_rows.append(
            (
                hidden_grad[lines, :]
                + norm_back(
                    x_rows[row].astype(f32), gain_attn, turned_grad[:, lines].T
                )
            ).astype(bf16)
        )
    out_stage[1, 0] = jnp.where(first_single, final_rows[0], final_rows[1])
    out_stage[1, 1] = jnp.where(first_single, final_rows[1], final_rows[0])
    write_grad = pltpu.make_async_copy(out_stage.at[1], igrad_hbm, out_sem.at[1])
    write_grad.start()

    last_copy.wait_send()
    pltpu.make_async_copy(
        stats_core.at[2, :, other_lanes], stats_core.at[2, :, other_lanes], st_last_recv
    ).wait()
    stats_out[...] = stats_core[2]

    end_do()

    def end_a(item, _):
        head = head_of_a(item)
        back_to_sources(
            0, o_send_a.at[item], head, att_recv, o_send_a_sem.at[item], att_sem, False
        )
        back_to_sources(0, slots_a.at[item], head, g_recv, g_send_a_sem.at[item], g_sem, False)
        return 0

    def end_b(item, _):
        head = head_of_b(item)
        back_to_sources(
            1, o_send_b.at[item], head, att_recv, o_send_b_sem.at[item], att_sem, False
        )
        back_to_sources(1, slots_b.at[item], head, g_recv, g_send_b_sem.at[item], g_sem, False)
        return 0

    lax.fori_loop(0, count_a, end_a, 0)
    lax.fori_loop(0, count_b, end_b, 0)
    write_out.wait()
    write_grad.wait()


def finish_kernel(
    stats,
    out_from,
    grad_from,
    out_to,
    grad_to,
    rule_out,
    dl_out,
    dr_out,
    ul_out,
    ur_out,
    db_out,
    ub_out,
    stage,
    sem,
):
    gets, puts = [], []
    for number, (source, target) in enumerate(((grad_from, grad_to), (out_from, out_to))):
        for row in range(2):
            gets.append(
                pltpu.make_async_copy(
                    source.at[row], stage.at[number, row], sem.at[0, number, row]
                )
            )
            puts.append(
                pltpu.make_async_copy(
                    stage.at[number, row], target.at[row], sem.at[1, number, row]
                )
            )
    for get in gets:
        get.start()
    for outer in range(4):
        rule_out[:, outer, :] = stats[12:16, 4 * outer : 4 * outer + 4]
    dl_out[...] = stats[0:4, 0:192]
    ur_out[...] = stats[4:8, 0:192]
    dr_out[...] = stats[8:12, 0:12]
    ul_out[...] = stats[8:12, 128:140]
    db_out[...] = stats[16:17, 0:48].reshape(48)
    ub_out[...] = jnp.concatenate([stats[17 + third : 18 + third, :] for third in range(3)], axis=1).reshape(768)
    for get, put in zip(gets, puts):
        get.wait()
        put.start()
    for put in puts:
        put.wait()


def layer_on_slice(rows_size, *arrays):
    (
        inputs,
        doc_lengths,
        w_query,
        w_key,
        w_value,
        w_out,
        w_in,
        w_ffout,
        rel_table,
        gain_attn,
        gain_ffn,
        phm_rule,
        down_left,
        down_right,
        up_left,
        up_right,
        down_bias,
        up_bias,
        cotangent,
    ) = arrays
    f32 = jnp.float32
    bf16 = jnp.bfloat16
    shape = jax.ShapeDtypeStruct
    vmem = pl.BlockSpec(memory_space=pltpu.VMEM)
    smem = pl.BlockSpec(memory_space=pltpu.SMEM)
    hbm = pl.BlockSpec(memory_space=pl.ANY)
    dma = pltpu.SemaphoreType.DMA
    results = pl.pallas_call(
        functools.partial(layer_kernel, rows_size),
        out_shape=[
            shape(inputs.shape, bf16),
            shape(inputs.shape, bf16),
            shape((24, 256), f32),
        ],
        in_specs=[smem] * 3 + [vmem] * 8 + [hbm] * 8,
        out_specs=[hbm] * 2 + [vmem],
        scratch_shapes=[
            pltpu.VMEM((768, 768), bf16),
            pltpu.VMEM((768, 768), bf16),
            pltpu.VMEM((768, 768), bf16),
            pltpu.VMEM((768, 768), bf16),
            pltpu.VMEM((768, 3072), bf16),
            pltpu.VMEM((3072, 768), bf16),
            pltpu.VMEM((2, LANES, 768), bf16),
            pltpu.VMEM((512, 768), bf16),
            pltpu.VMEM((512, 768), bf16),
            pltpu.VMEM((2, 12, 192, LANES), bf16),
            pltpu.VMEM((2, 8, 192, LANES), bf16),
            pltpu.VMEM((5, 4, 192, LANES), bf16),
            pltpu.VMEM((2048, 128), bf16),
            pltpu.VMEM((2048, 1024), f32),
            pltpu.VMEM((7, 5, 128, 128), f32),
            pltpu.VMEM((2, 64, 2048), f32),
            pltpu.VMEM((5, 64, 1024), f32),
            pltpu.VMEM((2, 1, 2048), f32),
            pltpu.VMEM((5, 1, 1024), f32),
            pltpu.VMEM((2, 8, 64, LANES), bf16),
            pltpu.VMEM((5, 4, 64, LANES), bf16),
            pltpu.VMEM((2, 12, 64, LANES), bf16),
            pltpu.VMEM((512, 768), f32),
            pltpu.VMEM((512, 3072), bf16),
            pltpu.VMEM((512, 768), bf16),
            pltpu.VMEM((768, 48), bf16),
            pltpu.VMEM((768, 48), bf16),
            pltpu.VMEM((512, 768), f32),
            pltpu.VMEM((2, 8, 64, LANES), bf16),
            pltpu.VMEM((5, 4, 64, LANES), bf16),
            pltpu.VMEM((64, 2048), f32),
            pltpu.VMEM((64, 2048), f32),
            pltpu.VMEM((64, 1024), f32),
            pltpu.VMEM((24, 256), f32),
            pltpu.VMEM((rows_size, 24, 256), f32),
            pltpu.VMEM((3, 24, 256), f32),
            pltpu.VMEM((4, 24, 128), f32),
            pltpu.VMEM((2, 2, LANES, 768), bf16),
            dma((8,)),
            dma((2, 12)),
            dma((2,)),
            dma((5,)),
            dma((2, 8)),
            dma((5, 4)),
            dma((2,)),
            dma((2, 12)),
            dma((2,)),
            dma((5,)),
            dma((2, 8)),
            dma((5, 4)),
            dma((2,)),
            dma((max(rows_size - 1, 1),)),
            dma((max(rows_size - 1, 1),)),
            dma(()),
            dma(()),
            dma((3,)),
            dma((3,)),
            dma(()),
            dma(()),
            dma((2,)),
        ],
        compiler_params=pltpu.CompilerParams(
            collective_id=0, has_side_effects=True, vmem_limit_bytes=56 * 1024 * 1024
        ),
        name="encoder_layer",
    )(
        doc_lengths,
        rel_table.T,
        phm_rule,
        gain_attn,
        gain_ffn,
        down_left,
        down_right,
        up_left,
        up_right,
        down_bias,
        up_bias,
        inputs,
        cotangent,
        w_query,
        w_key,
        w_value,
        w_out,
        w_in,
        w_ffout,
    )
    return pl.pallas_call(
        finish_kernel,
        out_shape=[
            shape(inputs.shape, bf16),
            shape(inputs.shape, bf16),
            shape(phm_rule.shape, f32),
            shape((4, 192), f32),
            shape((4, 12), f32),
            shape((4, 12), f32),
            shape((4, 192), f32),
            shape((48,), f32),
            shape((768,), f32),
        ],
        in_specs=[vmem] + [hbm] * 2,
        out_specs=[hbm] * 2 + [vmem] * 7,
        scratch_shapes=[pltpu.VMEM((2, 2, LANES, 768), bf16), dma((2, 2, 2))],
        name="finish",
    )(results[2], results[0], results[1])


def pick(rows_size, seq_size, *arrays):
    inputs, doc_lengths = arrays[:2]
    fits = (
        seq_size == 8
        and inputs.shape == (2, LANES, 768)
        and doc_lengths.shape == (2, 2)
        and arrays[8].shape == (32, 12)
        and arrays[6].shape == (768, 3072)
    )
    return layer_on_slice(rows_size, *arrays) if fits else local(*arrays)


def solution(mesh):
    return jax.shard_map(
        functools.partial(pick, mesh.shape["rows"], mesh.shape["seq"]),
        mesh=mesh,
        in_specs=(
            P("rows", "seq", None),
            P("rows", None),
            P(),
            P(),
            P(),
            P(),
            P(),
            P(),
            P(),
            P(),
            P(),
            P(),
            P(),
            P(),
            P(),
            P(),
            P(),
            P(),
            P("rows", "seq", None),
        ),
        out_specs=(
            P("rows", "seq", None),
            P("rows", "seq", None),
            P(),
            P(),
            P(),
            P(),
            P(),
            P(),
            P(),
        ),
        check_vma=False,
    )
```

```python
import functools
import math
from typing import Any, NamedTuple

import jax
import jax.numpy as jnp
from jax import lax
from jax.experimental import pallas as pl
from jax.experimental.pallas import tpu as pltpu
from jax.sharding import PartitionSpec as P

epsilon = 1e-06
highest = lax.Precision.HIGHEST
bucket_edges = (12, 16, 23, 32, 46, 64, 91)


def smooth_gelu(values):
    return (
        0.5
        * values
        * (1.0 + jnp.tanh(0.7978845608028654 * (values + 0.044715 * values * values * values)))
    )


def rms_norm(values, gain):
    return values * lax.rsqrt(jnp.mean(values * values, axis=-1, keepdims=True) + epsilon) * gain


def bucket_of(offset):
    magnitude = jnp.abs(offset)
    larger = jnp.full(offset.shape, 8, jnp.int32)
    for edge in bucket_edges:
        larger = larger + (magnitude >= edge).astype(jnp.int32)
    inside = jnp.where(magnitude < 8, magnitude, larger)
    return inside + jnp.where(offset > 0, 16, 0).astype(jnp.int32)


def segment_ids(lengths, token_positions):
    doc_ends = jnp.cumsum(lengths, axis=-1, dtype=jnp.int32)
    return jnp.sum(
        (token_positions[..., :, None] >= doc_ends[..., None, :]).astype(jnp.int32),
        axis=-1,
        dtype=jnp.int32,
    )


def kron_sum(rule_part, left_part, right_part):
    blocks = jnp.einsum("iab,ip,iq->apbq", rule_part, left_part, right_part, precision=highest)
    return blocks.reshape(
        rule_part.shape[1] * left_part.shape[1], rule_part.shape[2] * right_part.shape[1]
    )


def pair_bias(query_pos, key_pos, rel_table):
    buckets = bucket_of(key_pos[None, :] - query_pos[:, None])
    onehot = (buckets[:, :, None] == jnp.arange(rel_table.shape[0], dtype=jnp.int32)).astype(
        jnp.bfloat16
    )
    table_high = rel_table.astype(jnp.bfloat16)
    table_rest = (rel_table - table_high.astype(jnp.float32)).astype(jnp.bfloat16)
    high_part = jnp.einsum("qkb,bh->qhk", onehot, table_high, preferred_element_type=jnp.float32)
    rest_part = jnp.einsum("qkb,bh->qhk", onehot, table_rest, preferred_element_type=jnp.float32)
    return high_part + rest_part


def over_blocks(carried, pieces, blockwise):
    total_len = pieces[0].shape[1]
    block_len = math.gcd(total_len, 512)

    def one_step(block_index, inner_state):
        begin_row = block_index * block_len
        sliced = tuple(
            (lax.dynamic_slice_in_dim(member, begin_row, block_len, 1) for member in pieces)
        )
        return blockwise(inner_state, sliced, begin_row)

    return lax.fori_loop(0, total_len // block_len, one_step, carried)


def local(
    inputs,
    doc_lengths,
    w_query,
    w_key,
    w_value,
    w_out,
    w_in,
    w_ffout,
    rel_table,
    gain_attn,
    gain_ffn,
    phm_rule,
    down_left,
    down_right,
    up_left,
    up_right,
    down_bias,
    up_bias,
    cotangent,
):
    row_count, length, model_width = inputs.shape
    head_count = rel_table.shape[1]
    head_dim = model_width // head_count
    seq_place = lax.axis_index("seq")
    token_count = row_count * length
    local_pos = seq_place * length + jnp.arange(length, dtype=jnp.int32)
    local_seg = segment_ids(doc_lengths, local_pos[None, :])
    bf16 = jnp.bfloat16
    f32 = jnp.float32

    def heads_of(matrix, block_len):
        return matrix.reshape(row_count, block_len, head_count, head_dim)

    def norm_attn(values):
        return rms_norm(values, gain_attn)

    def norm_ffn(values):
        return rms_norm(values, gain_ffn)

    source = inputs.astype(f32).reshape(token_count, model_width)
    normed, norm_attn_back = jax.vjp(norm_attn, source)
    normed_b = normed.astype(bf16)
    queries = (
        jnp.dot(normed_b, w_query, preferred_element_type=f32)
        .astype(bf16)
        .reshape(row_count, length, model_width)
    )
    key_rows = (
        jnp.dot(normed_b, w_key, preferred_element_type=f32)
        .astype(bf16)
        .reshape(row_count, length, model_width)
    )
    value_rows = (
        jnp.dot(normed_b, w_value, preferred_element_type=f32)
        .astype(bf16)
        .reshape(row_count, length, model_width)
    )
    queries_h = heads_of(queries, length)
    keys_h = heads_of(key_rows, length)
    values_h = heads_of(value_rows, length)

    def scores_for(query_h, query_pos, query_seg, key_h, key_pos, key_seg):
        scores = jnp.einsum("rqhd,rkhd->rqhk", query_h, key_h, preferred_element_type=f32)
        scores = scores + pair_bias(query_pos, key_pos, rel_table)[None]
        allowed = (query_seg[:, :, None] == key_seg[:, None, :])[:, :, None, :]
        return (scores, allowed)

    def forward_piece(carried, pieces, first_row):
        weighted, running, mass_sum = carried
        key_part, value_part = pieces
        block_len = key_part.shape[1]
        key_pos = first_row + jnp.arange(block_len, dtype=jnp.int32)
        key_seg = segment_ids(doc_lengths, key_pos[None, :])
        scores, allowed = scores_for(
            queries_h, local_pos, local_seg, heads_of(key_part, block_len), key_pos, key_seg
        )
        scores = jnp.where(allowed, scores, -1e30)
        raised = jnp.maximum(running, jnp.max(scores, axis=-1))
        weights = jnp.where(allowed, jnp.exp(scores - raised[..., None]), 0.0)
        rescale = jnp.exp(running - raised)
        mass_sum = mass_sum * rescale + jnp.sum(weights, axis=-1)
        weighted = weighted * rescale[..., None] + jnp.einsum(
            "rqhk,rkhd->rqhd",
            weights.astype(bf16),
            heads_of(value_part, block_len),
            preferred_element_type=f32,
        )
        return (weighted, raised, mass_sum)

    start_state = (
        jnp.zeros((row_count, length, head_count, head_dim), f32),
        jnp.full((row_count, length, head_count), -1e30, f32),
        jnp.zeros((row_count, length, head_count), f32),
    )
    weighted, running, mass_sum = over_blocks(
        start_state,
        (
            lax.all_gather(key_rows, "seq", axis=1, tiled=True),
            lax.all_gather(value_rows, "seq", axis=1, tiled=True),
        ),
        forward_piece,
    )
    attended = weighted / mass_sum[..., None]
    log_mass = running + jnp.log(mass_sum)
    attended_b = attended.astype(bf16).reshape(token_count, model_width)
    hidden = source + jnp.dot(attended_b, w_out, preferred_element_type=f32)
    normed_ffn, norm_ffn_back = jax.vjp(norm_ffn, hidden)
    inner = jnp.dot(normed_ffn.astype(bf16), w_in, preferred_element_type=f32)
    activated, gelu_back = jax.vjp(smooth_gelu, inner)
    activated_b = activated.astype(bf16)
    ff_out = jnp.dot(activated_b, w_ffout, preferred_element_type=f32).astype(bf16)
    down_full, down_back = jax.vjp(kron_sum, phm_rule, down_left, down_right)
    up_full, up_back = jax.vjp(kron_sum, phm_rule, up_left, up_right)
    down_b = down_full.astype(bf16)
    up_b = up_full.astype(bf16)
    squeezed = jnp.dot(ff_out, down_b, preferred_element_type=f32) + down_bias
    squeezed_act, squeeze_back = jax.vjp(smooth_gelu, squeezed)
    squeezed_act_b = squeezed_act.astype(bf16)
    expanded = jnp.dot(squeezed_act_b, up_b, preferred_element_type=f32) + up_bias
    result = hidden + ff_out.astype(f32) + expanded
    output = result.astype(bf16).reshape(row_count, length, model_width)
    upstream = cotangent.astype(f32).reshape(token_count, model_width)
    up_bias_grad = jnp.sum(upstream, axis=0)
    upstream_b = upstream.astype(bf16)
    up_matrix_grad = jnp.einsum("ta,td->ad", squeezed_act_b, upstream_b, preferred_element_type=f32)
    squeezed_grad = squeeze_back(
        jnp.einsum("td,ad->ta", upstream_b, up_b, preferred_element_type=f32)
    )[0]
    down_bias_grad = jnp.sum(squeezed_grad, axis=0)
    squeezed_low = squeezed_grad.astype(bf16)
    down_matrix_grad = jnp.einsum("td,ta->da", ff_out, squeezed_low, preferred_element_type=f32)
    rule_down, down_left_grad, down_right_grad = down_back(down_matrix_grad)
    rule_up, up_left_grad, up_right_grad = up_back(up_matrix_grad)
    summed = lax.psum(
        (
            rule_down + rule_up,
            down_left_grad,
            down_right_grad,
            up_left_grad,
            up_right_grad,
            down_bias_grad,
            up_bias_grad,
        ),
        ("rows", "seq"),
    )
    ff_grad = upstream + jnp.einsum("ta,da->td", squeezed_low, down_b, preferred_element_type=f32)
    ff_grad_b = ff_grad.astype(bf16)
    inner_grad = gelu_back(jnp.einsum("td,fd->tf", ff_grad_b, w_ffout, preferred_element_type=f32))[
        0
    ]
    inner_grad_b = inner_grad.astype(bf16)
    hidden_grad = (
        upstream
        + norm_ffn_back(jnp.einsum("tf,df->td", inner_grad_b, w_in, preferred_element_type=f32))[0]
    )
    hidden_grad_b = hidden_grad.astype(bf16)
    attended_grad = jnp.einsum(
        "te,de->td", hidden_grad_b, w_out, preferred_element_type=f32
    ).astype(bf16)
    attended_grad = attended_grad.reshape(row_count, length, model_width)
    attended_grad_h = heads_of(attended_grad, length)
    row_delta = jnp.sum(attended_grad_h.astype(f32) * attended, axis=-1)

    def gradient_terms(
        query_h,
        query_pos,
        query_seg,
        grad_h,
        mass_part,
        delta_part,
        key_h,
        value_h,
        key_pos,
        key_seg,
    ):
        scores, allowed = scores_for(query_h, query_pos, query_seg, key_h, key_pos, key_seg)
        weights = jnp.exp(jnp.where(allowed, scores - mass_part[..., None], -1e30))
        weights_grad = jnp.einsum("rqhd,rkhd->rqhk", grad_h, value_h, preferred_element_type=f32)
        score_grad = (weights * (weights_grad - delta_part[..., None])).astype(bf16)
        return (weights.astype(bf16), score_grad)

    zero_grad = jnp.zeros((row_count, length, head_count, head_dim), f32)

    def query_side(carried, pieces, first_row):
        key_part, value_part = pieces
        block_len = key_part.shape[1]
        key_pos = first_row + jnp.arange(block_len, dtype=jnp.int32)
        key_seg = segment_ids(doc_lengths, key_pos[None, :])
        key_h = heads_of(key_part, block_len)
        weights_b, score_grad = gradient_terms(
            queries_h,
            local_pos,
            local_seg,
            attended_grad_h,
            log_mass,
            row_delta,
            key_h,
            heads_of(value_part, block_len),
            key_pos,
            key_seg,
        )
        return carried + jnp.einsum(
            "rqhk,rkhd->rqhd", score_grad, key_h, preferred_element_type=f32
        )

    query_grad = over_blocks(
        zero_grad,
        (
            lax.all_gather(key_rows, "seq", axis=1, tiled=True),
            lax.all_gather(value_rows, "seq", axis=1, tiled=True),
        ),
        query_side,
    )
    mass_all, delta_all = (
        lax.all_gather(log_mass, "seq", axis=1, tiled=True),
        lax.all_gather(row_delta, "seq", axis=1, tiled=True),
    )

    def key_side(carried, pieces, first_row):
        key_acc, value_acc = carried
        query_part, grad_part = pieces
        block_len = query_part.shape[1]
        query_pos = first_row + jnp.arange(block_len, dtype=jnp.int32)
        query_seg = segment_ids(doc_lengths, query_pos[None, :])
        mass_part = lax.dynamic_slice_in_dim(mass_all, first_row, block_len, 1)
        delta_part = lax.dynamic_slice_in_dim(delta_all, first_row, block_len, 1)
        query_h = heads_of(query_part, block_len)
        grad_h = heads_of(grad_part, block_len)
        weights_b, score_grad = gradient_terms(
            query_h,
            query_pos,
            query_seg,
            grad_h,
            mass_part,
            delta_part,
            keys_h,
            values_h,
            local_pos,
            local_seg,
        )
        key_acc = key_acc + jnp.einsum(
            "rqhk,rqhd->rkhd", score_grad, query_h, preferred_element_type=f32
        )
        value_acc = value_acc + jnp.einsum(
            "rqhk,rqhd->rkhd", weights_b, grad_h, preferred_element_type=f32
        )
        return (key_acc, value_acc)

    key_grad, value_grad = over_blocks(
        (zero_grad, zero_grad),
        (
            lax.all_gather(queries, "seq", axis=1, tiled=True),
            lax.all_gather(attended_grad, "seq", axis=1, tiled=True),
        ),
        key_side,
    )
    query_grad_b = query_grad.astype(bf16).reshape(token_count, model_width)
    key_grad_b = key_grad.astype(bf16).reshape(token_count, model_width)
    value_grad_b = value_grad.astype(bf16).reshape(token_count, model_width)
    normed_grad = jnp.einsum("te,de->td", query_grad_b, w_query, preferred_element_type=f32)
    normed_grad = normed_grad + jnp.einsum(
        "te,de->td", key_grad_b, w_key, preferred_element_type=f32
    )
    normed_grad = normed_grad + jnp.einsum(
        "te,de->td", value_grad_b, w_value, preferred_element_type=f32
    )
    input_grad = hidden_grad + norm_attn_back(normed_grad)[0]
    input_grad = input_grad.astype(bf16).reshape(row_count, length, model_width)
    return (
        output,
        input_grad,
        summed[0],
        summed[1],
        summed[2],
        summed[3],
        summed[4],
        summed[5],
        summed[6],
    )


MESH = pl.DeviceIdType.MESH
LANES = 256


def dot_nn(left, right, precision=None):
    return lax.dot_general(
        left, right, (((1,), (0,)), ((), ())), precision=precision, preferred_element_type=jnp.float32
    )


def dot_nt(left, right, precision=None):
    return lax.dot_general(
        left, right, (((1,), (1,)), ((), ())), precision=precision, preferred_element_type=jnp.float32
    )


def gelu_pair(values):
    square = values * values
    tanh = jnp.tanh(0.7978845608028654 * values * (1.0 + 0.044715 * square))
    half = 0.5 * (1.0 + tanh)
    slope = half + 0.5 * values * (1.0 - tanh * tanh) * (
        0.7978845608028654 * (1.0 + 3.0 * 0.044715 * square)
    )
    return values * half, slope


def inverse_rms(values):
    return lax.rsqrt(jnp.mean(values * values, axis=-1, keepdims=True) + epsilon)


def norm_back(values, gain, grad):
    inverse = inverse_rms(values)
    scaled = grad * gain
    return inverse * scaled - values * (
        inverse * inverse * inverse * jnp.mean(values * scaled, axis=-1, keepdims=True)
    )


class Refs(NamedTuple):
    doc_lengths: Any
    rel_table: Any
    phm_rule: Any
    gain_attn_hbm: Any
    gain_ffn_hbm: Any
    down_left_hbm: Any
    down_right_hbm: Any
    up_left_hbm: Any
    up_right_hbm: Any
    down_bias_hbm: Any
    up_bias_hbm: Any
    x_hbm: Any
    ct_hbm: Any
    w_query_hbm: Any
    w_key_hbm: Any
    w_value_hbm: Any
    w_out_hbm: Any
    w_in_hbm: Any
    w_ffout_hbm: Any
    out_hbm: Any
    grad_hbm: Any
    stats_out: Any
    w_query: Any
    w_key: Any
    w_value: Any
    w_out: Any
    w_in: Any
    w_ffout: Any
    x_rows: Any
    ct_rows: Any
    out_stage: Any
    normed: Any
    normed_b: Any
    qkv_send: Any
    slot_f: Any
    slot_c: Any
    natural_f: Any
    natural_c: Any
    keys_b: Any
    values_b: Any
    queries_b: Any
    wide: Any
    bias: Any
    att_f: Any
    att_c: Any
    att_b: Any
    mass_f: Any
    mass_c: Any
    mass_b: Any
    o_send_f: Any
    o_send_c: Any
    o_send_b: Any
    att_recv_a: Any
    att_recv_b: Any
    act: Any
    ff_out: Any
    ff_grad: Any
    down_b: Any
    up_b: Any
    down_grad: Any
    up_grad: Any
    bias_grad: Any
    hidden_grad: Any
    do_f: Any
    do_c: Any
    do_b: Any
    c_send: Any
    c_recv: Any
    part_recv: Any
    stats: Any
    gain_attn: Any
    gain_ffn: Any
    down_left: Any
    down_right: Any
    up_left: Any
    up_right: Any
    down_bias: Any
    up_bias: Any
    stats_rows: Any
    stats_core: Any
    stats_z: Any
    load_sem: Any
    small_sem: Any
    qkv_sem: Any
    slot_f_sem: Any
    slot_c_sem: Any
    pass_c_send: Any
    pass_c_recv: Any
    normed_send: Any
    normed_recv: Any
    ob_send: Any
    ob_recv: Any
    of_send: Any
    oc_send: Any
    att_sem: Any
    do_sem: Any
    do_f_sem: Any
    do_c_sem: Any
    dob_send: Any
    dob_recv: Any
    gkv_send: Any
    gq_send: Any
    gc_send: Any
    g_sem: Any
    c_send_sem: Any
    c_recv_sem: Any
    part_send_sem: Any
    part_recv_sem: Any
    st_rows_send: Any
    st_rows_recv: Any
    st_core_send: Any
    st_core_recv: Any
    st_z_send: Any
    st_z_recv: Any
    st_last_send: Any
    st_last_recv: Any
    out_sem: Any


BF16, F32 = jnp.bfloat16, jnp.float32

SCRATCH = (
    ((768, 768), BF16),
    ((768, 768), BF16),
    ((768, 768), BF16),
    ((768, 768), BF16),
    ((768, 3072), BF16),
    ((3072, 768), BF16),
    ((2, 256, 768), BF16),
    ((2, 256, 768), BF16),
    ((2, 2, 256, 768), BF16),
    ((256, 768), BF16),
    ((1024, 768), BF16),
    ((12, 192, 256), BF16),
    ((8, 192, 256), BF16),
    ((8, 192, 256), BF16),
    ((2048, 128), BF16),
    ((2048, 128), BF16),
    ((1024, 384), BF16),
    ((1024, 384), BF16),
    ((384, 512), BF16),
    ((2048, 1024), F32),
    ((8, 5, 128, 128), F32),
    ((2, 64, 1024), F32),
    ((1, 64, 1024), F32),
    ((3, 64, 1024), F32),
    ((2, 1, 1024), F32),
    ((1, 1, 1024), F32),
    ((3, 1, 1024), F32),
    ((8, 64, 256), BF16),
    ((4, 64, 256), BF16),
    ((6, 64, 256), BF16),
    ((12, 64, 256), BF16),
    ((12, 64, 256), BF16),
    ((256, 3072), BF16),
    ((256, 768), BF16),
    ((256, 768), BF16),
    ((768, 48), BF16),
    ((768, 48), BF16),
    ((768, 48), F32),
    ((768, 48), F32),
    ((8, 768), F32),
    ((2, 256, 768), F32),
    ((8, 64, 256), BF16),
    ((4, 64, 256), BF16),
    ((2, 6, 64, 256), BF16),
    ((4, 128, 256), BF16),
    ((4, 128, 256), BF16),
    ((3, 256, 768), BF16),
    ((24, 256), F32),
    ((768,), F32),
    ((768,), F32),
    ((4, 192), F32),
    ((4, 12), F32),
    ((4, 12), F32),
    ((4, 192), F32),
    ((48,), F32),
    ((768,), F32),
    ((None, 24, 256), F32),
    ((3, 24, 256), F32),
    ((4, 24, 128), F32),
)
SEMAPHORES = (
    (8,),
    (8,),
    (12,),
    (),
    (),
    (),
    (),
    (3,),
    (3,),
    (),
    (),
    (8,),
    (4,),
    (),
    (12,),
    (),
    (),
    (),
    (),
    (8,),
    (8,),
    (4,),
    (),
    (),
    (),
    (3,),
    (3,),
    (3,),
    (3,),
    (),
    (),
    (3,),
    (3,),
    (),
    (),
    (4,),
)


def layer_kernel(rows_size, *refs):
    f32 = jnp.float32
    bf16 = jnp.bfloat16
    highest_p = lax.Precision.HIGHEST
    r = Refs(*refs)
    row_place = lax.axis_index("rows")
    place = lax.axis_index("seq")
    chip = place // 2
    core = lax.rem(place, 2)
    half = chip // 2
    parity = lax.rem(chip, 2)
    inner_place = lax.rem(place, 4)
    sibling = (row_place, chip * 2 + 1 - core)
    partner = (row_place, (half * 2 + 1 - parity) * 2 + core)

    x_raw = r.out_stage.at[0]
    ct_raw = r.out_stage.at[1]
    do_send_a = r.att_recv_a
    do_send_b = r.att_recv_b
    g_recv = r.qkv_send
    hidden = r.wide.at[pl.ds(768, LANES), pl.ds(0, 768)]
    dq_acc = [r.wide.at[pl.ds(512 + 64 * tile, 64)] for tile in range(2)]
    dkv_own = r.wide.at[pl.ds(1024, 1024), pl.ds(0, 128)]
    part_own = r.wide.at[pl.ds(0, LANES), pl.ds(0, 768)]
    part_far = r.wide.at[pl.ds(LANES, LANES), pl.ds(0, 768)]
    part_send = [r.act.at[:, pl.ds(768 * number, 768)] for number in range(3)]
    turned_z = [
        [r.normed_b.at[:, pl.ds(256 * tile + 128 * number, 128)] for number in range(2)]
        for tile in range(2)
    ]

    def remote(src, dst, send_sem, recv_sem, device):
        return pltpu.make_async_remote_copy(
            src_ref=src,
            dst_ref=dst,
            send_sem=send_sem,
            recv_sem=recv_sem,
            device_id=device,
            device_id_type=MESH,
        )

    def arrived(ref, sem):
        pltpu.make_async_copy(ref, ref, sem).wait()

    loads = [
        pltpu.make_async_copy(src, dst, r.load_sem.at[index])
        for index, (src, dst) in enumerate(
            (
                (r.x_hbm, x_raw),
                (r.w_query_hbm, r.w_query),
                (r.w_key_hbm, r.w_key),
                (r.w_value_hbm, r.w_value),
                (r.ct_hbm, ct_raw),
                (r.w_out_hbm, r.w_out),
                (r.w_in_hbm, r.w_in),
                (r.w_ffout_hbm, r.w_ffout),
            )
        )
    ]
    small_loads = [
        pltpu.make_async_copy(src, dst, r.small_sem.at[index])
        for index, (src, dst) in enumerate(
            (
                (r.gain_attn_hbm, r.gain_attn),
                (r.gain_ffn_hbm, r.gain_ffn),
                (r.down_left_hbm, r.down_left),
                (r.down_right_hbm, r.down_right),
                (r.up_left_hbm, r.up_left),
                (r.up_right_hbm, r.up_right),
                (r.down_bias_hbm, r.down_bias),
                (r.up_bias_hbm, r.up_bias),
            )
        )
    ]
    loads[0].start()
    small_loads[0].start()
    barrier = pltpu.get_barrier_semaphore()
    for offset in range(1, 8):
        pl.semaphore_signal(
            barrier,
            inc=1,
            device_id=(row_place, lax.rem(place + offset, 8)),
            device_id_type=MESH,
        )
    for offset in range(1, rows_size):
        pl.semaphore_signal(
            barrier,
            inc=1,
            device_id=(lax.rem(row_place + offset, rows_size), place),
            device_id_type=MESH,
        )

    for load in loads[1:4]:
        load.start()
    for load in small_loads[1:]:
        load.start()

    first_single = r.doc_lengths[0, 1] == 0
    loads[0].wait()
    small_loads[0].wait()
    gain_attn = r.gain_attn[...].reshape(1, 768)

    def normalized(row):
        values = r.x_rows[row].astype(f32)
        return (values * inverse_rms(values) * gain_attn).astype(bf16)

    r.x_rows[1] = jnp.where(first_single, x_raw[1], x_raw[0])
    my_block = pl.ds(pl.multiple_of(inner_place * LANES, LANES), LANES)
    r.normed_b[my_block, :] = normalized(1)
    pl.semaphore_wait(barrier, 7 + rows_size - 1)

    far_block = pl.ds(
        pl.multiple_of(((1 - parity) * 2 + core) * LANES, LANES), LANES
    )
    far_other = pl.ds(
        pl.multiple_of(((1 - parity) * 2 + 1 - core) * LANES, LANES), LANES
    )
    near_other = pl.ds(pl.multiple_of((parity * 2 + 1 - core) * LANES, LANES), LANES)
    to_partner = remote(
        r.normed_b.at[my_block],
        r.normed_b.at[my_block],
        r.normed_send.at[0],
        r.normed_recv.at[0],
        partner,
    )
    to_sibling = remote(
        r.normed_b.at[my_block],
        r.normed_b.at[my_block],
        r.normed_send.at[1],
        r.normed_recv.at[1],
        sibling,
    )
    onward = remote(
        r.normed_b.at[far_block],
        r.normed_b.at[far_block],
        r.normed_send.at[2],
        r.normed_recv.at[2],
        sibling,
    )
    to_partner.start()
    to_sibling.start()
    for load in loads[4:]:
        load.start()
    r.x_rows[0] = jnp.where(first_single, x_raw[0], x_raw[1])
    r.normed[...] = normalized(0)
    for load in loads[1:4]:
        load.wait()

    for part, weight in enumerate((r.w_query, r.w_key, r.w_value)):
        turned = dot_nn(r.normed[...], weight[...]).astype(bf16).T
        for head in range(12):
            r.qkv_send[head, part * 64 : (part + 1) * 64, :] = turned[head * 64 : (head + 1) * 64]

    far_half = 2 * (1 - half)
    chips = (far_half + parity, far_half + 1 - parity, 2 * half + 1 - parity, chip)

    def exchange(
        source, full, full_sem, split, split_place, split_sem, send_sem, order, start, kinds=range(4)
    ):
        for inside in order:
            for kind in kinds:
                to_chip = chips[kind]
                head = 3 * to_chip + inside
                if inside < 2:
                    dst, sem, to_core = full.at[place], full_sem, inside
                else:
                    dst, sem, to_core = split.at[split_place], split_sem, half

                def go(dst=dst, sem=sem, head=head, device=(row_place, to_chip * 2 + to_core)):
                    copy = remote(source.at[head], dst, send_sem.at[head], sem, device)
                    if start:
                        copy.start()
                    else:
                        copy.wait_send()

                if kind < 3:
                    go()
                    continue
                pl.when(core != to_core)(go)
                if start:

                    @pl.when(core == to_core)
                    def _(dst=dst, sem=sem, head=head):
                        pltpu.make_async_copy(source.at[head], dst, sem).start()

    def exchange_qkv(start, kinds=range(4)):
        exchange(
            r.qkv_send,
            r.slot_f,
            r.slot_f_sem,
            r.slot_c,
            place,
            r.slot_c_sem,
            r.qkv_sem,
            (2, 0, 1),
            start,
            kinds,
        )

    def exchange_do(start):
        exchange(
            do_send_a, r.do_f, r.do_f_sem, r.do_c, inner_place, r.do_c_sem, r.do_sem, (0, 1, 2), start
        )

    middle = (chip == 1) | (chip == 2)

    @pl.when(middle)
    def _():
        exchange_qkv(True, (1,))

    my_heads = pl.ds(pl.multiple_of(core * 384, 128), 384)
    near_chip = pl.ds(pl.multiple_of(parity * 512, 512), 512)
    far_chip = pl.ds(pl.multiple_of((1 - parity) * 512, 512), 512)

    def project_b(lines):
        r.keys_b[lines, :] = dot_nn(r.normed_b[lines, :], r.w_key[:, my_heads]).astype(bf16)
        r.values_b[lines, :] = dot_nn(r.normed_b[lines, :], r.w_value[:, my_heads]).astype(bf16)

    arrived(r.normed_b.at[near_other], r.normed_recv.at[1])
    r.queries_b[...] = (
        dot_nn(r.normed_b[near_chip, :], r.w_query[:, my_heads]).astype(bf16).T
    )
    project_b(near_chip)
    arrived(r.normed_b.at[far_block], r.normed_recv.at[0])
    onward.start()

    @pl.when(middle)
    def _():
        exchange_qkv(True, (0, 2, 3))

    @pl.when(jnp.logical_not(middle))
    def _():
        exchange_qkv(True)

    for load in small_loads[1:]:
        load.wait()
    gain_ffn = r.gain_ffn[...].reshape(1, 768)
    down_bias = r.down_bias[...].reshape(1, 48)
    up_bias = r.up_bias[...].reshape(1, 768)

    def make_bias(slot, _):
        head = jnp.where(
            slot == 0, 3 * chip + core, jnp.where(slot == 1, 3 * chip + 2, 6 * core + slot - 2)
        )
        offset = 256 - lax.broadcasted_iota(jnp.int32, (8, 512), 1)
        bucket = bucket_of(offset)
        line = jnp.zeros((8, 512), f32)
        for number in range(32):
            line = jnp.where(bucket == number, r.rel_table[head, number], line)
        spread = pltpu.roll(
            jnp.broadcast_to(line[:1], (128, 512)), 0, 1, stride=1, stride_axis=0
        )
        r.bias[slot, 0] = jnp.full((128, 128), r.rel_table[head, 15], f32)
        r.bias[slot, 1] = spread[:, 384:512]
        r.bias[slot, 2] = spread[:, 256:384]
        r.bias[slot, 3] = spread[:, 128:256]
        r.bias[slot, 4] = jnp.full((128, 128), r.rel_table[head, 31], f32)
        return 0

    lax.fori_loop(0, 8, make_bias, 0)

    lane48 = lax.broadcasted_iota(jnp.int32, (4, 48), 1)
    term = lax.broadcasted_iota(jnp.int32, (4, 48), 0)
    fold12 = (
        lax.rem(lax.broadcasted_iota(jnp.int32, (12, 48), 1), 12)
        == lax.broadcasted_iota(jnp.int32, (12, 48), 0)
    ).astype(f32)

    def rule_lines(transposed, outer):
        made = jnp.zeros((4, 48), f32)
        for number in range(4):
            for inner in range(4):
                value = (
                    r.phm_rule[number, inner, outer]
                    if transposed
                    else r.phm_rule[number, outer, inner]
                )
                made = jnp.where((term == number) & (lane48 // 12 == inner), value, made)
        return made

    down_rules = [rule_lines(False, outer) for outer in range(4)]
    up_rules = [rule_lines(True, outer) for outer in range(4)]
    down_right_wide = dot_nn(r.down_right[...], fold12, highest_p)
    up_left_wide = dot_nn(r.up_left[...], fold12, highest_p)
    down_left_t = r.down_left[...].T
    up_right_t = r.up_right[...].T
    for outer in range(4):
        r.down_b[outer * 192 : (outer + 1) * 192, :] = dot_nn(
            down_left_t, down_rules[outer] * down_right_wide, highest_p
        ).astype(bf16)
        r.up_b[outer * 192 : (outer + 1) * 192, :] = dot_nn(
            up_right_t, up_rules[outer] * up_left_wide, highest_p
        ).astype(bf16)

    loads[4].wait()
    r.ct_rows[0] = jnp.where(first_single, ct_raw[0], ct_raw[1])
    r.ct_rows[1] = jnp.where(first_single, ct_raw[1], ct_raw[0])

    arrived(r.normed_b.at[far_other], r.normed_recv.at[2])
    project_b(far_chip)

    zero64 = jnp.zeros((64, 1024), bf16)
    zero512 = jnp.zeros((64, 512), bf16)

    def biased(scores, first_key, lane_of):
        lines = []
        for upper in range(scores.shape[0] // 128):
            pieces = []
            for lane in range(8):
                slot, query = lane_of(lane)
                distance = first_key + upper - query
                if isinstance(distance, int):
                    distance = max(-2, min(2, distance)) + 2
                else:
                    distance = jnp.clip(distance, -2, 2) + 2
                pieces.append(
                    scores[upper * 128 : (upper + 1) * 128, lane * 128 : (lane + 1) * 128]
                    + r.bias[slot, distance]
                )
            lines.append(jnp.concatenate(pieces, axis=1))
        return jnp.concatenate(lines, axis=0)

    def attend(blocks, natural, spread_q, lane_of, weighted, att, mass):
        peak = jnp.full((8, 1024), -1e30, f32)
        for block in range(blocks):
            lines = slice(block * 256, (block + 1) * 256)
            scores = biased(dot_nn(natural(lines), spread_q), 2 * block, lane_of)
            r.wide[lines, :] = scores
            peak = jnp.maximum(peak, jnp.max(scores.reshape(32, 8, 1024), axis=0))
        peak = jnp.max(peak, axis=0, keepdims=True)
        total = jnp.zeros((64, 1024), f32)
        mass_sum = jnp.zeros((8, 1024), f32)
        for block in range(blocks):
            lines = slice(block * 256, (block + 1) * 256)
            weights = jnp.exp(r.wide[lines, :] - peak)
            mass_sum = mass_sum + jnp.sum(weights.reshape(32, 8, 1024), axis=0)
            total = total + weighted(block, weights.astype(bf16))
        mass_sum = jnp.sum(mass_sum, axis=0, keepdims=True)
        total = total / mass_sum
        att[...] = total
        mass[...] = peak + jnp.log(mass_sum)
        return total

    def joined(slot, first, low, high):
        return jnp.concatenate([slot[first + u, low:high, :] for u in range(4)], axis=1)

    def lanes_b(pair):
        return lambda lane: (2 + 2 * pair + lane // 4, 4 * parity + lane % 4)

    def lanes_f(tile):
        return lambda lane: (0, 8 * tile + lane)

    def lanes_c(lane):
        return 1, 8 * core + lane

    def pair_lanes(pair):
        return pl.ds(pl.multiple_of(pair * 128, 128), 128)

    def spread_pair(first, second):
        return jnp.concatenate(
            [
                jnp.concatenate([first, zero512], axis=1),
                jnp.concatenate([zero512, second], axis=1),
            ],
            axis=0,
        )

    def pair_queries(pair):
        lines = pl.ds(pl.multiple_of(pair * 128, 128), 128)
        both = r.queries_b[lines, :]
        return spread_pair(both[:64], both[64:])

    def forward_b(pair):
        lanes = pair_lanes(pair)

        def weighted(block, weights):
            values = r.values_b[block * 256 : (block + 1) * 256, lanes].T
            return jnp.concatenate(
                [
                    dot_nn(values[:64], weights[:, :512]),
                    dot_nn(values[64:], weights[:, 512:]),
                ],
                axis=1,
            )

        attend(
            4,
            lambda lines: r.keys_b[lines, lanes],
            pair_queries(pair),
            lanes_b(pair),
            weighted,
            r.att_b.at[pair],
            r.mass_b.at[pair],
        )
        for upper in range(2):
            mine = pl.ds(pl.multiple_of(upper * 512 + core * 256, 256), 256)
            theirs = pl.ds(pl.multiple_of(upper * 512 + (1 - core) * 256, 256), 256)
            r.att_recv_b[6 * core + 2 * pair + upper] = r.att_b[pair, :, mine].astype(bf16)
            r.o_send_b[2 * pair + upper] = r.att_b[pair, :, theirs].astype(bf16)

    for pair in range(3):
        forward_b(pair)
    o_to_sibling = remote(
        r.o_send_b, r.att_recv_b.at[pl.ds(6 * core, 6)], r.ob_send, r.ob_recv, sibling
    )
    o_to_sibling.start()

    def dense(row, recv, do_send):
        attended = recv[...].reshape(768, LANES).T
        values = r.x_rows[row].astype(f32) + dot_nn(attended, r.w_out[...])
        hidden[...] = values
        r.normed[...] = (values * inverse_rms(values) * gain_ffn).astype(bf16)
        for chunk in range(3):
            columns = slice(chunk * 1024, (chunk + 1) * 1024)
            value, slope = gelu_pair(dot_nn(r.normed[...], r.w_in[:, columns]))
            r.act[:, columns] = value.astype(bf16)
            r.wide[chunk * LANES : (chunk + 1) * LANES, :] = slope
        r.ff_out[...] = dot_nn(r.act[...], r.w_ffout[...]).astype(bf16)
        squeezed_act, squeezed_slope = gelu_pair(
            dot_nn(r.ff_out[...], r.down_b[...]) + down_bias
        )
        squeezed_act = squeezed_act.astype(bf16)
        squeezed_grad = dot_nn(r.ct_rows[row], r.up_b[...]) * squeezed_slope
        squeezed_low = squeezed_grad.astype(bf16)
        r.out_stage[0, row] = (
            hidden[...]
            + r.ff_out[...].astype(f32)
            + dot_nt(squeezed_act, r.up_b[...])
            + up_bias
        ).astype(bf16)
        pltpu.make_async_copy(
            r.out_stage.at[0, row], r.out_hbm.at[row], r.out_sem.at[row]
        ).start()
        r.ff_grad[...] = (
            r.ct_rows[row].astype(f32) + dot_nt(squeezed_low, r.down_b[...])
        ).astype(bf16)
        for chunk in range(3):
            columns = slice(chunk * 1024, (chunk + 1) * 1024)
            r.act[:, columns] = (
                dot_nt(r.ff_grad[...], r.w_ffout[columns, :])
                * r.wide[chunk * LANES : (chunk + 1) * LANES, :]
            ).astype(bf16)
        normed_grad = dot_nt(r.act[...], r.w_in[...])
        values = r.ct_rows[row].astype(f32) + norm_back(hidden[...], gain_ffn, normed_grad)
        r.hidden_grad[row] = values
        turned = dot_nt(values.astype(bf16), r.w_out[...]).astype(bf16).T
        do_send[...] = turned.reshape(12, 64, LANES)
        return squeezed_act, squeezed_low, squeezed_grad

    def adapter_sums(row, squeezed_act, squeezed_low, squeezed_grad, first):
        up_part = dot_nn(r.ct_rows[row].T, squeezed_act)
        down_part = dot_nn(r.ff_out[...].T, squeezed_low)
        down_sum = jnp.sum(squeezed_grad, axis=0, keepdims=True)
        up_sum = jnp.sum(r.ct_rows[row].astype(f32), axis=0, keepdims=True)
        if first:
            r.up_grad[...] = up_part
            r.down_grad[...] = down_part
            r.bias_grad[0:1, 0:48] = down_sum
            r.bias_grad[1:2, :] = up_sum
        else:
            r.up_grad[...] += up_part
            r.down_grad[...] += down_part
            r.bias_grad[0:1, 0:48] += down_sum
            r.bias_grad[1:2, :] += up_sum

    for load in loads[5:]:
        load.wait()
    arrived(r.slot_c.at[pl.ds(4 * core, 4)], r.slot_c_sem)
    pass_c = remote(
        r.slot_c.at[pl.ds(4 * core, 4), pl.ds(64, 128)],
        r.slot_c.at[pl.ds(4 * core, 4), pl.ds(64, 128)],
        r.pass_c_send,
        r.pass_c_recv,
        sibling,
    )
    pass_c.start()
    arrived(r.att_recv_b.at[pl.ds(6 * (1 - core), 6)], r.ob_recv)
    adapter_sums(1, *dense(1, r.att_recv_b, do_send_b), True)
    o_to_sibling.wait_send()
    do_to_sibling = remote(
        do_send_b.at[pl.ds(6 * (1 - core), 6)], r.do_b.at[core], r.dob_send, r.dob_recv, sibling
    )
    do_to_sibling.start()
    r.do_b[core] = do_send_b[pl.ds(6 * core, 6)]

    def turn_slot(slot, natural, first, count):
        for u in range(count):
            lines = pl.ds(pl.multiple_of((first + u) * 256, 256), 256)
            natural[lines, :] = slot[first + u, 64:192, :].T

    def send_back(source, first, index, dst, send_sem, sem, start):
        def away():
            copy = remote(source, dst, send_sem, sem, (row_place, index))
            if start:
                copy.start()
            else:
                copy.wait_send()

        pl.when(index != place)(away)
        if start:

            @pl.when(index == place)
            def _():
                pltpu.make_async_copy(source, dst, sem).start()

    def send_o_f(tile, start):
        for u in range(4):
            index = 4 * tile + u
            send_back(
                r.o_send_f.at[index],
                None,
                index,
                r.att_recv_a.at[3 * chip + core],
                r.of_send.at[index],
                r.att_sem,
                start,
            )

    def send_o_c(start):
        for u in range(4):
            send_back(
                r.o_send_c.at[u],
                None,
                4 * core + u,
                r.att_recv_a.at[3 * chip + 2],
                r.oc_send.at[u],
                r.att_sem,
                start,
            )

    arrived(r.slot_c.at[pl.ds(4 * (1 - core), 4), pl.ds(64, 128)], r.pass_c_recv)
    turn_slot(r.slot_c, r.natural_c, 0, 8)
    total = attend(
        8,
        lambda lines: r.natural_c[lines, :],
        jnp.concatenate([joined(r.slot_c, 4 * core, 0, 64), zero64], axis=0),
        lanes_c,
        lambda block, weights: dot_nn(r.slot_c[block, 128:192, :], weights),
        r.att_c.at[0],
        r.mass_c.at[0],
    )
    for u in range(4):
        r.o_send_c[u] = total[:, u * 256 : (u + 1) * 256].astype(bf16)
    send_o_c(True)

    def back_block(first, second, spread_q, spread_do, first_key, lane_of, log_mass, delta):
        scores = biased(dot_nn(first, spread_q), first_key, lane_of)
        probs = jnp.exp(scores - log_mass)
        score_grad = probs * (dot_nn(second, spread_do) - delta)
        return probs.astype(bf16), score_grad.astype(bf16)

    def backward_b(pair):
        lanes = pair_lanes(pair)
        grads = [
            jnp.concatenate([r.do_b[0, 2 * pair + upper], r.do_b[1, 2 * pair + upper]], axis=1)
            for upper in range(2)
        ]
        delta = jnp.sum(
            jnp.concatenate(grads, axis=1).astype(f32) * r.att_b[pair], axis=0, keepdims=True
        )
        spread_q = pair_queries(pair)
        spread_do = spread_pair(*grads)
        turned_z[0][0][...] = spread_q.T
        turned_z[0][1][...] = spread_do.T
        dq = jnp.zeros((128, 1024), f32)
        for block in range(2):
            lines = slice(block * 512, (block + 1) * 512)
            keys = r.keys_b[lines, lanes]
            probs, score_grad = back_block(
                keys,
                r.values_b[lines, lanes],
                spread_q,
                spread_do,
                4 * block,
                lanes_b(pair),
                r.mass_b[pair],
                delta,
            )
            dq = dq + dot_nn(keys.T, score_grad)
            r.keys_b[lines, lanes] = dot_nn(score_grad, turned_z[0][0][...]).astype(bf16)
            r.values_b[lines, lanes] = dot_nn(probs, turned_z[0][1][...]).astype(bf16)
        first = pl.ds(pl.multiple_of(pair * 128, 64), 64)
        second = pl.ds(pl.multiple_of(pair * 128 + 64, 64), 64)
        r.queries_b[first, :] = dq[:64, :512].astype(bf16)
        r.queries_b[second, :] = dq[64:, 512:].astype(bf16)

    for copy in (to_partner, to_sibling, onward):
        copy.wait_send()
    arrived(r.do_b.at[1 - core], r.dob_recv)
    arrived(r.slot_f, r.slot_f_sem)
    turn_slot(r.slot_f, r.natural_f, 0, 8)

    def forward_f(tile):
        total = attend(
            8,
            lambda lines: r.natural_f[lines, :],
            jnp.concatenate([joined(r.slot_f, 4 * tile, 0, 64), zero64], axis=0),
            lanes_f(tile),
            lambda block, weights: dot_nn(r.slot_f[block, 128:192, :], weights),
            r.att_f.at[tile],
            r.mass_f.at[tile],
        )
        for u in range(4):
            r.o_send_f[4 * tile + u] = total[:, u * 256 : (u + 1) * 256].astype(bf16)
        send_o_f(tile, True)

    for tile in (1 - half, half):
        forward_f(tile)

    backward_b(0)

    arrived(r.att_recv_a, r.att_sem)
    kept = dense(0, r.att_recv_a, do_send_a)
    exchange_qkv(False)
    exchange_do(True)
    adapter_sums(0, *kept, False)

    backward_b(1)
    backward_b(2)

    def project_back(lines):
        return dot_nt(r.keys_b[lines, :], r.w_key[:, my_heads]) + dot_nt(
            r.values_b[lines, :], r.w_value[:, my_heads]
        )

    my_half = pl.ds(pl.multiple_of(core * LANES, LANES), LANES)
    their_half = pl.ds(pl.multiple_of((1 - core) * LANES, LANES), LANES)
    part_far[...] = project_back(far_block)
    part_send[0][...] = project_back(far_other).astype(bf16)
    far_copy = remote(
        part_send[0], r.part_recv.at[0], r.part_send_sem.at[0], r.part_recv_sem.at[0], sibling
    )
    far_copy.start()
    arrived(r.part_recv.at[0], r.part_recv_sem.at[0])
    part_send[2][...] = (part_far[...] + r.part_recv[0].astype(f32)).astype(bf16)
    partner_copy = remote(
        part_send[2], r.part_recv.at[2], r.part_send_sem.at[2], r.part_recv_sem.at[2], partner
    )
    partner_copy.start()

    def set_tile(slot_index, queries, grads):
        spread_q = jnp.concatenate([queries, zero64], axis=0)
        spread_do = jnp.concatenate([zero64, grads], axis=0)
        turned_z[slot_index][0][...] = spread_q.T
        turned_z[slot_index][1][...] = spread_do.T
        return spread_q, spread_do

    def merged(score_grad, probs, slot_index):
        queries, grads = turned_z[slot_index]
        return dot_nn(score_grad, queries[...]) + dot_nn(probs, grads[...])

    def key_lines(block):
        return pl.ds(pl.multiple_of(block * 512, 512), 512)

    def keys_t(slot, block):
        return jnp.concatenate([slot[2 * block + u, 64:128, :] for u in range(2)], axis=1)

    arrived(r.do_f, r.do_f_sem)
    deltas = []
    spreads = []
    for tile in range(2):
        grads = joined(r.do_f, 4 * tile, 0, 64)
        spreads.append(set_tile(tile, joined(r.slot_f, 4 * tile, 0, 64), grads))
        deltas.append(jnp.sum(grads.astype(f32) * r.att_f[tile], axis=0, keepdims=True))
        dq_acc[tile][...] = jnp.zeros((64, 1024), f32)

    def send_g_f(index, start):
        send_back(
            r.slot_f.at[index, pl.ds(64, 128)],
            None,
            index,
            g_recv.at[3 * chip + core, pl.ds(64, 128)],
            r.gkv_send.at[index],
            r.g_sem,
            start,
        )

    def send_dq_f(index, start):
        send_back(
            r.slot_f.at[index, pl.ds(0, 64)],
            None,
            index,
            g_recv.at[3 * chip + core, pl.ds(0, 64)],
            r.gq_send.at[index],
            r.g_sem,
            start,
        )

    def whole_block(block):
        natural = r.natural_f[key_lines(block), :]
        turned_keys = keys_t(r.slot_f, block)
        made = jnp.zeros((512, 128), f32)
        for tile in range(2):
            probs, score_grad = back_block(
                natural,
                natural,
                *spreads[tile],
                4 * block,
                lanes_f(tile),
                r.mass_f[tile],
                deltas[tile],
            )
            dq_acc[tile][...] += dot_nn(turned_keys, score_grad)
            made = made + merged(score_grad, probs, tile)
        turned = made.astype(bf16).T
        for u in range(2):
            r.slot_f[2 * block + u, 64:192, :] = turned[:, u * 256 : (u + 1) * 256]
            send_g_f(2 * block + u, True)

    for step in range(4):
        whole_block(far_half + step if step < 2 else 2 * half + step - 2)
    for step in range(8):
        index = 4 * (1 - half) + step if step < 4 else 4 * half + step - 4
        r.slot_f[index, 0:64, :] = r.wide[
            pl.ds(pl.multiple_of(512 + 64 * (1 - half if step < 4 else half), 64), 64),
            (step % 4) * 256 : (step % 4 + 1) * 256,
        ].astype(bf16)
        send_dq_f(index, True)

    arrived(r.do_c, r.do_c_sem)
    grads_c = joined(r.do_c, 0, 0, 64)
    spread_qc, spread_doc = set_tile(0, joined(r.slot_c, 4 * core, 0, 64), grads_c)
    delta_c = jnp.sum(grads_c.astype(f32) * r.att_c[0], axis=0, keepdims=True)
    dq_acc[0][...] = jnp.zeros((64, 1024), f32)

    def split_block(block):
        natural = r.natural_c[key_lines(block), :]
        probs, score_grad = back_block(
            natural, natural, spread_qc, spread_doc, 4 * block, lanes_c, r.mass_c[0], delta_c
        )
        dq_acc[0][...] += dot_nn(keys_t(r.slot_c, block), score_grad)
        return merged(score_grad, probs, 0)

    def split_theirs(step):
        turned = split_block(2 * (1 - core) + step).astype(bf16).T
        for u in range(2):
            r.c_send[2 * step + u] = turned[:, u * 256 : (u + 1) * 256]

    def split_mine(step):
        dkv_own[key_lines(step), :] = split_block(2 * core + step)

    for step in range(2):
        split_theirs(step)
    c_copy = remote(r.c_send, r.c_recv, r.c_send_sem, r.c_recv_sem, sibling)
    c_copy.start()
    for step in range(2):
        split_mine(step)

    arrived(r.c_recv, r.c_recv_sem)

    def send_g_c(start):
        for u in range(4):
            send_back(
                r.slot_c.at[4 * core + u],
                None,
                4 * core + u,
                g_recv.at[3 * chip + 2],
                r.gc_send.at[u],
                r.g_sem,
                start,
            )

    pass_c.wait_send()
    for u in range(4):
        r.slot_c[4 * core + u, 0:64, :] = dq_acc[0][:, u * 256 : (u + 1) * 256].astype(bf16)
        r.slot_c[4 * core + u, 64:192, :] = (
            dkv_own[u * 256 : (u + 1) * 256, :].T + r.c_recv[u].astype(f32)
        ).astype(bf16)
    send_g_c(True)

    column48 = lax.broadcasted_iota(jnp.int32, (48, 16), 0) // 12
    lane16 = lax.broadcasted_iota(jnp.int32, (48, 16), 1)

    def kron_back(grad, left, right_wide, rules, transposed):
        left_grad = jnp.zeros((4, 192), f32)
        right_grad = jnp.zeros((4, 48), f32)
        rule_grad = jnp.zeros((4, 16), f32)
        for outer in range(4):
            block = grad[outer * 192 : (outer + 1) * 192, :]
            left_grad = left_grad + dot_nt(rules[outer] * right_wide, block, highest_p)
            contracted = dot_nn(left, block, highest_p)
            right_grad = right_grad + contracted * rules[outer]
            target = column48 * 4 + outer if transposed else outer * 4 + column48
            rule_grad = rule_grad + dot_nn(
                contracted * right_wide, (target == lane16).astype(f32), highest_p
            )
        return left_grad, dot_nt(right_grad, fold12, highest_p), rule_grad

    dl_grad, dr_grad, rule_down = kron_back(
        r.down_grad, r.down_left[...], down_right_wide, down_rules, False
    )
    ur_grad, ul_grad, rule_up = kron_back(
        r.up_grad, r.up_right[...], up_left_wide, up_rules, True
    )
    r.stats[...] = jnp.zeros_like(r.stats)
    r.stats[0:4, 0:192] = dl_grad
    r.stats[4:8, 0:192] = ur_grad
    r.stats[8:12, 0:12] = dr_grad
    r.stats[8:12, 128:140] = ul_grad
    r.stats[12:16, 0:16] = rule_down + rule_up
    r.stats[16:17, 0:48] = r.bias_grad[0:1, 0:48]
    for third in range(3):
        r.stats[17 + third : 18 + third, :] = r.bias_grad[1:2, third * 256 : (third + 1) * 256]

    def rows_copy(offset):
        return remote(
            r.stats,
            r.stats_rows.at[row_place],
            r.st_rows_send.at[offset - 1],
            r.st_rows_recv.at[offset - 1],
            (lax.rem(row_place + offset, rows_size), place),
        )

    for offset in range(1, rows_size):
        rows_copy(offset).start()
    r.stats_rows[row_place] = r.stats[...]

    part_send[1][...] = (
        project_back(near_other)
        + dot_nt(r.queries_b[:, their_half].T, r.w_query[:, my_heads])
    ).astype(bf16)
    near_copy = remote(
        part_send[1], r.part_recv.at[1], r.part_send_sem.at[1], r.part_recv_sem.at[1], sibling
    )
    near_copy.start()

    def finish_row(row, normed_grad):
        r.out_stage[1, row] = (
            r.hidden_grad[row] + norm_back(r.x_rows[row].astype(f32), gain_attn, normed_grad)
        ).astype(bf16)
        pltpu.make_async_copy(
            r.out_stage.at[1, row], r.grad_hbm.at[row], r.out_sem.at[2 + row]
        ).start()

    part_own[...] = project_back(my_block) + dot_nt(
        r.queries_b[:, my_half].T, r.w_query[:, my_heads]
    )

    my_lanes = pl.ds(pl.multiple_of(core * 128, 128), 128)
    other_lanes = pl.ds(pl.multiple_of((1 - core) * 128, 128), 128)
    for offset in range(1, rows_size):
        rows_copy(offset).wait()
    summed = r.stats_rows[0]
    for number in range(1, rows_size):
        summed = summed + r.stats_rows[number]
    r.stats_core[0] = summed
    core_copy = remote(
        r.stats_core.at[0, :, other_lanes],
        r.stats_core.at[1, :, other_lanes],
        r.st_core_send,
        r.st_core_recv,
        sibling,
    )
    core_copy.start()

    core_copy.wait_send()
    arrived(r.stats_core.at[1, :, my_lanes], r.st_core_recv)
    r.stats_z[chip] = r.stats_core[0, :, my_lanes] + r.stats_core[1, :, my_lanes]

    def z_copy(offset):
        return remote(
            r.stats_z.at[chip],
            r.stats_z.at[chip],
            r.st_z_send.at[offset - 1],
            r.st_z_recv.at[offset - 1],
            (row_place, lax.rem(chip + offset, 4) * 2 + core),
        )

    for offset in range(1, 4):
        z_copy(offset).start()

    arrived(r.part_recv.at[1], r.part_recv_sem.at[1])
    arrived(r.part_recv.at[2], r.part_recv_sem.at[2])
    finish_row(
        1, part_own[...] + r.part_recv[1].astype(f32) + r.part_recv[2].astype(f32)
    )

    for offset in range(1, 4):
        z_copy(offset).wait()
    r.stats_core[2, :, my_lanes] = (r.stats_z[0] + r.stats_z[1]) + (r.stats_z[2] + r.stats_z[3])
    last_copy = remote(
        r.stats_core.at[2, :, my_lanes],
        r.stats_core.at[2, :, my_lanes],
        r.st_last_send,
        r.st_last_recv,
        sibling,
    )
    last_copy.start()

    arrived(g_recv, r.g_sem)
    turned_grad = jnp.zeros((768, LANES), f32)
    for part, weight in enumerate((r.w_query, r.w_key, r.w_value)):
        turned_grad = turned_grad + dot_nn(
            weight[...], g_recv[:, part * 64 : (part + 1) * 64, :].reshape(768, LANES)
        )
    finish_row(0, turned_grad.T)
    last_copy.wait_send()
    arrived(r.stats_core.at[2, :, other_lanes], r.st_last_recv)
    r.stats_out[...] = r.stats_core[2]

    for copy in (do_to_sibling, c_copy):
        copy.wait_send()
    for copy in (far_copy, near_copy, partner_copy):
        copy.wait_send()
    exchange_do(False)
    for tile in range(2):
        send_o_f(tile, False)
    send_o_c(False)
    send_g_c(False)
    for index in range(8):
        send_g_f(index, False)
        send_dq_f(index, False)
    for row in range(2):
        pltpu.make_async_copy(
            r.out_stage.at[0, row], r.out_hbm.at[row], r.out_sem.at[row]
        ).wait()
        pltpu.make_async_copy(
            r.out_stage.at[1, row], r.grad_hbm.at[row], r.out_sem.at[2 + row]
        ).wait()


def finish_kernel(
    doc_lengths,
    stats,
    out_from,
    grad_from,
    out_to,
    grad_to,
    rule_out,
    dl_out,
    dr_out,
    ul_out,
    ur_out,
    db_out,
    ub_out,
    stage,
    sem,
):
    first_single = doc_lengths[0, 1] == 0
    gets, puts = [], []
    for number, (source, target) in enumerate(((grad_from, grad_to), (out_from, out_to))):
        for row in range(2):
            to_row = jnp.where(first_single, row, 1 - row)
            gets.append(
                pltpu.make_async_copy(
                    source.at[row], stage.at[number, row], sem.at[0, number, row]
                )
            )
            puts.append(
                pltpu.make_async_copy(
                    stage.at[number, row], target.at[to_row], sem.at[1, number, row]
                )
            )
    for get in gets:
        get.start()
    for outer in range(4):
        rule_out[:, outer, :] = stats[12:16, 4 * outer : 4 * outer + 4]
    dl_out[...] = stats[0:4, 0:192]
    ur_out[...] = stats[4:8, 0:192]
    dr_out[...] = stats[8:12, 0:12]
    ul_out[...] = stats[8:12, 128:140]
    db_out[...] = stats[16:17, 0:48].reshape(48)
    ub_out[...] = jnp.concatenate(
        [stats[17 + third : 18 + third, :] for third in range(3)], axis=1
    ).reshape(768)
    for get, put in zip(gets, puts):
        get.wait()
        put.start()
    for put in puts:
        put.wait()


def layer_on_slice(rows_size, *arrays):
    (
        inputs,
        doc_lengths,
        w_query,
        w_key,
        w_value,
        w_out,
        w_in,
        w_ffout,
        rel_table,
        gain_attn,
        gain_ffn,
        phm_rule,
        down_left,
        down_right,
        up_left,
        up_right,
        down_bias,
        up_bias,
        cotangent,
    ) = arrays
    f32 = jnp.float32
    bf16 = jnp.bfloat16
    shape = jax.ShapeDtypeStruct
    vmem = pl.BlockSpec(memory_space=pltpu.VMEM)
    smem = pl.BlockSpec(memory_space=pltpu.SMEM)
    hbm = pl.BlockSpec(memory_space=pl.ANY)
    dma = pltpu.SemaphoreType.DMA
    results = pl.pallas_call(
        functools.partial(layer_kernel, rows_size),
        out_shape=[
            shape(inputs.shape, bf16),
            shape(inputs.shape, bf16),
            shape((24, 256), f32),
        ],
        in_specs=[smem] * 3 + [hbm] * 16,
        out_specs=[hbm] * 2 + [vmem],
        scratch_shapes=[
            pltpu.VMEM(tuple(rows_size if size is None else size for size in sizes), kind)
            for sizes, kind in SCRATCH
        ]
        + [dma(sizes) for sizes in SEMAPHORES],
        compiler_params=pltpu.CompilerParams(
            collective_id=0, has_side_effects=True, vmem_limit_bytes=56 * 1024 * 1024
        ),
        name="encoder_layer",
    )(
        doc_lengths,
        rel_table.T,
        phm_rule,
        gain_attn,
        gain_ffn,
        down_left,
        down_right,
        up_left,
        up_right,
        down_bias,
        up_bias,
        inputs,
        cotangent,
        w_query,
        w_key,
        w_value,
        w_out,
        w_in,
        w_ffout,
    )
    return pl.pallas_call(
        finish_kernel,
        out_shape=[
            shape(inputs.shape, bf16),
            shape(inputs.shape, bf16),
            shape(phm_rule.shape, f32),
            shape((4, 192), f32),
            shape((4, 12), f32),
            shape((4, 12), f32),
            shape((4, 192), f32),
            shape((48,), f32),
            shape((768,), f32),
        ],
        in_specs=[smem, vmem] + [hbm] * 2,
        out_specs=[hbm] * 2 + [vmem] * 7,
        scratch_shapes=[pltpu.VMEM((2, 2, LANES, 768), bf16), dma((2, 2, 2))],
        name="finish",
    )(doc_lengths, results[2], results[0], results[1])


def pick(rows_size, seq_size, *arrays):
    inputs, doc_lengths = arrays[:2]
    fits = (
        seq_size == 8
        and inputs.shape == (2, LANES, 768)
        and doc_lengths.shape == (2, 2)
        and arrays[8].shape == (32, 12)
        and arrays[6].shape == (768, 3072)
    )
    return layer_on_slice(rows_size, *arrays) if fits else local(*arrays)


def solution(mesh):
    return jax.shard_map(
        functools.partial(pick, mesh.shape["rows"], mesh.shape["seq"]),
        mesh=mesh,
        in_specs=(
            P("rows", "seq", None),
            P("rows", None),
            P(),
            P(),
            P(),
            P(),
            P(),
            P(),
            P(),
            P(),
            P(),
            P(),
            P(),
            P(),
            P(),
            P(),
            P(),
            P(),
            P("rows", "seq", None),
        ),
        out_specs=(
            P("rows", "seq", None),
            P("rows", "seq", None),
            P(),
            P(),
            P(),
            P(),
            P(),
            P(),
            P(),
        ),
        check_vma=False,
    )
```

```python
import functools
import math
from typing import Any, NamedTuple

import jax
import jax.numpy as jnp
from jax import lax
from jax.experimental import pallas as pl
from jax.experimental.pallas import tpu as pltpu
from jax.sharding import PartitionSpec as P

epsilon = 1e-06
highest = lax.Precision.HIGHEST
bucket_edges = (12, 16, 23, 32, 46, 64, 91)


def smooth_gelu(values):
    return (
        0.5
        * values
        * (1.0 + jnp.tanh(0.7978845608028654 * (values + 0.044715 * values * values * values)))
    )


def rms_norm(values, gain):
    return values * lax.rsqrt(jnp.mean(values * values, axis=-1, keepdims=True) + epsilon) * gain


def bucket_of(offset):
    magnitude = jnp.abs(offset)
    larger = jnp.full(offset.shape, 8, jnp.int32)
    for edge in bucket_edges:
        larger = larger + (magnitude >= edge).astype(jnp.int32)
    inside = jnp.where(magnitude < 8, magnitude, larger)
    return inside + jnp.where(offset > 0, 16, 0).astype(jnp.int32)


def segment_ids(lengths, token_positions):
    doc_ends = jnp.cumsum(lengths, axis=-1, dtype=jnp.int32)
    return jnp.sum(
        (token_positions[..., :, None] >= doc_ends[..., None, :]).astype(jnp.int32),
        axis=-1,
        dtype=jnp.int32,
    )


def kron_sum(rule_part, left_part, right_part):
    blocks = jnp.einsum("iab,ip,iq->apbq", rule_part, left_part, right_part, precision=highest)
    return blocks.reshape(
        rule_part.shape[1] * left_part.shape[1], rule_part.shape[2] * right_part.shape[1]
    )


def pair_bias(query_pos, key_pos, rel_table):
    buckets = bucket_of(key_pos[None, :] - query_pos[:, None])
    onehot = (buckets[:, :, None] == jnp.arange(rel_table.shape[0], dtype=jnp.int32)).astype(
        jnp.bfloat16
    )
    table_high = rel_table.astype(jnp.bfloat16)
    table_rest = (rel_table - table_high.astype(jnp.float32)).astype(jnp.bfloat16)
    high_part = jnp.einsum("qkb,bh->qhk", onehot, table_high, preferred_element_type=jnp.float32)
    rest_part = jnp.einsum("qkb,bh->qhk", onehot, table_rest, preferred_element_type=jnp.float32)
    return high_part + rest_part


def over_blocks(carried, pieces, blockwise):
    total_len = pieces[0].shape[1]
    block_len = math.gcd(total_len, 512)

    def one_step(block_index, inner_state):
        begin_row = block_index * block_len
        sliced = tuple(
            (lax.dynamic_slice_in_dim(member, begin_row, block_len, 1) for member in pieces)
        )
        return blockwise(inner_state, sliced, begin_row)

    return lax.fori_loop(0, total_len // block_len, one_step, carried)


def local(
    inputs,
    doc_lengths,
    w_query,
    w_key,
    w_value,
    w_out,
    w_in,
    w_ffout,
    rel_table,
    gain_attn,
    gain_ffn,
    phm_rule,
    down_left,
    down_right,
    up_left,
    up_right,
    down_bias,
    up_bias,
    cotangent,
):
    row_count, length, model_width = inputs.shape
    head_count = rel_table.shape[1]
    head_dim = model_width // head_count
    seq_place = lax.axis_index("seq")
    token_count = row_count * length
    local_pos = seq_place * length + jnp.arange(length, dtype=jnp.int32)
    local_seg = segment_ids(doc_lengths, local_pos[None, :])
    bf16 = jnp.bfloat16
    f32 = jnp.float32

    def heads_of(matrix, block_len):
        return matrix.reshape(row_count, block_len, head_count, head_dim)

    def norm_attn(values):
        return rms_norm(values, gain_attn)

    def norm_ffn(values):
        return rms_norm(values, gain_ffn)

    source = inputs.astype(f32).reshape(token_count, model_width)
    normed, norm_attn_back = jax.vjp(norm_attn, source)
    normed_b = normed.astype(bf16)
    queries = (
        jnp.dot(normed_b, w_query, preferred_element_type=f32)
        .astype(bf16)
        .reshape(row_count, length, model_width)
    )
    key_rows = (
        jnp.dot(normed_b, w_key, preferred_element_type=f32)
        .astype(bf16)
        .reshape(row_count, length, model_width)
    )
    value_rows = (
        jnp.dot(normed_b, w_value, preferred_element_type=f32)
        .astype(bf16)
        .reshape(row_count, length, model_width)
    )
    queries_h = heads_of(queries, length)
    keys_h = heads_of(key_rows, length)
    values_h = heads_of(value_rows, length)

    def scores_for(query_h, query_pos, query_seg, key_h, key_pos, key_seg):
        scores = jnp.einsum("rqhd,rkhd->rqhk", query_h, key_h, preferred_element_type=f32)
        scores = scores + pair_bias(query_pos, key_pos, rel_table)[None]
        allowed = (query_seg[:, :, None] == key_seg[:, None, :])[:, :, None, :]
        return (scores, allowed)

    def forward_piece(carried, pieces, first_row):
        weighted, running, mass_sum = carried
        key_part, value_part = pieces
        block_len = key_part.shape[1]
        key_pos = first_row + jnp.arange(block_len, dtype=jnp.int32)
        key_seg = segment_ids(doc_lengths, key_pos[None, :])
        scores, allowed = scores_for(
            queries_h, local_pos, local_seg, heads_of(key_part, block_len), key_pos, key_seg
        )
        scores = jnp.where(allowed, scores, -1e30)
        raised = jnp.maximum(running, jnp.max(scores, axis=-1))
        weights = jnp.where(allowed, jnp.exp(scores - raised[..., None]), 0.0)
        rescale = jnp.exp(running - raised)
        mass_sum = mass_sum * rescale + jnp.sum(weights, axis=-1)
        weighted = weighted * rescale[..., None] + jnp.einsum(
            "rqhk,rkhd->rqhd",
            weights.astype(bf16),
            heads_of(value_part, block_len),
            preferred_element_type=f32,
        )
        return (weighted, raised, mass_sum)

    start_state = (
        jnp.zeros((row_count, length, head_count, head_dim), f32),
        jnp.full((row_count, length, head_count), -1e30, f32),
        jnp.zeros((row_count, length, head_count), f32),
    )
    weighted, running, mass_sum = over_blocks(
        start_state,
        (
            lax.all_gather(key_rows, "seq", axis=1, tiled=True),
            lax.all_gather(value_rows, "seq", axis=1, tiled=True),
        ),
        forward_piece,
    )
    attended = weighted / mass_sum[..., None]
    log_mass = running + jnp.log(mass_sum)
    attended_b = attended.astype(bf16).reshape(token_count, model_width)
    hidden = source + jnp.dot(attended_b, w_out, preferred_element_type=f32)
    normed_ffn, norm_ffn_back = jax.vjp(norm_ffn, hidden)
    inner = jnp.dot(normed_ffn.astype(bf16), w_in, preferred_element_type=f32)
    activated, gelu_back = jax.vjp(smooth_gelu, inner)
    activated_b = activated.astype(bf16)
    ff_out = jnp.dot(activated_b, w_ffout, preferred_element_type=f32).astype(bf16)
    down_full, down_back = jax.vjp(kron_sum, phm_rule, down_left, down_right)
    up_full, up_back = jax.vjp(kron_sum, phm_rule, up_left, up_right)
    down_b = down_full.astype(bf16)
    up_b = up_full.astype(bf16)
    squeezed = jnp.dot(ff_out, down_b, preferred_element_type=f32) + down_bias
    squeezed_act, squeeze_back = jax.vjp(smooth_gelu, squeezed)
    squeezed_act_b = squeezed_act.astype(bf16)
    expanded = jnp.dot(squeezed_act_b, up_b, preferred_element_type=f32) + up_bias
    result = hidden + ff_out.astype(f32) + expanded
    output = result.astype(bf16).reshape(row_count, length, model_width)
    upstream = cotangent.astype(f32).reshape(token_count, model_width)
    up_bias_grad = jnp.sum(upstream, axis=0)
    upstream_b = upstream.astype(bf16)
    up_matrix_grad = jnp.einsum("ta,td->ad", squeezed_act_b, upstream_b, preferred_element_type=f32)
    squeezed_grad = squeeze_back(
        jnp.einsum("td,ad->ta", upstream_b, up_b, preferred_element_type=f32)
    )[0]
    down_bias_grad = jnp.sum(squeezed_grad, axis=0)
    squeezed_low = squeezed_grad.astype(bf16)
    down_matrix_grad = jnp.einsum("td,ta->da", ff_out, squeezed_low, preferred_element_type=f32)
    rule_down, down_left_grad, down_right_grad = down_back(down_matrix_grad)
    rule_up, up_left_grad, up_right_grad = up_back(up_matrix_grad)
    summed = lax.psum(
        (
            rule_down + rule_up,
            down_left_grad,
            down_right_grad,
            up_left_grad,
            up_right_grad,
            down_bias_grad,
            up_bias_grad,
        ),
        ("rows", "seq"),
    )
    ff_grad = upstream + jnp.einsum("ta,da->td", squeezed_low, down_b, preferred_element_type=f32)
    ff_grad_b = ff_grad.astype(bf16)
    inner_grad = gelu_back(jnp.einsum("td,fd->tf", ff_grad_b, w_ffout, preferred_element_type=f32))[
        0
    ]
    inner_grad_b = inner_grad.astype(bf16)
    hidden_grad = (
        upstream
        + norm_ffn_back(jnp.einsum("tf,df->td", inner_grad_b, w_in, preferred_element_type=f32))[0]
    )
    hidden_grad_b = hidden_grad.astype(bf16)
    attended_grad = jnp.einsum(
        "te,de->td", hidden_grad_b, w_out, preferred_element_type=f32
    ).astype(bf16)
    attended_grad = attended_grad.reshape(row_count, length, model_width)
    attended_grad_h = heads_of(attended_grad, length)
    row_delta = jnp.sum(attended_grad_h.astype(f32) * attended, axis=-1)

    def gradient_terms(
        query_h,
        query_pos,
        query_seg,
        grad_h,
        mass_part,
        delta_part,
        key_h,
        value_h,
        key_pos,
        key_seg,
    ):
        scores, allowed = scores_for(query_h, query_pos, query_seg, key_h, key_pos, key_seg)
        weights = jnp.exp(jnp.where(allowed, scores - mass_part[..., None], -1e30))
        weights_grad = jnp.einsum("rqhd,rkhd->rqhk", grad_h, value_h, preferred_element_type=f32)
        score_grad = (weights * (weights_grad - delta_part[..., None])).astype(bf16)
        return (weights.astype(bf16), score_grad)

    zero_grad = jnp.zeros((row_count, length, head_count, head_dim), f32)

    def query_side(carried, pieces, first_row):
        key_part, value_part = pieces
        block_len = key_part.shape[1]
        key_pos = first_row + jnp.arange(block_len, dtype=jnp.int32)
        key_seg = segment_ids(doc_lengths, key_pos[None, :])
        key_h = heads_of(key_part, block_len)
        weights_b, score_grad = gradient_terms(
            queries_h,
            local_pos,
            local_seg,
            attended_grad_h,
            log_mass,
            row_delta,
            key_h,
            heads_of(value_part, block_len),
            key_pos,
            key_seg,
        )
        return carried + jnp.einsum(
            "rqhk,rkhd->rqhd", score_grad, key_h, preferred_element_type=f32
        )

    query_grad = over_blocks(
        zero_grad,
        (
            lax.all_gather(key_rows, "seq", axis=1, tiled=True),
            lax.all_gather(value_rows, "seq", axis=1, tiled=True),
        ),
        query_side,
    )
    mass_all, delta_all = (
        lax.all_gather(log_mass, "seq", axis=1, tiled=True),
        lax.all_gather(row_delta, "seq", axis=1, tiled=True),
    )

    def key_side(carried, pieces, first_row):
        key_acc, value_acc = carried
        query_part, grad_part = pieces
        block_len = query_part.shape[1]
        query_pos = first_row + jnp.arange(block_len, dtype=jnp.int32)
        query_seg = segment_ids(doc_lengths, query_pos[None, :])
        mass_part = lax.dynamic_slice_in_dim(mass_all, first_row, block_len, 1)
        delta_part = lax.dynamic_slice_in_dim(delta_all, first_row, block_len, 1)
        query_h = heads_of(query_part, block_len)
        grad_h = heads_of(grad_part, block_len)
        weights_b, score_grad = gradient_terms(
            query_h,
            query_pos,
            query_seg,
            grad_h,
            mass_part,
            delta_part,
            keys_h,
            values_h,
            local_pos,
            local_seg,
        )
        key_acc = key_acc + jnp.einsum(
            "rqhk,rqhd->rkhd", score_grad, query_h, preferred_element_type=f32
        )
        value_acc = value_acc + jnp.einsum(
            "rqhk,rqhd->rkhd", weights_b, grad_h, preferred_element_type=f32
        )
        return (key_acc, value_acc)

    key_grad, value_grad = over_blocks(
        (zero_grad, zero_grad),
        (
            lax.all_gather(queries, "seq", axis=1, tiled=True),
            lax.all_gather(attended_grad, "seq", axis=1, tiled=True),
        ),
        key_side,
    )
    query_grad_b = query_grad.astype(bf16).reshape(token_count, model_width)
    key_grad_b = key_grad.astype(bf16).reshape(token_count, model_width)
    value_grad_b = value_grad.astype(bf16).reshape(token_count, model_width)
    normed_grad = jnp.einsum("te,de->td", query_grad_b, w_query, preferred_element_type=f32)
    normed_grad = normed_grad + jnp.einsum(
        "te,de->td", key_grad_b, w_key, preferred_element_type=f32
    )
    normed_grad = normed_grad + jnp.einsum(
        "te,de->td", value_grad_b, w_value, preferred_element_type=f32
    )
    input_grad = hidden_grad + norm_attn_back(normed_grad)[0]
    input_grad = input_grad.astype(bf16).reshape(row_count, length, model_width)
    return (
        output,
        input_grad,
        summed[0],
        summed[1],
        summed[2],
        summed[3],
        summed[4],
        summed[5],
        summed[6],
    )


MESH = pl.DeviceIdType.MESH
LANES = 256


def dot_nn(left, right, precision=None):
    return lax.dot_general(
        left, right, (((1,), (0,)), ((), ())), precision=precision, preferred_element_type=jnp.float32
    )


def dot_nt(left, right, precision=None):
    return lax.dot_general(
        left, right, (((1,), (1,)), ((), ())), precision=precision, preferred_element_type=jnp.float32
    )


def gelu_pair(values):
    square = values * values
    tanh = jnp.tanh(0.7978845608028654 * values * (1.0 + 0.044715 * square))
    half = 0.5 * (1.0 + tanh)
    slope = half + 0.5 * values * (1.0 - tanh * tanh) * (
        0.7978845608028654 * (1.0 + 3.0 * 0.044715 * square)
    )
    return values * half, slope


def inverse_rms(values):
    return lax.rsqrt(jnp.mean(values * values, axis=-1, keepdims=True) + epsilon)


def norm_back(values, gain, grad):
    inverse = inverse_rms(values)
    scaled = grad * gain
    return inverse * scaled - values * (
        inverse * inverse * inverse * jnp.mean(values * scaled, axis=-1, keepdims=True)
    )


class Refs(NamedTuple):
    doc_lengths: Any
    rel_table: Any
    phm_rule: Any
    gain_attn_hbm: Any
    gain_ffn_hbm: Any
    down_left_hbm: Any
    down_right_hbm: Any
    up_left_hbm: Any
    up_right_hbm: Any
    down_bias_hbm: Any
    up_bias_hbm: Any
    x_hbm: Any
    ct_hbm: Any
    w_query_hbm: Any
    w_key_hbm: Any
    w_value_hbm: Any
    w_out_hbm: Any
    w_in_hbm: Any
    w_ffout_hbm: Any
    out_hbm: Any
    grad_hbm: Any
    stats_out: Any
    w_query: Any
    w_key: Any
    w_value: Any
    w_out: Any
    w_in: Any
    w_ffout: Any
    x_rows: Any
    ct_rows: Any
    out_stage: Any
    normed: Any
    normed_b: Any
    qkv_send: Any
    slot_f: Any
    slot_c: Any
    natural_f: Any
    natural_c: Any
    keys_b: Any
    values_b: Any
    queries_b: Any
    wide: Any
    bias: Any
    att_f: Any
    att_c: Any
    att_b: Any
    mass_f: Any
    mass_c: Any
    mass_b: Any
    sum_b: Any
    o_send_f: Any
    o_send_c: Any
    o_send_b: Any
    att_recv_a: Any
    att_recv_b: Any
    act: Any
    ff_out: Any
    ff_grad: Any
    down_b: Any
    up_b: Any
    down_grad: Any
    up_grad: Any
    bias_grad: Any
    hidden_grad: Any
    do_f: Any
    do_c: Any
    do_b: Any
    c_send: Any
    c_recv: Any
    part_recv: Any
    stats: Any
    gain_attn: Any
    gain_ffn: Any
    down_left: Any
    down_right: Any
    up_left: Any
    up_right: Any
    down_bias: Any
    up_bias: Any
    stats_rows: Any
    stats_core: Any
    stats_z: Any
    load_sem: Any
    small_sem: Any
    qkv_sem: Any
    slot_f_sem: Any
    slot_c_sem: Any
    pass_c_send: Any
    pass_c_recv: Any
    normed_send: Any
    normed_recv: Any
    ob_send: Any
    ob_recv: Any
    of_send: Any
    oc_send: Any
    att_sem: Any
    do_sem: Any
    do_f_sem: Any
    do_c_sem: Any
    dob_send: Any
    dob_recv: Any
    gkv_send: Any
    gq_send: Any
    gc_send: Any
    g_sem: Any
    c_send_sem: Any
    c_recv_sem: Any
    part_send_sem: Any
    part_recv_sem: Any
    st_rows_send: Any
    st_rows_recv: Any
    st_core_send: Any
    st_core_recv: Any
    st_z_send: Any
    st_z_recv: Any
    st_last_send: Any
    st_last_recv: Any
    out_sem: Any


BF16, F32 = jnp.bfloat16, jnp.float32

SCRATCH = (
    ((768, 768), BF16),
    ((768, 768), BF16),
    ((768, 768), BF16),
    ((768, 768), BF16),
    ((768, 3072), BF16),
    ((3072, 768), BF16),
    ((2, 256, 768), BF16),
    ((2, 256, 768), BF16),
    ((2, 2, 256, 768), BF16),
    ((256, 768), BF16),
    ((1024, 768), BF16),
    ((12, 192, 256), BF16),
    ((8, 192, 256), BF16),
    ((8, 192, 256), BF16),
    ((2048, 128), BF16),
    ((2048, 128), BF16),
    ((1024, 384), BF16),
    ((1024, 384), BF16),
    ((384, 512), BF16),
    ((2048, 1024), F32),
    ((8, 5, 128, 128), F32),
    ((2, 64, 1024), F32),
    ((1, 64, 1024), F32),
    ((3, 64, 1024), F32),
    ((2, 1, 1024), F32),
    ((1, 1, 1024), F32),
    ((3, 1, 1024), F32),
    ((3, 1, 1024), F32),
    ((8, 64, 256), BF16),
    ((4, 64, 256), BF16),
    ((6, 64, 256), BF16),
    ((12, 64, 256), BF16),
    ((12, 64, 256), BF16),
    ((256, 3072), BF16),
    ((256, 768), BF16),
    ((256, 768), BF16),
    ((768, 48), BF16),
    ((768, 48), BF16),
    ((768, 48), F32),
    ((768, 48), F32),
    ((8, 768), F32),
    ((2, 256, 768), F32),
    ((8, 64, 256), BF16),
    ((4, 64, 256), BF16),
    ((2, 6, 64, 256), BF16),
    ((4, 128, 256), BF16),
    ((4, 128, 256), BF16),
    ((3, 256, 768), BF16),
    ((24, 256), F32),
    ((768,), F32),
    ((768,), F32),
    ((4, 192), F32),
    ((4, 12), F32),
    ((4, 12), F32),
    ((4, 192), F32),
    ((48,), F32),
    ((768,), F32),
    ((None, 24, 256), F32),
    ((3, 24, 256), F32),
    ((4, 24, 128), F32),
)
SEMAPHORES = (
    (8,),
    (8,),
    (12,),
    (),
    (),
    (),
    (),
    (3,),
    (3,),
    (),
    (),
    (8,),
    (4,),
    (),
    (12,),
    (),
    (),
    (),
    (),
    (8,),
    (8,),
    (4,),
    (),
    (),
    (),
    (3,),
    (3,),
    (3,),
    (3,),
    (),
    (),
    (3,),
    (3,),
    (),
    (),
    (4,),
)


def layer_kernel(rows_size, *refs):
    f32 = jnp.float32
    bf16 = jnp.bfloat16
    highest_p = lax.Precision.HIGHEST
    r = Refs(*refs)
    row_place = lax.axis_index("rows")
    place = lax.axis_index("seq")
    chip = place // 2
    core = lax.rem(place, 2)
    half = chip // 2
    parity = lax.rem(chip, 2)
    inner_place = lax.rem(place, 4)
    sibling = (row_place, chip * 2 + 1 - core)
    partner = (row_place, (half * 2 + 1 - parity) * 2 + core)

    x_raw = r.out_stage.at[0]
    ct_raw = r.out_stage.at[1]
    do_send_a = r.att_recv_a
    do_send_b = r.att_recv_b
    g_recv = r.qkv_send
    hidden = r.wide.at[pl.ds(768, LANES), pl.ds(0, 768)]
    dq_acc = [r.wide.at[pl.ds(512 + 64 * tile, 64)] for tile in range(2)]
    dkv_own = r.wide.at[pl.ds(1024, 1024), pl.ds(0, 128)]
    part_own = r.wide.at[pl.ds(0, LANES), pl.ds(0, 768)]
    part_far = r.wide.at[pl.ds(LANES, LANES), pl.ds(0, 768)]
    part_send = [r.act.at[:, pl.ds(768 * number, 768)] for number in range(3)]
    turned_z = [
        [r.normed_b.at[:, pl.ds(256 * tile + 128 * number, 128)] for number in range(2)]
        for tile in range(2)
    ]

    def remote(src, dst, send_sem, recv_sem, device):
        return pltpu.make_async_remote_copy(
            src_ref=src,
            dst_ref=dst,
            send_sem=send_sem,
            recv_sem=recv_sem,
            device_id=device,
            device_id_type=MESH,
        )

    def arrived(ref, sem):
        pltpu.make_async_copy(ref, ref, sem).wait()

    loads = [
        pltpu.make_async_copy(src, dst, r.load_sem.at[index])
        for index, (src, dst) in enumerate(
            (
                (r.x_hbm, x_raw),
                (r.w_query_hbm, r.w_query),
                (r.w_key_hbm, r.w_key),
                (r.w_value_hbm, r.w_value),
                (r.ct_hbm, ct_raw),
                (r.w_out_hbm, r.w_out),
                (r.w_in_hbm, r.w_in),
                (r.w_ffout_hbm, r.w_ffout),
            )
        )
    ]
    small_loads = [
        pltpu.make_async_copy(src, dst, r.small_sem.at[index])
        for index, (src, dst) in enumerate(
            (
                (r.gain_attn_hbm, r.gain_attn),
                (r.gain_ffn_hbm, r.gain_ffn),
                (r.down_left_hbm, r.down_left),
                (r.down_right_hbm, r.down_right),
                (r.up_left_hbm, r.up_left),
                (r.up_right_hbm, r.up_right),
                (r.down_bias_hbm, r.down_bias),
                (r.up_bias_hbm, r.up_bias),
            )
        )
    ]
    loads[0].start()
    small_loads[0].start()
    barrier = pltpu.get_barrier_semaphore()
    for offset in range(1, 8):
        pl.semaphore_signal(
            barrier,
            inc=1,
            device_id=(row_place, lax.rem(place + offset, 8)),
            device_id_type=MESH,
        )
    for offset in range(1, rows_size):
        pl.semaphore_signal(
            barrier,
            inc=1,
            device_id=(lax.rem(row_place + offset, rows_size), place),
            device_id_type=MESH,
        )

    for load in loads[1:4]:
        load.start()
    for load in small_loads[1:]:
        load.start()

    first_single = r.doc_lengths[0, 1] == 0
    loads[0].wait()
    small_loads[0].wait()
    gain_attn = r.gain_attn[...].reshape(1, 768)

    def normalized(row):
        values = r.x_rows[row].astype(f32)
        return (values * inverse_rms(values) * gain_attn).astype(bf16)

    r.x_rows[1] = jnp.where(first_single, x_raw[1], x_raw[0])
    my_block = pl.ds(pl.multiple_of(inner_place * LANES, LANES), LANES)
    r.normed_b[my_block, :] = normalized(1)
    pl.semaphore_wait(barrier, 7 + rows_size - 1)

    far_block = pl.ds(
        pl.multiple_of(((1 - parity) * 2 + core) * LANES, LANES), LANES
    )
    far_other = pl.ds(
        pl.multiple_of(((1 - parity) * 2 + 1 - core) * LANES, LANES), LANES
    )
    near_other = pl.ds(pl.multiple_of((parity * 2 + 1 - core) * LANES, LANES), LANES)
    to_partner = remote(
        r.normed_b.at[my_block],
        r.normed_b.at[my_block],
        r.normed_send.at[0],
        r.normed_recv.at[0],
        partner,
    )
    to_sibling = remote(
        r.normed_b.at[my_block],
        r.normed_b.at[my_block],
        r.normed_send.at[1],
        r.normed_recv.at[1],
        sibling,
    )
    onward = remote(
        r.normed_b.at[far_block],
        r.normed_b.at[far_block],
        r.normed_send.at[2],
        r.normed_recv.at[2],
        sibling,
    )
    to_partner.start()
    to_sibling.start()
    for load in loads[4:]:
        load.start()
    r.x_rows[0] = jnp.where(first_single, x_raw[0], x_raw[1])
    r.normed[...] = normalized(0)
    for load in loads[1:4]:
        load.wait()

    for part, weight in enumerate((r.w_query, r.w_key, r.w_value)):
        turned = dot_nn(r.normed[...], weight[...]).astype(bf16).T
        for head in range(12):
            r.qkv_send[head, part * 64 : (part + 1) * 64, :] = turned[head * 64 : (head + 1) * 64]

    far_half = 2 * (1 - half)
    chips = (far_half + parity, far_half + 1 - parity, 2 * half + 1 - parity, chip)

    def exchange(
        source, full, full_sem, split, split_place, split_sem, send_sem, order, start, kinds=range(4)
    ):
        for inside in order:
            for kind in kinds:
                to_chip = chips[kind]
                head = 3 * to_chip + inside
                if inside < 2:
                    dst, sem, to_core = full.at[place], full_sem, inside
                else:
                    dst, sem, to_core = split.at[split_place], split_sem, half

                def go(dst=dst, sem=sem, head=head, device=(row_place, to_chip * 2 + to_core)):
                    copy = remote(source.at[head], dst, send_sem.at[head], sem, device)
                    if start:
                        copy.start()
                    else:
                        copy.wait_send()

                if kind < 3:
                    go()
                    continue
                pl.when(core != to_core)(go)
                if start:

                    @pl.when(core == to_core)
                    def _(dst=dst, sem=sem, head=head):
                        pltpu.make_async_copy(source.at[head], dst, sem).start()

    def exchange_qkv(start, kinds=range(4)):
        exchange(
            r.qkv_send,
            r.slot_f,
            r.slot_f_sem,
            r.slot_c,
            place,
            r.slot_c_sem,
            r.qkv_sem,
            (2, 0, 1),
            start,
            kinds,
        )

    def exchange_do(start):
        exchange(
            do_send_a, r.do_f, r.do_f_sem, r.do_c, inner_place, r.do_c_sem, r.do_sem, (0, 1, 2), start
        )

    middle = (chip == 1) | (chip == 2)

    @pl.when(middle)
    def _():
        exchange_qkv(True, (1,))

    my_heads = pl.ds(pl.multiple_of(core * 384, 128), 384)
    near_chip = pl.ds(pl.multiple_of(parity * 512, 512), 512)
    far_chip = pl.ds(pl.multiple_of((1 - parity) * 512, 512), 512)

    def project_b(lines):
        r.keys_b[lines, :] = dot_nn(r.normed_b[lines, :], r.w_key[:, my_heads]).astype(bf16)
        r.values_b[lines, :] = dot_nn(r.normed_b[lines, :], r.w_value[:, my_heads]).astype(bf16)

    arrived(r.normed_b.at[near_other], r.normed_recv.at[1])
    r.queries_b[...] = (
        dot_nn(r.normed_b[near_chip, :], r.w_query[:, my_heads]).astype(bf16).T
    )
    project_b(near_chip)
    for load in small_loads[1:]:
        load.wait()
    gain_ffn = r.gain_ffn[...].reshape(1, 768)
    down_bias = r.down_bias[...].reshape(1, 48)
    up_bias = r.up_bias[...].reshape(1, 768)

    def make_bias(slot, _):
        head = jnp.where(
            slot == 0, 3 * chip + core, jnp.where(slot == 1, 3 * chip + 2, 6 * core + slot - 2)
        )
        offset = 256 - lax.broadcasted_iota(jnp.int32, (8, 512), 1)
        bucket = bucket_of(offset)
        line = jnp.zeros((8, 512), f32)
        for number in range(32):
            line = jnp.where(bucket == number, r.rel_table[head, number], line)
        spread = pltpu.roll(
            jnp.broadcast_to(line[:1], (128, 512)), 0, 1, stride=1, stride_axis=0
        )
        r.bias[slot, 0] = jnp.full((128, 128), r.rel_table[head, 15], f32)
        r.bias[slot, 1] = spread[:, 384:512]
        r.bias[slot, 2] = spread[:, 256:384]
        r.bias[slot, 3] = spread[:, 128:256]
        r.bias[slot, 4] = jnp.full((128, 128), r.rel_table[head, 31], f32)
        return 0

    lax.fori_loop(0, 8, make_bias, 0)

    zero64 = jnp.zeros((64, 1024), bf16)
    zero512 = jnp.zeros((64, 512), bf16)

    def biased(scores, first_key, lane_of):
        lines = []
        for upper in range(scores.shape[0] // 128):
            pieces = []
            for lane in range(8):
                slot, query = lane_of(lane)
                distance = first_key + upper - query
                if isinstance(distance, int):
                    distance = max(-2, min(2, distance)) + 2
                else:
                    distance = jnp.clip(distance, -2, 2) + 2
                pieces.append(
                    scores[upper * 128 : (upper + 1) * 128, lane * 128 : (lane + 1) * 128]
                    + r.bias[slot, distance]
                )
            lines.append(jnp.concatenate(pieces, axis=1))
        return jnp.concatenate(lines, axis=0)

    def attend_part(blocks, natural, spread_q, first_key, lane_of, weighted):
        peak = jnp.full((8, 1024), -1e30, f32)
        for block in range(blocks):
            lines = slice(block * 256, (block + 1) * 256)
            scores = biased(dot_nn(natural(block), spread_q), first_key + 2 * block, lane_of)
            r.wide[lines, :] = scores
            peak = jnp.maximum(peak, jnp.max(scores.reshape(32, 8, 1024), axis=0))
        peak = jnp.max(peak, axis=0, keepdims=True)
        total = jnp.zeros((64, 1024), f32)
        mass_sum = jnp.zeros((8, 1024), f32)
        for block in range(blocks):
            lines = slice(block * 256, (block + 1) * 256)
            weights = jnp.exp(r.wide[lines, :] - peak)
            mass_sum = mass_sum + jnp.sum(weights.reshape(32, 8, 1024), axis=0)
            total = total + weighted(block, weights.astype(bf16))
        return peak, jnp.sum(mass_sum, axis=0, keepdims=True), total

    def attend(blocks, natural, spread_q, lane_of, weighted, att, mass):
        peak, mass_sum, total = attend_part(blocks, natural, spread_q, 0, lane_of, weighted)
        total = total / mass_sum
        att[...] = total
        mass[...] = peak + jnp.log(mass_sum)
        return total

    def joined(slot, first, low, high):
        return jnp.concatenate([slot[first + u, low:high, :] for u in range(4)], axis=1)

    def lanes_b(pair):
        return lambda lane: (2 + 2 * pair + lane // 4, 4 * parity + lane % 4)

    def lanes_f(tile):
        return lambda lane: (0, 8 * tile + lane)

    def lanes_c(lane):
        return 1, 8 * core + lane

    def pair_lanes(pair):
        return pl.ds(pl.multiple_of(pair * 128, 128), 128)

    def spread_pair(first, second):
        return jnp.concatenate(
            [
                jnp.concatenate([first, zero512], axis=1),
                jnp.concatenate([zero512, second], axis=1),
            ],
            axis=0,
        )

    def pair_queries(pair):
        lines = pl.ds(pl.multiple_of(pair * 128, 128), 128)
        both = r.queries_b[lines, :]
        return spread_pair(both[:64], both[64:])

    def part_b(pair, side):
        lanes = pair_lanes(pair)

        def lines(block):
            return pl.ds(pl.multiple_of(side * 512 + block * 256, 256), 256)

        def weighted(block, weights):
            values = r.values_b[lines(block), lanes].T
            return jnp.concatenate(
                [
                    dot_nn(values[:64], weights[:, :512]),
                    dot_nn(values[64:], weights[:, 512:]),
                ],
                axis=1,
            )

        return attend_part(
            2,
            lambda block: r.keys_b[lines(block), lanes],
            pair_queries(pair),
            4 * side,
            lanes_b(pair),
            weighted,
        )

    def near_b(pair):
        r.mass_b[pair], r.sum_b[pair], r.att_b[pair] = part_b(pair, parity)

    def forward_b(pair):
        peak, mass_sum, total = part_b(pair, 1 - parity)
        near_peak = r.mass_b[pair]
        top = jnp.maximum(peak, near_peak)
        scale, near_scale = jnp.exp(peak - top), jnp.exp(near_peak - top)
        mass_sum = mass_sum * scale + r.sum_b[pair] * near_scale
        r.att_b[pair] = (total * scale + r.att_b[pair] * near_scale) / mass_sum
        r.mass_b[pair] = top + jnp.log(mass_sum)
        for upper in range(2):
            mine = pl.ds(pl.multiple_of(upper * 512 + core * 256, 256), 256)
            theirs = pl.ds(pl.multiple_of(upper * 512 + (1 - core) * 256, 256), 256)
            r.att_recv_b[6 * core + 2 * pair + upper] = r.att_b[pair, :, mine].astype(bf16)
            r.o_send_b[2 * pair + upper] = r.att_b[pair, :, theirs].astype(bf16)

    for pair in range(3):
        near_b(pair)

    arrived(r.normed_b.at[far_block], r.normed_recv.at[0])
    onward.start()

    @pl.when(middle)
    def _():
        exchange_qkv(True, (0, 2, 3))

    @pl.when(jnp.logical_not(middle))
    def _():
        exchange_qkv(True)

    lane48 = lax.broadcasted_iota(jnp.int32, (4, 48), 1)
    term = lax.broadcasted_iota(jnp.int32, (4, 48), 0)
    fold12 = (
        lax.rem(lax.broadcasted_iota(jnp.int32, (12, 48), 1), 12)
        == lax.broadcasted_iota(jnp.int32, (12, 48), 0)
    ).astype(f32)

    def rule_lines(transposed, outer):
        made = jnp.zeros((4, 48), f32)
        for number in range(4):
            for inner in range(4):
                value = (
                    r.phm_rule[number, inner, outer]
                    if transposed
                    else r.phm_rule[number, outer, inner]
                )
                made = jnp.where((term == number) & (lane48 // 12 == inner), value, made)
        return made

    down_rules = [rule_lines(False, outer) for outer in range(4)]
    up_rules = [rule_lines(True, outer) for outer in range(4)]
    down_right_wide = dot_nn(r.down_right[...], fold12, highest_p)
    up_left_wide = dot_nn(r.up_left[...], fold12, highest_p)
    down_left_t = r.down_left[...].T
    up_right_t = r.up_right[...].T
    for outer in range(4):
        r.down_b[outer * 192 : (outer + 1) * 192, :] = dot_nn(
            down_left_t, down_rules[outer] * down_right_wide, highest_p
        ).astype(bf16)
        r.up_b[outer * 192 : (outer + 1) * 192, :] = dot_nn(
            up_right_t, up_rules[outer] * up_left_wide, highest_p
        ).astype(bf16)

    loads[4].wait()
    r.ct_rows[0] = jnp.where(first_single, ct_raw[0], ct_raw[1])
    r.ct_rows[1] = jnp.where(first_single, ct_raw[1], ct_raw[0])

    arrived(r.normed_b.at[far_other], r.normed_recv.at[2])
    project_b(far_chip)

    for pair in range(3):
        forward_b(pair)
    o_to_sibling = remote(
        r.o_send_b, r.att_recv_b.at[pl.ds(6 * core, 6)], r.ob_send, r.ob_recv, sibling
    )
    o_to_sibling.start()

    def dense(row, recv, do_send):
        attended = recv[...].reshape(768, LANES).T
        values = r.x_rows[row].astype(f32) + dot_nn(attended, r.w_out[...])
        hidden[...] = values
        r.normed[...] = (values * inverse_rms(values) * gain_ffn).astype(bf16)
        for chunk in range(3):
            columns = slice(chunk * 1024, (chunk + 1) * 1024)
            value, slope = gelu_pair(dot_nn(r.normed[...], r.w_in[:, columns]))
            r.act[:, columns] = value.astype(bf16)
            r.wide[chunk * LANES : (chunk + 1) * LANES, :] = slope
        r.ff_out[...] = dot_nn(r.act[...], r.w_ffout[...]).astype(bf16)
        squeezed_act, squeezed_slope = gelu_pair(
            dot_nn(r.ff_out[...], r.down_b[...]) + down_bias
        )
        squeezed_act = squeezed_act.astype(bf16)
        squeezed_grad = dot_nn(r.ct_rows[row], r.up_b[...]) * squeezed_slope
        squeezed_low = squeezed_grad.astype(bf16)
        r.out_stage[0, row] = (
            hidden[...]
            + r.ff_out[...].astype(f32)
            + dot_nt(squeezed_act, r.up_b[...])
            + up_bias
        ).astype(bf16)
        pltpu.make_async_copy(
            r.out_stage.at[0, row], r.out_hbm.at[row], r.out_sem.at[row]
        ).start()
        r.ff_grad[...] = (
            r.ct_rows[row].astype(f32) + dot_nt(squeezed_low, r.down_b[...])
        ).astype(bf16)
        for chunk in range(3):
            columns = slice(chunk * 1024, (chunk + 1) * 1024)
            r.act[:, columns] = (
                dot_nt(r.ff_grad[...], r.w_ffout[columns, :])
                * r.wide[chunk * LANES : (chunk + 1) * LANES, :]
            ).astype(bf16)
        normed_grad = dot_nt(r.act[...], r.w_in[...])
        values = r.ct_rows[row].astype(f32) + norm_back(hidden[...], gain_ffn, normed_grad)
        r.hidden_grad[row] = values
        turned = dot_nt(values.astype(bf16), r.w_out[...]).astype(bf16).T
        do_send[...] = turned.reshape(12, 64, LANES)
        return squeezed_act, squeezed_low, squeezed_grad

    def adapter_sums(row, squeezed_act, squeezed_low, squeezed_grad, first):
        up_part = dot_nn(r.ct_rows[row].T, squeezed_act)
        down_part = dot_nn(r.ff_out[...].T, squeezed_low)
        down_sum = jnp.sum(squeezed_grad, axis=0, keepdims=True)
        up_sum = jnp.sum(r.ct_rows[row].astype(f32), axis=0, keepdims=True)
        if first:
            r.up_grad[...] = up_part
            r.down_grad[...] = down_part
            r.bias_grad[0:1, 0:48] = down_sum
            r.bias_grad[1:2, :] = up_sum
        else:
            r.up_grad[...] += up_part
            r.down_grad[...] += down_part
            r.bias_grad[0:1, 0:48] += down_sum
            r.bias_grad[1:2, :] += up_sum

    for load in loads[5:]:
        load.wait()
    arrived(r.att_recv_b.at[pl.ds(6 * (1 - core), 6)], r.ob_recv)
    adapter_sums(1, *dense(1, r.att_recv_b, do_send_b), True)
    o_to_sibling.wait_send()
    do_to_sibling = remote(
        do_send_b.at[pl.ds(6 * (1 - core), 6)], r.do_b.at[core], r.dob_send, r.dob_recv, sibling
    )
    do_to_sibling.start()
    r.do_b[core] = do_send_b[pl.ds(6 * core, 6)]

    arrived(r.slot_c.at[pl.ds(4 * core, 4)], r.slot_c_sem)
    pass_c = remote(
        r.slot_c.at[pl.ds(4 * core, 4), pl.ds(64, 128)],
        r.slot_c.at[pl.ds(4 * core, 4), pl.ds(64, 128)],
        r.pass_c_send,
        r.pass_c_recv,
        sibling,
    )
    pass_c.start()
    def turn_slot(slot, natural, first, count):
        for u in range(count):
            lines = pl.ds(pl.multiple_of((first + u) * 256, 256), 256)
            natural[lines, :] = slot[first + u, 64:192, :].T

    def send_back(source, first, index, dst, send_sem, sem, start):
        def away():
            copy = remote(source, dst, send_sem, sem, (row_place, index))
            if start:
                copy.start()
            else:
                copy.wait_send()

        pl.when(index != place)(away)
        if start:

            @pl.when(index == place)
            def _():
                pltpu.make_async_copy(source, dst, sem).start()

    def send_o_f(tile, start):
        for u in range(4):
            index = 4 * tile + u
            send_back(
                r.o_send_f.at[index],
                None,
                index,
                r.att_recv_a.at[3 * chip + core],
                r.of_send.at[index],
                r.att_sem,
                start,
            )

    def send_o_c(start):
        for u in range(4):
            send_back(
                r.o_send_c.at[u],
                None,
                4 * core + u,
                r.att_recv_a.at[3 * chip + 2],
                r.oc_send.at[u],
                r.att_sem,
                start,
            )

    def back_block(first, second, spread_q, spread_do, first_key, lane_of, log_mass, delta):
        scores = biased(dot_nn(first, spread_q), first_key, lane_of)
        probs = jnp.exp(scores - log_mass)
        score_grad = probs * (dot_nn(second, spread_do) - delta)
        return probs.astype(bf16), score_grad.astype(bf16)

    def backward_b(pair):
        lanes = pair_lanes(pair)
        grads = [
            jnp.concatenate([r.do_b[0, 2 * pair + upper], r.do_b[1, 2 * pair + upper]], axis=1)
            for upper in range(2)
        ]
        delta = jnp.sum(
            jnp.concatenate(grads, axis=1).astype(f32) * r.att_b[pair], axis=0, keepdims=True
        )
        spread_q = pair_queries(pair)
        spread_do = spread_pair(*grads)
        turned_z[0][0][...] = spread_q.T
        turned_z[0][1][...] = spread_do.T
        dq = jnp.zeros((128, 1024), f32)
        for block in range(2):
            lines = slice(block * 512, (block + 1) * 512)
            keys = r.keys_b[lines, lanes]
            probs, score_grad = back_block(
                keys,
                r.values_b[lines, lanes],
                spread_q,
                spread_do,
                4 * block,
                lanes_b(pair),
                r.mass_b[pair],
                delta,
            )
            dq = dq + dot_nn(keys.T, score_grad)
            r.keys_b[lines, lanes] = dot_nn(score_grad, turned_z[0][0][...]).astype(bf16)
            r.values_b[lines, lanes] = dot_nn(probs, turned_z[0][1][...]).astype(bf16)
        first = pl.ds(pl.multiple_of(pair * 128, 64), 64)
        second = pl.ds(pl.multiple_of(pair * 128 + 64, 64), 64)
        r.queries_b[first, :] = dq[:64, :512].astype(bf16)
        r.queries_b[second, :] = dq[64:, 512:].astype(bf16)

    for copy in (to_partner, to_sibling, onward):
        copy.wait_send()
    arrived(r.do_b.at[1 - core], r.dob_recv)
    arrived(r.slot_c.at[pl.ds(4 * (1 - core), 4), pl.ds(64, 128)], r.pass_c_recv)
    turn_slot(r.slot_c, r.natural_c, 0, 8)
    total = attend(
        8,
        lambda block: r.natural_c[block * 256 : (block + 1) * 256, :],
        jnp.concatenate([joined(r.slot_c, 4 * core, 0, 64), zero64], axis=0),
        lanes_c,
        lambda block, weights: dot_nn(r.slot_c[block, 128:192, :], weights),
        r.att_c.at[0],
        r.mass_c.at[0],
    )
    for u in range(4):
        r.o_send_c[u] = total[:, u * 256 : (u + 1) * 256].astype(bf16)
    send_o_c(True)

    arrived(r.slot_f, r.slot_f_sem)
    turn_slot(r.slot_f, r.natural_f, 0, 8)

    def forward_f(tile):
        total = attend(
            8,
            lambda block: r.natural_f[block * 256 : (block + 1) * 256, :],
            jnp.concatenate([joined(r.slot_f, 4 * tile, 0, 64), zero64], axis=0),
            lanes_f(tile),
            lambda block, weights: dot_nn(r.slot_f[block, 128:192, :], weights),
            r.att_f.at[tile],
            r.mass_f.at[tile],
        )
        for u in range(4):
            r.o_send_f[4 * tile + u] = total[:, u * 256 : (u + 1) * 256].astype(bf16)
        send_o_f(tile, True)

    for tile in (1 - half, half):
        forward_f(tile)

    backward_b(0)

    arrived(r.att_recv_a, r.att_sem)
    kept = dense(0, r.att_recv_a, do_send_a)
    exchange_qkv(False)
    exchange_do(True)
    adapter_sums(0, *kept, False)

    backward_b(1)
    backward_b(2)

    def project_back(lines):
        return dot_nt(r.keys_b[lines, :], r.w_key[:, my_heads]) + dot_nt(
            r.values_b[lines, :], r.w_value[:, my_heads]
        )

    my_half = pl.ds(pl.multiple_of(core * LANES, LANES), LANES)
    their_half = pl.ds(pl.multiple_of((1 - core) * LANES, LANES), LANES)
    part_far[...] = project_back(far_block)
    part_send[0][...] = project_back(far_other).astype(bf16)
    far_copy = remote(
        part_send[0], r.part_recv.at[0], r.part_send_sem.at[0], r.part_recv_sem.at[0], sibling
    )
    far_copy.start()
    arrived(r.part_recv.at[0], r.part_recv_sem.at[0])
    part_send[2][...] = (part_far[...] + r.part_recv[0].astype(f32)).astype(bf16)
    partner_copy = remote(
        part_send[2], r.part_recv.at[2], r.part_send_sem.at[2], r.part_recv_sem.at[2], partner
    )
    partner_copy.start()

    def set_tile(slot_index, queries, grads):
        spread_q = jnp.concatenate([queries, zero64], axis=0)
        spread_do = jnp.concatenate([zero64, grads], axis=0)
        turned_z[slot_index][0][...] = spread_q.T
        turned_z[slot_index][1][...] = spread_do.T
        return spread_q, spread_do

    def merged(score_grad, probs, slot_index):
        queries, grads = turned_z[slot_index]
        return dot_nn(score_grad, queries[...]) + dot_nn(probs, grads[...])

    def key_lines(block):
        return pl.ds(pl.multiple_of(block * 512, 512), 512)

    def keys_t(slot, block):
        return jnp.concatenate([slot[2 * block + u, 64:128, :] for u in range(2)], axis=1)

    arrived(r.do_f, r.do_f_sem)
    deltas = []
    spreads = []
    for tile in range(2):
        grads = joined(r.do_f, 4 * tile, 0, 64)
        spreads.append(set_tile(tile, joined(r.slot_f, 4 * tile, 0, 64), grads))
        deltas.append(jnp.sum(grads.astype(f32) * r.att_f[tile], axis=0, keepdims=True))
        dq_acc[tile][...] = jnp.zeros((64, 1024), f32)

    def send_g_f(index, start):
        send_back(
            r.slot_f.at[index, pl.ds(64, 128)],
            None,
            index,
            g_recv.at[3 * chip + core, pl.ds(64, 128)],
            r.gkv_send.at[index],
            r.g_sem,
            start,
        )

    def send_dq_f(index, start):
        send_back(
            r.slot_f.at[index, pl.ds(0, 64)],
            None,
            index,
            g_recv.at[3 * chip + core, pl.ds(0, 64)],
            r.gq_send.at[index],
            r.g_sem,
            start,
        )

    def whole_block(block):
        natural = r.natural_f[key_lines(block), :]
        turned_keys = keys_t(r.slot_f, block)
        made = jnp.zeros((512, 128), f32)
        for tile in range(2):
            probs, score_grad = back_block(
                natural,
                natural,
                *spreads[tile],
                4 * block,
                lanes_f(tile),
                r.mass_f[tile],
                deltas[tile],
            )
            dq_acc[tile][...] += dot_nn(turned_keys, score_grad)
            made = made + merged(score_grad, probs, tile)
        turned = made.astype(bf16).T
        for u in range(2):
            r.slot_f[2 * block + u, 64:192, :] = turned[:, u * 256 : (u + 1) * 256]
            send_g_f(2 * block + u, True)

    for step in range(4):
        whole_block(far_half + step if step < 2 else 2 * half + step - 2)
    for step in range(8):
        index = 4 * (1 - half) + step if step < 4 else 4 * half + step - 4
        r.slot_f[index, 0:64, :] = r.wide[
            pl.ds(pl.multiple_of(512 + 64 * (1 - half if step < 4 else half), 64), 64),
            (step % 4) * 256 : (step % 4 + 1) * 256,
        ].astype(bf16)
        send_dq_f(index, True)

    arrived(r.do_c, r.do_c_sem)
    grads_c = joined(r.do_c, 0, 0, 64)
    spread_qc, spread_doc = set_tile(0, joined(r.slot_c, 4 * core, 0, 64), grads_c)
    delta_c = jnp.sum(grads_c.astype(f32) * r.att_c[0], axis=0, keepdims=True)
    dq_acc[0][...] = jnp.zeros((64, 1024), f32)

    def split_block(block):
        natural = r.natural_c[key_lines(block), :]
        probs, score_grad = back_block(
            natural, natural, spread_qc, spread_doc, 4 * block, lanes_c, r.mass_c[0], delta_c
        )
        dq_acc[0][...] += dot_nn(keys_t(r.slot_c, block), score_grad)
        return merged(score_grad, probs, 0)

    def split_theirs(step):
        turned = split_block(2 * (1 - core) + step).astype(bf16).T
        for u in range(2):
            r.c_send[2 * step + u] = turned[:, u * 256 : (u + 1) * 256]

    def split_mine(step):
        dkv_own[key_lines(step), :] = split_block(2 * core + step)

    for step in range(2):
        split_theirs(step)
    c_copy = remote(r.c_send, r.c_recv, r.c_send_sem, r.c_recv_sem, sibling)
    c_copy.start()
    for step in range(2):
        split_mine(step)

    arrived(r.c_recv, r.c_recv_sem)

    def send_g_c(start):
        for u in range(4):
            send_back(
                r.slot_c.at[4 * core + u],
                None,
                4 * core + u,
                g_recv.at[3 * chip + 2],
                r.gc_send.at[u],
                r.g_sem,
                start,
            )

    pass_c.wait_send()
    for u in range(4):
        r.slot_c[4 * core + u, 0:64, :] = dq_acc[0][:, u * 256 : (u + 1) * 256].astype(bf16)
        r.slot_c[4 * core + u, 64:192, :] = (
            dkv_own[u * 256 : (u + 1) * 256, :].T + r.c_recv[u].astype(f32)
        ).astype(bf16)
    send_g_c(True)

    column48 = lax.broadcasted_iota(jnp.int32, (48, 16), 0) // 12
    lane16 = lax.broadcasted_iota(jnp.int32, (48, 16), 1)

    def kron_back(grad, left, right_wide, rules, transposed):
        left_grad = jnp.zeros((4, 192), f32)
        right_grad = jnp.zeros((4, 48), f32)
        rule_grad = jnp.zeros((4, 16), f32)
        for outer in range(4):
            block = grad[outer * 192 : (outer + 1) * 192, :]
            left_grad = left_grad + dot_nt(rules[outer] * right_wide, block, highest_p)
            contracted = dot_nn(left, block, highest_p)
            right_grad = right_grad + contracted * rules[outer]
            target = column48 * 4 + outer if transposed else outer * 4 + column48
            rule_grad = rule_grad + dot_nn(
                contracted * right_wide, (target == lane16).astype(f32), highest_p
            )
        return left_grad, dot_nt(right_grad, fold12, highest_p), rule_grad

    dl_grad, dr_grad, rule_down = kron_back(
        r.down_grad, r.down_left[...], down_right_wide, down_rules, False
    )
    ur_grad, ul_grad, rule_up = kron_back(
        r.up_grad, r.up_right[...], up_left_wide, up_rules, True
    )
    r.stats[...] = jnp.zeros_like(r.stats)
    r.stats[0:4, 0:192] = dl_grad
    r.stats[4:8, 0:192] = ur_grad
    r.stats[8:12, 0:12] = dr_grad
    r.stats[8:12, 128:140] = ul_grad
    r.stats[12:16, 0:16] = rule_down + rule_up
    r.stats[16:17, 0:48] = r.bias_grad[0:1, 0:48]
    for third in range(3):
        r.stats[17 + third : 18 + third, :] = r.bias_grad[1:2, third * 256 : (third + 1) * 256]

    def rows_copy(offset):
        return remote(
            r.stats,
            r.stats_rows.at[row_place],
            r.st_rows_send.at[offset - 1],
            r.st_rows_recv.at[offset - 1],
            (lax.rem(row_place + offset, rows_size), place),
        )

    for offset in range(1, rows_size):
        rows_copy(offset).start()
    r.stats_rows[row_place] = r.stats[...]

    part_send[1][...] = (
        project_back(near_other)
        + dot_nt(r.queries_b[:, their_half].T, r.w_query[:, my_heads])
    ).astype(bf16)
    near_copy = remote(
        part_send[1], r.part_recv.at[1], r.part_send_sem.at[1], r.part_recv_sem.at[1], sibling
    )
    near_copy.start()

    def finish_row(row, normed_grad):
        r.out_stage[1, row] = (
            r.hidden_grad[row] + norm_back(r.x_rows[row].astype(f32), gain_attn, normed_grad)
        ).astype(bf16)
        pltpu.make_async_copy(
            r.out_stage.at[1, row], r.grad_hbm.at[row], r.out_sem.at[2 + row]
        ).start()

    part_own[...] = project_back(my_block) + dot_nt(
        r.queries_b[:, my_half].T, r.w_query[:, my_heads]
    )

    my_lanes = pl.ds(pl.multiple_of(core * 128, 128), 128)
    other_lanes = pl.ds(pl.multiple_of((1 - core) * 128, 128), 128)
    for offset in range(1, rows_size):
        rows_copy(offset).wait()
    summed = r.stats_rows[0]
    for number in range(1, rows_size):
        summed = summed + r.stats_rows[number]
    r.stats_core[0] = summed
    core_copy = remote(
        r.stats_core.at[0, :, other_lanes],
        r.stats_core.at[1, :, other_lanes],
        r.st_core_send,
        r.st_core_recv,
        sibling,
    )
    core_copy.start()

    core_copy.wait_send()
    arrived(r.stats_core.at[1, :, my_lanes], r.st_core_recv)
    r.stats_z[chip] = r.stats_core[0, :, my_lanes] + r.stats_core[1, :, my_lanes]

    def z_copy(offset):
        return remote(
            r.stats_z.at[chip],
            r.stats_z.at[chip],
            r.st_z_send.at[offset - 1],
            r.st_z_recv.at[offset - 1],
            (row_place, lax.rem(chip + offset, 4) * 2 + core),
        )

    for offset in range(1, 4):
        z_copy(offset).start()

    arrived(r.part_recv.at[1], r.part_recv_sem.at[1])
    arrived(r.part_recv.at[2], r.part_recv_sem.at[2])
    finish_row(
        1, part_own[...] + r.part_recv[1].astype(f32) + r.part_recv[2].astype(f32)
    )

    for offset in range(1, 4):
        z_copy(offset).wait()
    r.stats_core[2, :, my_lanes] = (r.stats_z[0] + r.stats_z[1]) + (r.stats_z[2] + r.stats_z[3])
    last_copy = remote(
        r.stats_core.at[2, :, my_lanes],
        r.stats_core.at[2, :, my_lanes],
        r.st_last_send,
        r.st_last_recv,
        sibling,
    )
    last_copy.start()

    for copy in (do_to_sibling, c_copy, far_copy, near_copy, partner_copy):
        copy.wait_send()
    exchange_do(False)
    for tile in range(2):
        send_o_f(tile, False)
    send_o_c(False)
    for row in range(2):
        pltpu.make_async_copy(
            r.out_stage.at[0, row], r.out_hbm.at[row], r.out_sem.at[row]
        ).wait()
    arrived(g_recv, r.g_sem)
    turned_grad = jnp.zeros((768, LANES), f32)
    for part, weight in enumerate((r.w_query, r.w_key, r.w_value)):
        turned_grad = turned_grad + dot_nn(
            weight[...], g_recv[:, part * 64 : (part + 1) * 64, :].reshape(768, LANES)
        )
    finish_row(0, turned_grad.T)
    last_copy.wait_send()
    arrived(r.stats_core.at[2, :, other_lanes], r.st_last_recv)
    r.stats_out[...] = r.stats_core[2]

    send_g_c(False)
    for index in range(8):
        send_g_f(index, False)
        send_dq_f(index, False)
    for row in range(2):
        pltpu.make_async_copy(
            r.out_stage.at[1, row], r.grad_hbm.at[row], r.out_sem.at[2 + row]
        ).wait()


def finish_kernel(
    doc_lengths,
    stats_from,
    out_from,
    grad_from,
    out_to,
    grad_to,
    rule_out,
    dl_out,
    dr_out,
    ul_out,
    ur_out,
    db_out,
    ub_out,
    stage,
    stats,
    sem,
    stats_sem,
):
    gets, puts = [], []
    first_single = doc_lengths[0, 1] == 0
    for number, (source, target) in enumerate(((grad_from, grad_to), (out_from, out_to))):
        for row in range(2):
            to_row = jnp.where(first_single, row, 1 - row)
            gets.append(
                pltpu.make_async_copy(
                    source.at[row], stage.at[number, row], sem.at[0, number, row]
                )
            )
            puts.append(
                pltpu.make_async_copy(
                    stage.at[number, row], target.at[to_row], sem.at[1, number, row]
                )
            )
    get_stats = pltpu.make_async_copy(stats_from, stats, stats_sem)
    get_stats.start()
    for get in gets:
        get.start()
    get_stats.wait()
    for outer in range(4):
        rule_out[:, outer, :] = stats[12:16, 4 * outer : 4 * outer + 4]
    dl_out[...] = stats[0:4, 0:192]
    ur_out[...] = stats[4:8, 0:192]
    dr_out[...] = stats[8:12, 0:12]
    ul_out[...] = stats[8:12, 128:140]
    db_out[...] = stats[16:17, 0:48].reshape(48)
    ub_out[...] = jnp.concatenate(
        [stats[17 + third : 18 + third, :] for third in range(3)], axis=1
    ).reshape(768)
    for get, put in zip(gets, puts):
        get.wait()
        put.start()
    for put in puts:
        put.wait()


def layer_on_slice(rows_size, *arrays):
    (
        inputs,
        doc_lengths,
        w_query,
        w_key,
        w_value,
        w_out,
        w_in,
        w_ffout,
        rel_table,
        gain_attn,
        gain_ffn,
        phm_rule,
        down_left,
        down_right,
        up_left,
        up_right,
        down_bias,
        up_bias,
        cotangent,
    ) = arrays
    f32 = jnp.float32
    bf16 = jnp.bfloat16
    shape = jax.ShapeDtypeStruct
    vmem = pl.BlockSpec(memory_space=pltpu.VMEM)
    smem = pl.BlockSpec(memory_space=pltpu.SMEM)
    hbm = pl.BlockSpec(memory_space=pl.ANY)
    dma = pltpu.SemaphoreType.DMA
    results = pl.pallas_call(
        functools.partial(layer_kernel, rows_size),
        out_shape=[
            shape(inputs.shape, bf16),
            shape(inputs.shape, bf16),
            shape((24, 256), f32),
        ],
        in_specs=[smem] * 3 + [hbm] * 16,
        out_specs=[hbm] * 2 + [vmem],
        scratch_shapes=[
            pltpu.VMEM(tuple(rows_size if size is None else size for size in sizes), kind)
            for sizes, kind in SCRATCH
        ]
        + [dma(sizes) for sizes in SEMAPHORES],
        compiler_params=pltpu.CompilerParams(
            collective_id=0, has_side_effects=True, vmem_limit_bytes=56 * 1024 * 1024
        ),
        name="encoder_layer",
    )(
        doc_lengths,
        rel_table.T,
        phm_rule,
        gain_attn,
        gain_ffn,
        down_left,
        down_right,
        up_left,
        up_right,
        down_bias,
        up_bias,
        inputs,
        cotangent,
        w_query,
        w_key,
        w_value,
        w_out,
        w_in,
        w_ffout,
    )
    return pl.pallas_call(
        finish_kernel,
        out_shape=[
            shape(inputs.shape, bf16),
            shape(inputs.shape, bf16),
            shape(phm_rule.shape, f32),
            shape((4, 192), f32),
            shape((4, 12), f32),
            shape((4, 12), f32),
            shape((4, 192), f32),
            shape((48,), f32),
            shape((768,), f32),
        ],
        in_specs=[smem] + [hbm] * 3,
        out_specs=[hbm] * 2 + [vmem] * 7,
        scratch_shapes=[
            pltpu.VMEM((2, 2, LANES, 768), bf16),
            pltpu.VMEM((24, 256), f32),
            dma((2, 2, 2)),
            dma(()),
        ],
        name="finish",
    )(doc_lengths, results[2], results[0], results[1])


def pick(rows_size, seq_size, *arrays):
    inputs, doc_lengths = arrays[:2]
    fits = (
        seq_size == 8
        and inputs.shape == (2, LANES, 768)
        and doc_lengths.shape == (2, 2)
        and arrays[8].shape == (32, 12)
        and arrays[6].shape == (768, 3072)
    )
    return layer_on_slice(rows_size, *arrays) if fits else local(*arrays)


def solution(mesh):
    return jax.shard_map(
        functools.partial(pick, mesh.shape["rows"], mesh.shape["seq"]),
        mesh=mesh,
        in_specs=(
            P("rows", "seq", None),
            P("rows", None),
            P(),
            P(),
            P(),
            P(),
            P(),
            P(),
            P(),
            P(),
            P(),
            P(),
            P(),
            P(),
            P(),
            P(),
            P(),
            P(),
            P("rows", "seq", None),
        ),
        out_specs=(
            P("rows", "seq", None),
            P("rows", "seq", None),
            P(),
            P(),
            P(),
            P(),
            P(),
            P(),
            P(),
        ),
        check_vma=False,
    )
```

```python
import functools
import math
from typing import Any, NamedTuple

import jax
import jax.numpy as jnp
from jax import lax
from jax.experimental import pallas as pl
from jax.experimental.pallas import tpu as pltpu
from jax.sharding import PartitionSpec as P

epsilon = 1e-06
highest = lax.Precision.HIGHEST
bucket_edges = (12, 16, 23, 32, 46, 64, 91)


def smooth_gelu(values):
    return (
        0.5
        * values
        * (1.0 + jnp.tanh(0.7978845608028654 * (values + 0.044715 * values * values * values)))
    )


def rms_norm(values, gain):
    return values * lax.rsqrt(jnp.mean(values * values, axis=-1, keepdims=True) + epsilon) * gain


def bucket_of(offset):
    magnitude = jnp.abs(offset)
    larger = jnp.full(offset.shape, 8, jnp.int32)
    for edge in bucket_edges:
        larger = larger + (magnitude >= edge).astype(jnp.int32)
    inside = jnp.where(magnitude < 8, magnitude, larger)
    return inside + jnp.where(offset > 0, 16, 0).astype(jnp.int32)


def segment_ids(lengths, token_positions):
    doc_ends = jnp.cumsum(lengths, axis=-1, dtype=jnp.int32)
    return jnp.sum(
        (token_positions[..., :, None] >= doc_ends[..., None, :]).astype(jnp.int32),
        axis=-1,
        dtype=jnp.int32,
    )


def kron_sum(rule_part, left_part, right_part):
    blocks = jnp.einsum("iab,ip,iq->apbq", rule_part, left_part, right_part, precision=highest)
    return blocks.reshape(
        rule_part.shape[1] * left_part.shape[1], rule_part.shape[2] * right_part.shape[1]
    )


def pair_bias(query_pos, key_pos, rel_table):
    buckets = bucket_of(key_pos[None, :] - query_pos[:, None])
    onehot = (buckets[:, :, None] == jnp.arange(rel_table.shape[0], dtype=jnp.int32)).astype(
        jnp.bfloat16
    )
    table_high = rel_table.astype(jnp.bfloat16)
    table_rest = (rel_table - table_high.astype(jnp.float32)).astype(jnp.bfloat16)
    high_part = jnp.einsum("qkb,bh->qhk", onehot, table_high, preferred_element_type=jnp.float32)
    rest_part = jnp.einsum("qkb,bh->qhk", onehot, table_rest, preferred_element_type=jnp.float32)
    return high_part + rest_part


def over_blocks(carried, pieces, blockwise):
    total_len = pieces[0].shape[1]
    block_len = math.gcd(total_len, 512)

    def one_step(block_index, inner_state):
        begin_row = block_index * block_len
        sliced = tuple(
            (lax.dynamic_slice_in_dim(member, begin_row, block_len, 1) for member in pieces)
        )
        return blockwise(inner_state, sliced, begin_row)

    return lax.fori_loop(0, total_len // block_len, one_step, carried)


def local(
    inputs,
    doc_lengths,
    w_query,
    w_key,
    w_value,
    w_out,
    w_in,
    w_ffout,
    rel_table,
    gain_attn,
    gain_ffn,
    phm_rule,
    down_left,
    down_right,
    up_left,
    up_right,
    down_bias,
    up_bias,
    cotangent,
):
    row_count, length, model_width = inputs.shape
    head_count = rel_table.shape[1]
    head_dim = model_width // head_count
    seq_place = lax.axis_index("seq")
    token_count = row_count * length
    local_pos = seq_place * length + jnp.arange(length, dtype=jnp.int32)
    local_seg = segment_ids(doc_lengths, local_pos[None, :])
    bf16 = jnp.bfloat16
    f32 = jnp.float32

    def heads_of(matrix, block_len):
        return matrix.reshape(row_count, block_len, head_count, head_dim)

    def norm_attn(values):
        return rms_norm(values, gain_attn)

    def norm_ffn(values):
        return rms_norm(values, gain_ffn)

    source = inputs.astype(f32).reshape(token_count, model_width)
    normed, norm_attn_back = jax.vjp(norm_attn, source)
    normed_b = normed.astype(bf16)
    queries = (
        jnp.dot(normed_b, w_query, preferred_element_type=f32)
        .astype(bf16)
        .reshape(row_count, length, model_width)
    )
    key_rows = (
        jnp.dot(normed_b, w_key, preferred_element_type=f32)
        .astype(bf16)
        .reshape(row_count, length, model_width)
    )
    value_rows = (
        jnp.dot(normed_b, w_value, preferred_element_type=f32)
        .astype(bf16)
        .reshape(row_count, length, model_width)
    )
    queries_h = heads_of(queries, length)
    keys_h = heads_of(key_rows, length)
    values_h = heads_of(value_rows, length)

    def scores_for(query_h, query_pos, query_seg, key_h, key_pos, key_seg):
        scores = jnp.einsum("rqhd,rkhd->rqhk", query_h, key_h, preferred_element_type=f32)
        scores = scores + pair_bias(query_pos, key_pos, rel_table)[None]
        allowed = (query_seg[:, :, None] == key_seg[:, None, :])[:, :, None, :]
        return (scores, allowed)

    def forward_piece(carried, pieces, first_row):
        weighted, running, mass_sum = carried
        key_part, value_part = pieces
        block_len = key_part.shape[1]
        key_pos = first_row + jnp.arange(block_len, dtype=jnp.int32)
        key_seg = segment_ids(doc_lengths, key_pos[None, :])
        scores, allowed = scores_for(
            queries_h, local_pos, local_seg, heads_of(key_part, block_len), key_pos, key_seg
        )
        scores = jnp.where(allowed, scores, -1e30)
        raised = jnp.maximum(running, jnp.max(scores, axis=-1))
        weights = jnp.where(allowed, jnp.exp(scores - raised[..., None]), 0.0)
        rescale = jnp.exp(running - raised)
        mass_sum = mass_sum * rescale + jnp.sum(weights, axis=-1)
        weighted = weighted * rescale[..., None] + jnp.einsum(
            "rqhk,rkhd->rqhd",
            weights.astype(bf16),
            heads_of(value_part, block_len),
            preferred_element_type=f32,
        )
        return (weighted, raised, mass_sum)

    start_state = (
        jnp.zeros((row_count, length, head_count, head_dim), f32),
        jnp.full((row_count, length, head_count), -1e30, f32),
        jnp.zeros((row_count, length, head_count), f32),
    )
    weighted, running, mass_sum = over_blocks(
        start_state,
        (
            lax.all_gather(key_rows, "seq", axis=1, tiled=True),
            lax.all_gather(value_rows, "seq", axis=1, tiled=True),
        ),
        forward_piece,
    )
    attended = weighted / mass_sum[..., None]
    log_mass = running + jnp.log(mass_sum)
    attended_b = attended.astype(bf16).reshape(token_count, model_width)
    hidden = source + jnp.dot(attended_b, w_out, preferred_element_type=f32)
    normed_ffn, norm_ffn_back = jax.vjp(norm_ffn, hidden)
    inner = jnp.dot(normed_ffn.astype(bf16), w_in, preferred_element_type=f32)
    activated, gelu_back = jax.vjp(smooth_gelu, inner)
    activated_b = activated.astype(bf16)
    ff_out = jnp.dot(activated_b, w_ffout, preferred_element_type=f32).astype(bf16)
    down_full, down_back = jax.vjp(kron_sum, phm_rule, down_left, down_right)
    up_full, up_back = jax.vjp(kron_sum, phm_rule, up_left, up_right)
    down_b = down_full.astype(bf16)
    up_b = up_full.astype(bf16)
    squeezed = jnp.dot(ff_out, down_b, preferred_element_type=f32) + down_bias
    squeezed_act, squeeze_back = jax.vjp(smooth_gelu, squeezed)
    squeezed_act_b = squeezed_act.astype(bf16)
    expanded = jnp.dot(squeezed_act_b, up_b, preferred_element_type=f32) + up_bias
    result = hidden + ff_out.astype(f32) + expanded
    output = result.astype(bf16).reshape(row_count, length, model_width)
    upstream = cotangent.astype(f32).reshape(token_count, model_width)
    up_bias_grad = jnp.sum(upstream, axis=0)
    upstream_b = upstream.astype(bf16)
    up_matrix_grad = jnp.einsum("ta,td->ad", squeezed_act_b, upstream_b, preferred_element_type=f32)
    squeezed_grad = squeeze_back(
        jnp.einsum("td,ad->ta", upstream_b, up_b, preferred_element_type=f32)
    )[0]
    down_bias_grad = jnp.sum(squeezed_grad, axis=0)
    squeezed_low = squeezed_grad.astype(bf16)
    down_matrix_grad = jnp.einsum("td,ta->da", ff_out, squeezed_low, preferred_element_type=f32)
    rule_down, down_left_grad, down_right_grad = down_back(down_matrix_grad)
    rule_up, up_left_grad, up_right_grad = up_back(up_matrix_grad)
    summed = lax.psum(
        (
            rule_down + rule_up,
            down_left_grad,
            down_right_grad,
            up_left_grad,
            up_right_grad,
            down_bias_grad,
            up_bias_grad,
        ),
        ("rows", "seq"),
    )
    ff_grad = upstream + jnp.einsum("ta,da->td", squeezed_low, down_b, preferred_element_type=f32)
    ff_grad_b = ff_grad.astype(bf16)
    inner_grad = gelu_back(jnp.einsum("td,fd->tf", ff_grad_b, w_ffout, preferred_element_type=f32))[
        0
    ]
    inner_grad_b = inner_grad.astype(bf16)
    hidden_grad = (
        upstream
        + norm_ffn_back(jnp.einsum("tf,df->td", inner_grad_b, w_in, preferred_element_type=f32))[0]
    )
    hidden_grad_b = hidden_grad.astype(bf16)
    attended_grad = jnp.einsum(
        "te,de->td", hidden_grad_b, w_out, preferred_element_type=f32
    ).astype(bf16)
    attended_grad = attended_grad.reshape(row_count, length, model_width)
    attended_grad_h = heads_of(attended_grad, length)
    row_delta = jnp.sum(attended_grad_h.astype(f32) * attended, axis=-1)

    def gradient_terms(
        query_h,
        query_pos,
        query_seg,
        grad_h,
        mass_part,
        delta_part,
        key_h,
        value_h,
        key_pos,
        key_seg,
    ):
        scores, allowed = scores_for(query_h, query_pos, query_seg, key_h, key_pos, key_seg)
        weights = jnp.exp(jnp.where(allowed, scores - mass_part[..., None], -1e30))
        weights_grad = jnp.einsum("rqhd,rkhd->rqhk", grad_h, value_h, preferred_element_type=f32)
        score_grad = (weights * (weights_grad - delta_part[..., None])).astype(bf16)
        return (weights.astype(bf16), score_grad)

    zero_grad = jnp.zeros((row_count, length, head_count, head_dim), f32)

    def query_side(carried, pieces, first_row):
        key_part, value_part = pieces
        block_len = key_part.shape[1]
        key_pos = first_row + jnp.arange(block_len, dtype=jnp.int32)
        key_seg = segment_ids(doc_lengths, key_pos[None, :])
        key_h = heads_of(key_part, block_len)
        weights_b, score_grad = gradient_terms(
            queries_h,
            local_pos,
            local_seg,
            attended_grad_h,
            log_mass,
            row_delta,
            key_h,
            heads_of(value_part, block_len),
            key_pos,
            key_seg,
        )
        return carried + jnp.einsum(
            "rqhk,rkhd->rqhd", score_grad, key_h, preferred_element_type=f32
        )

    query_grad = over_blocks(
        zero_grad,
        (
            lax.all_gather(key_rows, "seq", axis=1, tiled=True),
            lax.all_gather(value_rows, "seq", axis=1, tiled=True),
        ),
        query_side,
    )
    mass_all, delta_all = (
        lax.all_gather(log_mass, "seq", axis=1, tiled=True),
        lax.all_gather(row_delta, "seq", axis=1, tiled=True),
    )

    def key_side(carried, pieces, first_row):
        key_acc, value_acc = carried
        query_part, grad_part = pieces
        block_len = query_part.shape[1]
        query_pos = first_row + jnp.arange(block_len, dtype=jnp.int32)
        query_seg = segment_ids(doc_lengths, query_pos[None, :])
        mass_part = lax.dynamic_slice_in_dim(mass_all, first_row, block_len, 1)
        delta_part = lax.dynamic_slice_in_dim(delta_all, first_row, block_len, 1)
        query_h = heads_of(query_part, block_len)
        grad_h = heads_of(grad_part, block_len)
        weights_b, score_grad = gradient_terms(
            query_h,
            query_pos,
            query_seg,
            grad_h,
            mass_part,
            delta_part,
            keys_h,
            values_h,
            local_pos,
            local_seg,
        )
        key_acc = key_acc + jnp.einsum(
            "rqhk,rqhd->rkhd", score_grad, query_h, preferred_element_type=f32
        )
        value_acc = value_acc + jnp.einsum(
            "rqhk,rqhd->rkhd", weights_b, grad_h, preferred_element_type=f32
        )
        return (key_acc, value_acc)

    key_grad, value_grad = over_blocks(
        (zero_grad, zero_grad),
        (
            lax.all_gather(queries, "seq", axis=1, tiled=True),
            lax.all_gather(attended_grad, "seq", axis=1, tiled=True),
        ),
        key_side,
    )
    query_grad_b = query_grad.astype(bf16).reshape(token_count, model_width)
    key_grad_b = key_grad.astype(bf16).reshape(token_count, model_width)
    value_grad_b = value_grad.astype(bf16).reshape(token_count, model_width)
    normed_grad = jnp.einsum("te,de->td", query_grad_b, w_query, preferred_element_type=f32)
    normed_grad = normed_grad + jnp.einsum(
        "te,de->td", key_grad_b, w_key, preferred_element_type=f32
    )
    normed_grad = normed_grad + jnp.einsum(
        "te,de->td", value_grad_b, w_value, preferred_element_type=f32
    )
    input_grad = hidden_grad + norm_attn_back(normed_grad)[0]
    input_grad = input_grad.astype(bf16).reshape(row_count, length, model_width)
    return (
        output,
        input_grad,
        summed[0],
        summed[1],
        summed[2],
        summed[3],
        summed[4],
        summed[5],
        summed[6],
    )


MESH = pl.DeviceIdType.MESH
LANES = 256


def dot_nn(left, right, precision=None):
    return lax.dot_general(
        left, right, (((1,), (0,)), ((), ())), precision=precision, preferred_element_type=jnp.float32
    )


def dot_nt(left, right, precision=None):
    return lax.dot_general(
        left, right, (((1,), (1,)), ((), ())), precision=precision, preferred_element_type=jnp.float32
    )


def gelu_pair(values):
    square = values * values
    tanh = jnp.tanh(0.7978845608028654 * values * (1.0 + 0.044715 * square))
    half = 0.5 * (1.0 + tanh)
    slope = half + 0.5 * values * (1.0 - tanh * tanh) * (
        0.7978845608028654 * (1.0 + 3.0 * 0.044715 * square)
    )
    return values * half, slope


def inverse_rms(values):
    return lax.rsqrt(jnp.mean(values * values, axis=-1, keepdims=True) + epsilon)


def norm_back(values, gain, grad):
    inverse = inverse_rms(values)
    scaled = grad * gain
    return inverse * scaled - values * (
        inverse * inverse * inverse * jnp.mean(values * scaled, axis=-1, keepdims=True)
    )


class Refs(NamedTuple):
    doc_lengths: Any
    rel_table: Any
    phm_rule: Any
    gain_attn_hbm: Any
    gain_ffn_hbm: Any
    down_left_hbm: Any
    down_right_hbm: Any
    up_left_hbm: Any
    up_right_hbm: Any
    down_bias_hbm: Any
    up_bias_hbm: Any
    x_hbm: Any
    ct_hbm: Any
    w_query_hbm: Any
    w_key_hbm: Any
    w_value_hbm: Any
    w_out_hbm: Any
    w_in_hbm: Any
    w_ffout_hbm: Any
    out_hbm: Any
    grad_hbm: Any
    stats_out: Any
    w_query: Any
    w_key: Any
    w_value: Any
    w_out: Any
    w_in: Any
    w_ffout: Any
    x_rows: Any
    ct_rows: Any
    out_stage: Any
    normed: Any
    normed_b: Any
    qkv_send: Any
    slot_f: Any
    slot_c: Any
    natural_f: Any
    natural_c: Any
    keys_b: Any
    values_b: Any
    queries_b: Any
    wide: Any
    bias: Any
    att_f: Any
    att_c: Any
    att_b: Any
    mass_f: Any
    mass_c: Any
    mass_b: Any
    sum_b: Any
    o_send_f: Any
    o_send_c: Any
    o_send_b: Any
    att_recv_a: Any
    att_recv_b: Any
    act: Any
    ff_out: Any
    ff_grad: Any
    down_b: Any
    up_b: Any
    down_grad: Any
    up_grad: Any
    bias_grad: Any
    hidden_grad: Any
    do_f: Any
    do_c: Any
    do_b: Any
    c_send: Any
    c_recv: Any
    part_recv: Any
    stats: Any
    gain_attn: Any
    gain_ffn: Any
    down_left: Any
    down_right: Any
    up_left: Any
    up_right: Any
    down_bias: Any
    up_bias: Any
    stats_rows: Any
    stats_core: Any
    stats_z: Any
    load_sem: Any
    small_sem: Any
    qkv_sem: Any
    slot_f_sem: Any
    slot_c_sem: Any
    pass_c_send: Any
    pass_c_recv: Any
    normed_send: Any
    normed_recv: Any
    ob_send: Any
    ob_recv: Any
    of_send: Any
    oc_send: Any
    att_sem: Any
    do_sem: Any
    do_f_sem: Any
    do_c_sem: Any
    dob_send: Any
    dob_recv: Any
    gkv_send: Any
    gq_send: Any
    gc_send: Any
    g_sem: Any
    c_send_sem: Any
    c_recv_sem: Any
    part_send_sem: Any
    part_recv_sem: Any
    st_rows_send: Any
    st_rows_recv: Any
    st_core_send: Any
    st_core_recv: Any
    st_z_send: Any
    st_z_recv: Any
    st_last_send: Any
    st_last_recv: Any
    out_sem: Any
    stats_out_sem: Any


BF16, F32 = jnp.bfloat16, jnp.float32

SCRATCH = (
    ((768, 768), BF16),
    ((768, 768), BF16),
    ((768, 768), BF16),
    ((768, 768), BF16),
    ((768, 3072), BF16),
    ((3072, 768), BF16),
    ((2, 256, 768), BF16),
    ((2, 256, 768), BF16),
    ((2, 2, 256, 768), BF16),
    ((256, 768), BF16),
    ((1024, 768), BF16),
    ((12, 192, 256), BF16),
    ((8, 192, 256), BF16),
    ((8, 192, 256), BF16),
    ((2048, 128), BF16),
    ((2048, 128), BF16),
    ((1024, 384), BF16),
    ((1024, 384), BF16),
    ((384, 512), BF16),
    ((2048, 1024), F32),
    ((8, 5, 128, 128), F32),
    ((2, 64, 1024), F32),
    ((1, 64, 1024), F32),
    ((3, 64, 1024), F32),
    ((2, 1, 1024), F32),
    ((1, 1, 1024), F32),
    ((3, 1, 1024), F32),
    ((3, 1, 1024), F32),
    ((8, 64, 256), BF16),
    ((4, 64, 256), BF16),
    ((6, 64, 256), BF16),
    ((12, 64, 256), BF16),
    ((12, 64, 256), BF16),
    ((256, 3072), BF16),
    ((256, 768), BF16),
    ((256, 768), BF16),
    ((768, 48), BF16),
    ((768, 48), BF16),
    ((768, 48), F32),
    ((768, 48), F32),
    ((8, 768), F32),
    ((2, 256, 768), F32),
    ((8, 64, 256), BF16),
    ((4, 64, 256), BF16),
    ((2, 6, 64, 256), BF16),
    ((4, 128, 256), BF16),
    ((4, 128, 256), BF16),
    ((3, 256, 768), BF16),
    ((24, 256), F32),
    ((768,), F32),
    ((768,), F32),
    ((4, 192), F32),
    ((4, 12), F32),
    ((4, 12), F32),
    ((4, 192), F32),
    ((48,), F32),
    ((768,), F32),
    ((None, 24, 256), F32),
    ((3, 24, 256), F32),
    ((4, 24, 128), F32),
)
SEMAPHORES = (
    (8,),
    (8,),
    (12,),
    (),
    (),
    (),
    (),
    (3,),
    (3,),
    (),
    (),
    (8,),
    (4,),
    (),
    (12,),
    (),
    (),
    (),
    (),
    (8,),
    (8,),
    (4,),
    (),
    (),
    (),
    (3,),
    (3,),
    (3,),
    (3,),
    (),
    (),
    (3,),
    (3,),
    (),
    (),
    (4,),
    (),
)


def layer_kernel(rows_size, *refs):
    f32 = jnp.float32
    bf16 = jnp.bfloat16
    highest_p = lax.Precision.HIGHEST
    r = Refs(*refs)
    row_place = lax.axis_index("rows")
    place = lax.axis_index("seq")
    chip = place // 2
    core = lax.rem(place, 2)
    half = chip // 2
    parity = lax.rem(chip, 2)
    inner_place = lax.rem(place, 4)
    sibling = (row_place, chip * 2 + 1 - core)
    partner = (row_place, (half * 2 + 1 - parity) * 2 + core)

    x_raw = r.out_stage.at[0]
    ct_raw = r.out_stage.at[1]
    do_send_a = r.att_recv_a
    do_send_b = r.att_recv_b
    g_recv = r.qkv_send
    hidden = r.wide.at[pl.ds(768, LANES), pl.ds(0, 768)]
    dq_acc = [r.wide.at[pl.ds(512 + 64 * tile, 64)] for tile in range(2)]
    dkv_own = r.wide.at[pl.ds(1024, 1024), pl.ds(0, 128)]
    part_own = r.wide.at[pl.ds(0, LANES), pl.ds(0, 768)]
    part_far = r.wide.at[pl.ds(LANES, LANES), pl.ds(0, 768)]
    part_send = [r.act.at[:, pl.ds(768 * number, 768)] for number in range(3)]
    turned_z = [
        [r.normed_b.at[:, pl.ds(256 * tile + 128 * number, 128)] for number in range(2)]
        for tile in range(2)
    ]

    def remote(src, dst, send_sem, recv_sem, device):
        return pltpu.make_async_remote_copy(
            src_ref=src,
            dst_ref=dst,
            send_sem=send_sem,
            recv_sem=recv_sem,
            device_id=device,
            device_id_type=MESH,
        )

    def arrived(ref, sem):
        pltpu.make_async_copy(ref, ref, sem).wait()

    loads = [
        pltpu.make_async_copy(src, dst, r.load_sem.at[index])
        for index, (src, dst) in enumerate(
            (
                (r.x_hbm, x_raw),
                (r.w_query_hbm, r.w_query),
                (r.w_key_hbm, r.w_key),
                (r.w_value_hbm, r.w_value),
                (r.ct_hbm, ct_raw),
                (r.w_out_hbm, r.w_out),
                (r.w_in_hbm, r.w_in),
                (r.w_ffout_hbm, r.w_ffout),
            )
        )
    ]
    small_loads = [
        pltpu.make_async_copy(src, dst, r.small_sem.at[index])
        for index, (src, dst) in enumerate(
            (
                (r.gain_attn_hbm, r.gain_attn),
                (r.gain_ffn_hbm, r.gain_ffn),
                (r.down_left_hbm, r.down_left),
                (r.down_right_hbm, r.down_right),
                (r.up_left_hbm, r.up_left),
                (r.up_right_hbm, r.up_right),
                (r.down_bias_hbm, r.down_bias),
                (r.up_bias_hbm, r.up_bias),
            )
        )
    ]
    loads[0].start()
    small_loads[0].start()
    barrier = pltpu.get_barrier_semaphore()
    for offset in range(1, 8):
        pl.semaphore_signal(
            barrier,
            inc=1,
            device_id=(row_place, lax.rem(place + offset, 8)),
            device_id_type=MESH,
        )
    for offset in range(1, rows_size):
        pl.semaphore_signal(
            barrier,
            inc=1,
            device_id=(lax.rem(row_place + offset, rows_size), place),
            device_id_type=MESH,
        )

    for load in loads[1:4]:
        load.start()
    for load in small_loads[1:]:
        load.start()

    first_single = r.doc_lengths[0, 1] == 0
    loads[0].wait()
    small_loads[0].wait()
    gain_attn = r.gain_attn[...].reshape(1, 768)

    def normalized(row):
        values = r.x_rows[row].astype(f32)
        return (values * inverse_rms(values) * gain_attn).astype(bf16)

    r.x_rows[1] = jnp.where(first_single, x_raw[1], x_raw[0])
    my_block = pl.ds(pl.multiple_of(inner_place * LANES, LANES), LANES)
    r.normed_b[my_block, :] = normalized(1)
    pl.semaphore_wait(barrier, 7 + rows_size - 1)

    far_block = pl.ds(
        pl.multiple_of(((1 - parity) * 2 + core) * LANES, LANES), LANES
    )
    far_other = pl.ds(
        pl.multiple_of(((1 - parity) * 2 + 1 - core) * LANES, LANES), LANES
    )
    near_other = pl.ds(pl.multiple_of((parity * 2 + 1 - core) * LANES, LANES), LANES)
    to_partner = remote(
        r.normed_b.at[my_block],
        r.normed_b.at[my_block],
        r.normed_send.at[0],
        r.normed_recv.at[0],
        partner,
    )
    to_sibling = remote(
        r.normed_b.at[my_block],
        r.normed_b.at[my_block],
        r.normed_send.at[1],
        r.normed_recv.at[1],
        sibling,
    )
    onward = remote(
        r.normed_b.at[far_block],
        r.normed_b.at[far_block],
        r.normed_send.at[2],
        r.normed_recv.at[2],
        sibling,
    )
    to_partner.start()
    to_sibling.start()
    for load in loads[4:]:
        load.start()
    r.x_rows[0] = jnp.where(first_single, x_raw[0], x_raw[1])
    r.normed[...] = normalized(0)
    for load in loads[1:4]:
        load.wait()

    for part, weight in enumerate((r.w_query, r.w_key, r.w_value)):
        turned = dot_nn(r.normed[...], weight[...]).astype(bf16).T
        for head in range(12):
            r.qkv_send[head, part * 64 : (part + 1) * 64, :] = turned[head * 64 : (head + 1) * 64]

    far_half = 2 * (1 - half)
    chips = (far_half + parity, far_half + 1 - parity, 2 * half + 1 - parity, chip)

    def exchange(
        source, full, full_sem, split, split_place, split_sem, send_sem, order, start, kinds=range(4)
    ):
        for inside in order:
            for kind in kinds:
                to_chip = chips[kind]
                head = 3 * to_chip + inside
                if inside < 2:
                    dst, sem, to_core = full.at[place], full_sem, inside
                else:
                    dst, sem, to_core = split.at[split_place], split_sem, half

                def go(dst=dst, sem=sem, head=head, device=(row_place, to_chip * 2 + to_core)):
                    copy = remote(source.at[head], dst, send_sem.at[head], sem, device)
                    if start:
                        copy.start()
                    else:
                        copy.wait_send()

                if kind < 3:
                    go()
                    continue
                pl.when(core != to_core)(go)
                if start:

                    @pl.when(core == to_core)
                    def _(dst=dst, sem=sem, head=head):
                        pltpu.make_async_copy(source.at[head], dst, sem).start()

    def exchange_qkv(start, kinds=range(4)):
        exchange(
            r.qkv_send,
            r.slot_f,
            r.slot_f_sem,
            r.slot_c,
            place,
            r.slot_c_sem,
            r.qkv_sem,
            (2, 0, 1),
            start,
            kinds,
        )

    def exchange_do(start):
        exchange(
            do_send_a, r.do_f, r.do_f_sem, r.do_c, inner_place, r.do_c_sem, r.do_sem, (0, 1, 2), start
        )

    middle = (chip == 1) | (chip == 2)

    @pl.when(middle)
    def _():
        exchange_qkv(True, (1,))

    my_heads = pl.ds(pl.multiple_of(core * 384, 128), 384)
    near_chip = pl.ds(pl.multiple_of(parity * 512, 512), 512)
    far_chip = pl.ds(pl.multiple_of((1 - parity) * 512, 512), 512)

    def project_b(lines):
        r.keys_b[lines, :] = dot_nn(r.normed_b[lines, :], r.w_key[:, my_heads]).astype(bf16)
        r.values_b[lines, :] = dot_nn(r.normed_b[lines, :], r.w_value[:, my_heads]).astype(bf16)

    arrived(r.normed_b.at[near_other], r.normed_recv.at[1])
    r.queries_b[...] = (
        dot_nn(r.normed_b[near_chip, :], r.w_query[:, my_heads]).astype(bf16).T
    )
    project_b(near_chip)
    for load in small_loads[1:]:
        load.wait()
    gain_ffn = r.gain_ffn[...].reshape(1, 768)
    down_bias = r.down_bias[...].reshape(1, 48)
    up_bias = r.up_bias[...].reshape(1, 768)

    def make_bias(slot, _):
        head = jnp.where(
            slot == 0, 3 * chip + core, jnp.where(slot == 1, 3 * chip + 2, 6 * core + slot - 2)
        )
        offset = 256 - lax.broadcasted_iota(jnp.int32, (8, 512), 1)
        bucket = bucket_of(offset)
        line = jnp.zeros((8, 512), f32)
        for number in range(32):
            line = jnp.where(bucket == number, r.rel_table[head, number], line)
        spread = pltpu.roll(
            jnp.broadcast_to(line[:1], (128, 512)), 0, 1, stride=1, stride_axis=0
        )
        r.bias[slot, 0] = jnp.full((128, 128), r.rel_table[head, 15], f32)
        r.bias[slot, 1] = spread[:, 384:512]
        r.bias[slot, 2] = spread[:, 256:384]
        r.bias[slot, 3] = spread[:, 128:256]
        r.bias[slot, 4] = jnp.full((128, 128), r.rel_table[head, 31], f32)
        return 0

    lax.fori_loop(0, 8, make_bias, 0)

    zero64 = jnp.zeros((64, 1024), bf16)
    zero512 = jnp.zeros((64, 512), bf16)

    def biased(scores, first_key, lane_of):
        lines = []
        for upper in range(scores.shape[0] // 128):
            pieces = []
            for lane in range(8):
                slot, query = lane_of(lane)
                distance = first_key + upper - query
                if isinstance(distance, int):
                    distance = max(-2, min(2, distance)) + 2
                else:
                    distance = jnp.clip(distance, -2, 2) + 2
                pieces.append(
                    scores[upper * 128 : (upper + 1) * 128, lane * 128 : (lane + 1) * 128]
                    + r.bias[slot, distance]
                )
            lines.append(jnp.concatenate(pieces, axis=1))
        return jnp.concatenate(lines, axis=0)

    def attend_part(blocks, natural, spread_q, first_key, lane_of, weighted):
        peak = jnp.full((8, 1024), -1e30, f32)
        for block in range(blocks):
            lines = slice(block * 256, (block + 1) * 256)
            scores = biased(dot_nn(natural(block), spread_q), first_key + 2 * block, lane_of)
            r.wide[lines, :] = scores
            peak = jnp.maximum(peak, jnp.max(scores.reshape(32, 8, 1024), axis=0))
        peak = jnp.max(peak, axis=0, keepdims=True)
        total = jnp.zeros((64, 1024), f32)
        mass_sum = jnp.zeros((8, 1024), f32)
        for block in range(blocks):
            lines = slice(block * 256, (block + 1) * 256)
            weights = jnp.exp(r.wide[lines, :] - peak)
            mass_sum = mass_sum + jnp.sum(weights.reshape(32, 8, 1024), axis=0)
            total = total + weighted(block, weights.astype(bf16))
        return peak, jnp.sum(mass_sum, axis=0, keepdims=True), total

    def attend(blocks, natural, spread_q, lane_of, weighted, att, mass):
        peak, mass_sum, total = attend_part(blocks, natural, spread_q, 0, lane_of, weighted)
        total = total / mass_sum
        att[...] = total
        mass[...] = peak + jnp.log(mass_sum)
        return total

    def joined(slot, first, low, high):
        return jnp.concatenate([slot[first + u, low:high, :] for u in range(4)], axis=1)

    def lanes_b(pair):
        return lambda lane: (2 + 2 * pair + lane // 4, 4 * parity + lane % 4)

    def lanes_f(tile):
        return lambda lane: (0, 8 * tile + lane)

    def lanes_c(lane):
        return 1, 8 * core + lane

    def pair_lanes(pair):
        return pl.ds(pl.multiple_of(pair * 128, 128), 128)

    def spread_pair(first, second):
        return jnp.concatenate(
            [
                jnp.concatenate([first, zero512], axis=1),
                jnp.concatenate([zero512, second], axis=1),
            ],
            axis=0,
        )

    def pair_queries(pair):
        lines = pl.ds(pl.multiple_of(pair * 128, 128), 128)
        both = r.queries_b[lines, :]
        return spread_pair(both[:64], both[64:])

    def part_b(pair, side):
        lanes = pair_lanes(pair)

        def lines(block):
            return pl.ds(pl.multiple_of(side * 512 + block * 256, 256), 256)

        def weighted(block, weights):
            values = r.values_b[lines(block), lanes].T
            return jnp.concatenate(
                [
                    dot_nn(values[:64], weights[:, :512]),
                    dot_nn(values[64:], weights[:, 512:]),
                ],
                axis=1,
            )

        return attend_part(
            2,
            lambda block: r.keys_b[lines(block), lanes],
            pair_queries(pair),
            4 * side,
            lanes_b(pair),
            weighted,
        )

    def near_b(pair):
        r.mass_b[pair], r.sum_b[pair], r.att_b[pair] = part_b(pair, parity)

    def forward_b(pair):
        peak, mass_sum, total = part_b(pair, 1 - parity)
        near_peak = r.mass_b[pair]
        top = jnp.maximum(peak, near_peak)
        scale, near_scale = jnp.exp(peak - top), jnp.exp(near_peak - top)
        mass_sum = mass_sum * scale + r.sum_b[pair] * near_scale
        r.att_b[pair] = (total * scale + r.att_b[pair] * near_scale) / mass_sum
        r.mass_b[pair] = top + jnp.log(mass_sum)
        for upper in range(2):
            mine = pl.ds(pl.multiple_of(upper * 512 + core * 256, 256), 256)
            theirs = pl.ds(pl.multiple_of(upper * 512 + (1 - core) * 256, 256), 256)
            r.att_recv_b[6 * core + 2 * pair + upper] = r.att_b[pair, :, mine].astype(bf16)
            r.o_send_b[2 * pair + upper] = r.att_b[pair, :, theirs].astype(bf16)

    for pair in range(3):
        near_b(pair)

    arrived(r.normed_b.at[far_block], r.normed_recv.at[0])
    onward.start()

    @pl.when(middle)
    def _():
        exchange_qkv(True, (0, 2, 3))

    @pl.when(jnp.logical_not(middle))
    def _():
        exchange_qkv(True)

    lane48 = lax.broadcasted_iota(jnp.int32, (4, 48), 1)
    term = lax.broadcasted_iota(jnp.int32, (4, 48), 0)
    fold12 = (
        lax.rem(lax.broadcasted_iota(jnp.int32, (12, 48), 1), 12)
        == lax.broadcasted_iota(jnp.int32, (12, 48), 0)
    ).astype(f32)

    def rule_lines(transposed, outer):
        made = jnp.zeros((4, 48), f32)
        for number in range(4):
            for inner in range(4):
                value = (
                    r.phm_rule[number, inner, outer]
                    if transposed
                    else r.phm_rule[number, outer, inner]
                )
                made = jnp.where((term == number) & (lane48 // 12 == inner), value, made)
        return made

    down_rules = [rule_lines(False, outer) for outer in range(4)]
    up_rules = [rule_lines(True, outer) for outer in range(4)]
    down_right_wide = dot_nn(r.down_right[...], fold12, highest_p)
    up_left_wide = dot_nn(r.up_left[...], fold12, highest_p)
    down_left_t = r.down_left[...].T
    up_right_t = r.up_right[...].T
    for outer in range(4):
        r.down_b[outer * 192 : (outer + 1) * 192, :] = dot_nn(
            down_left_t, down_rules[outer] * down_right_wide, highest_p
        ).astype(bf16)
        r.up_b[outer * 192 : (outer + 1) * 192, :] = dot_nn(
            up_right_t, up_rules[outer] * up_left_wide, highest_p
        ).astype(bf16)

    loads[4].wait()
    r.ct_rows[0] = jnp.where(first_single, ct_raw[0], ct_raw[1])
    r.ct_rows[1] = jnp.where(first_single, ct_raw[1], ct_raw[0])

    arrived(r.normed_b.at[far_other], r.normed_recv.at[2])
    project_b(far_chip)

    for pair in range(3):
        forward_b(pair)
    o_to_sibling = remote(
        r.o_send_b, r.att_recv_b.at[pl.ds(6 * core, 6)], r.ob_send, r.ob_recv, sibling
    )
    o_to_sibling.start()

    def dense(row, recv, do_send):
        attended = recv[...].reshape(768, LANES).T
        values = r.x_rows[row].astype(f32) + dot_nn(attended, r.w_out[...])
        hidden[...] = values
        r.normed[...] = (values * inverse_rms(values) * gain_ffn).astype(bf16)
        for chunk in range(3):
            columns = slice(chunk * 1024, (chunk + 1) * 1024)
            value, slope = gelu_pair(dot_nn(r.normed[...], r.w_in[:, columns]))
            r.act[:, columns] = value.astype(bf16)
            r.wide[chunk * LANES : (chunk + 1) * LANES, :] = slope
        r.ff_out[...] = dot_nn(r.act[...], r.w_ffout[...]).astype(bf16)
        squeezed_act, squeezed_slope = gelu_pair(
            dot_nn(r.ff_out[...], r.down_b[...]) + down_bias
        )
        squeezed_act = squeezed_act.astype(bf16)
        squeezed_grad = dot_nn(r.ct_rows[row], r.up_b[...]) * squeezed_slope
        squeezed_low = squeezed_grad.astype(bf16)
        r.out_stage[0, row] = (
            hidden[...]
            + r.ff_out[...].astype(f32)
            + dot_nt(squeezed_act, r.up_b[...])
            + up_bias
        ).astype(bf16)
        pltpu.make_async_copy(
            r.out_stage.at[0, row], r.out_hbm.at[row], r.out_sem.at[row]
        ).start()
        r.ff_grad[...] = (
            r.ct_rows[row].astype(f32) + dot_nt(squeezed_low, r.down_b[...])
        ).astype(bf16)
        for chunk in range(3):
            columns = slice(chunk * 1024, (chunk + 1) * 1024)
            r.act[:, columns] = (
                dot_nt(r.ff_grad[...], r.w_ffout[columns, :])
                * r.wide[chunk * LANES : (chunk + 1) * LANES, :]
            ).astype(bf16)
        normed_grad = dot_nt(r.act[...], r.w_in[...])
        values = r.ct_rows[row].astype(f32) + norm_back(hidden[...], gain_ffn, normed_grad)
        r.hidden_grad[row] = values
        turned = dot_nt(values.astype(bf16), r.w_out[...]).astype(bf16).T
        do_send[...] = turned.reshape(12, 64, LANES)
        return squeezed_act, squeezed_low, squeezed_grad

    def adapter_sums(row, squeezed_act, squeezed_low, squeezed_grad, first):
        up_part = dot_nn(r.ct_rows[row].T, squeezed_act)
        down_part = dot_nn(r.ff_out[...].T, squeezed_low)
        down_sum = jnp.sum(squeezed_grad, axis=0, keepdims=True)
        up_sum = jnp.sum(r.ct_rows[row].astype(f32), axis=0, keepdims=True)
        if first:
            r.up_grad[...] = up_part
            r.down_grad[...] = down_part
            r.bias_grad[0:1, 0:48] = down_sum
            r.bias_grad[1:2, :] = up_sum
        else:
            r.up_grad[...] += up_part
            r.down_grad[...] += down_part
            r.bias_grad[0:1, 0:48] += down_sum
            r.bias_grad[1:2, :] += up_sum

    for load in loads[5:]:
        load.wait()
    arrived(r.att_recv_b.at[pl.ds(6 * (1 - core), 6)], r.ob_recv)
    adapter_sums(1, *dense(1, r.att_recv_b, do_send_b), True)
    o_to_sibling.wait_send()
    do_to_sibling = remote(
        do_send_b.at[pl.ds(6 * (1 - core), 6)], r.do_b.at[core], r.dob_send, r.dob_recv, sibling
    )
    do_to_sibling.start()
    r.do_b[core] = do_send_b[pl.ds(6 * core, 6)]

    arrived(r.slot_c.at[pl.ds(4 * core, 4)], r.slot_c_sem)
    pass_c = remote(
        r.slot_c.at[pl.ds(4 * core, 4), pl.ds(64, 128)],
        r.slot_c.at[pl.ds(4 * core, 4), pl.ds(64, 128)],
        r.pass_c_send,
        r.pass_c_recv,
        sibling,
    )
    pass_c.start()
    def turn_slot(slot, natural, first, count):
        for u in range(count):
            lines = pl.ds(pl.multiple_of((first + u) * 256, 256), 256)
            natural[lines, :] = slot[first + u, 64:192, :].T

    def send_back(source, first, index, dst, send_sem, sem, start):
        def away():
            copy = remote(source, dst, send_sem, sem, (row_place, index))
            if start:
                copy.start()
            else:
                copy.wait_send()

        pl.when(index != place)(away)
        if start:

            @pl.when(index == place)
            def _():
                pltpu.make_async_copy(source, dst, sem).start()

    def send_o_f(tile, start):
        for u in range(4):
            index = 4 * tile + u
            send_back(
                r.o_send_f.at[index],
                None,
                index,
                r.att_recv_a.at[3 * chip + core],
                r.of_send.at[index],
                r.att_sem,
                start,
            )

    def send_o_c(start):
        for u in range(4):
            send_back(
                r.o_send_c.at[u],
                None,
                4 * core + u,
                r.att_recv_a.at[3 * chip + 2],
                r.oc_send.at[u],
                r.att_sem,
                start,
            )

    def back_block(first, second, spread_q, spread_do, first_key, lane_of, log_mass, delta):
        scores = biased(dot_nn(first, spread_q), first_key, lane_of)
        probs = jnp.exp(scores - log_mass)
        score_grad = probs * (dot_nn(second, spread_do) - delta)
        return probs.astype(bf16), score_grad.astype(bf16)

    def backward_b(pair):
        lanes = pair_lanes(pair)
        grads = [
            jnp.concatenate([r.do_b[0, 2 * pair + upper], r.do_b[1, 2 * pair + upper]], axis=1)
            for upper in range(2)
        ]
        delta = jnp.sum(
            jnp.concatenate(grads, axis=1).astype(f32) * r.att_b[pair], axis=0, keepdims=True
        )
        spread_q = pair_queries(pair)
        spread_do = spread_pair(*grads)
        turned_z[0][0][...] = spread_q.T
        turned_z[0][1][...] = spread_do.T
        dq = jnp.zeros((128, 1024), f32)
        for block in range(2):
            lines = slice(block * 512, (block + 1) * 512)
            keys = r.keys_b[lines, lanes]
            probs, score_grad = back_block(
                keys,
                r.values_b[lines, lanes],
                spread_q,
                spread_do,
                4 * block,
                lanes_b(pair),
                r.mass_b[pair],
                delta,
            )
            dq = dq + dot_nn(keys.T, score_grad)
            r.keys_b[lines, lanes] = dot_nn(score_grad, turned_z[0][0][...]).astype(bf16)
            r.values_b[lines, lanes] = dot_nn(probs, turned_z[0][1][...]).astype(bf16)
        first = pl.ds(pl.multiple_of(pair * 128, 64), 64)
        second = pl.ds(pl.multiple_of(pair * 128 + 64, 64), 64)
        r.queries_b[first, :] = dq[:64, :512].astype(bf16)
        r.queries_b[second, :] = dq[64:, 512:].astype(bf16)

    for copy in (to_partner, to_sibling, onward):
        copy.wait_send()
    arrived(r.do_b.at[1 - core], r.dob_recv)
    arrived(r.slot_c.at[pl.ds(4 * (1 - core), 4), pl.ds(64, 128)], r.pass_c_recv)
    turn_slot(r.slot_c, r.natural_c, 0, 8)
    total = attend(
        8,
        lambda block: r.natural_c[block * 256 : (block + 1) * 256, :],
        jnp.concatenate([joined(r.slot_c, 4 * core, 0, 64), zero64], axis=0),
        lanes_c,
        lambda block, weights: dot_nn(r.slot_c[block, 128:192, :], weights),
        r.att_c.at[0],
        r.mass_c.at[0],
    )
    for u in range(4):
        r.o_send_c[u] = total[:, u * 256 : (u + 1) * 256].astype(bf16)
    send_o_c(True)

    arrived(r.slot_f, r.slot_f_sem)
    turn_slot(r.slot_f, r.natural_f, 0, 8)

    def forward_f(tile):
        total = attend(
            8,
            lambda block: r.natural_f[block * 256 : (block + 1) * 256, :],
            jnp.concatenate([joined(r.slot_f, 4 * tile, 0, 64), zero64], axis=0),
            lanes_f(tile),
            lambda block, weights: dot_nn(r.slot_f[block, 128:192, :], weights),
            r.att_f.at[tile],
            r.mass_f.at[tile],
        )
        for u in range(4):
            r.o_send_f[4 * tile + u] = total[:, u * 256 : (u + 1) * 256].astype(bf16)
        send_o_f(tile, True)

    for tile in (1 - half, half):
        forward_f(tile)

    backward_b(0)

    arrived(r.att_recv_a, r.att_sem)
    kept = dense(0, r.att_recv_a, do_send_a)
    exchange_qkv(False)
    exchange_do(True)

    backward_b(1)
    backward_b(2)

    def project_back(lines):
        return dot_nt(r.keys_b[lines, :], r.w_key[:, my_heads]) + dot_nt(
            r.values_b[lines, :], r.w_value[:, my_heads]
        )

    my_half = pl.ds(pl.multiple_of(core * LANES, LANES), LANES)
    their_half = pl.ds(pl.multiple_of((1 - core) * LANES, LANES), LANES)
    part_far[...] = project_back(far_block)
    part_send[0][...] = project_back(far_other).astype(bf16)
    far_copy = remote(
        part_send[0], r.part_recv.at[0], r.part_send_sem.at[0], r.part_recv_sem.at[0], sibling
    )
    far_copy.start()

    def set_tile(slot_index, queries, grads):
        spread_q = jnp.concatenate([queries, zero64], axis=0)
        spread_do = jnp.concatenate([zero64, grads], axis=0)
        turned_z[slot_index][0][...] = spread_q.T
        turned_z[slot_index][1][...] = spread_do.T
        return spread_q, spread_do

    def merged(score_grad, probs, slot_index):
        queries, grads = turned_z[slot_index]
        return dot_nn(score_grad, queries[...]) + dot_nn(probs, grads[...])

    def key_lines(block):
        return pl.ds(pl.multiple_of(block * 512, 512), 512)

    def keys_t(slot, block):
        return jnp.concatenate([slot[2 * block + u, 64:128, :] for u in range(2)], axis=1)

    arrived(r.do_f, r.do_f_sem)
    deltas = []
    spreads = []
    for tile in range(2):
        grads = joined(r.do_f, 4 * tile, 0, 64)
        spreads.append(set_tile(tile, joined(r.slot_f, 4 * tile, 0, 64), grads))
        deltas.append(jnp.sum(grads.astype(f32) * r.att_f[tile], axis=0, keepdims=True))
        dq_acc[tile][...] = jnp.zeros((64, 1024), f32)

    def send_g_f(index, start):
        send_back(
            r.slot_f.at[index, pl.ds(64, 128)],
            None,
            index,
            g_recv.at[3 * chip + core, pl.ds(64, 128)],
            r.gkv_send.at[index],
            r.g_sem,
            start,
        )

    def send_dq_f(index, start):
        send_back(
            r.slot_f.at[index, pl.ds(0, 64)],
            None,
            index,
            g_recv.at[3 * chip + core, pl.ds(0, 64)],
            r.gq_send.at[index],
            r.g_sem,
            start,
        )

    def whole_block(block):
        natural = r.natural_f[key_lines(block), :]
        turned_keys = keys_t(r.slot_f, block)
        made = jnp.zeros((512, 128), f32)
        for tile in range(2):
            probs, score_grad = back_block(
                natural,
                natural,
                *spreads[tile],
                4 * block,
                lanes_f(tile),
                r.mass_f[tile],
                deltas[tile],
            )
            dq_acc[tile][...] += dot_nn(turned_keys, score_grad)
            made = made + merged(score_grad, probs, tile)
        turned = made.astype(bf16).T
        for u in range(2):
            r.slot_f[2 * block + u, 64:192, :] = turned[:, u * 256 : (u + 1) * 256]
            send_g_f(2 * block + u, True)

    def whole_piece(piece):
        natural = r.natural_f[pl.ds(pl.multiple_of(piece * 256, 256), 256), :]
        made = jnp.zeros((256, 128), f32)
        for tile in range(2):
            probs, score_grad = back_block(
                natural,
                natural,
                *spreads[tile],
                2 * piece,
                lanes_f(tile),
                r.mass_f[tile],
                deltas[tile],
            )
            dq_acc[tile][...] += dot_nn(r.slot_f[piece, 64:128, :], score_grad)
            made = made + merged(score_grad, probs, tile)
        r.slot_f[piece, 64:192, :] = made.astype(bf16).T
        send_g_f(piece, True)

    for step in range(4):
        whole_piece(2 * far_half + step)
        if step == 1:
            arrived(r.part_recv.at[0], r.part_recv_sem.at[0])
            part_send[2][...] = (part_far[...] + r.part_recv[0].astype(f32)).astype(bf16)
            partner_copy = remote(
                part_send[2], r.part_recv.at[2], r.part_send_sem.at[2], r.part_recv_sem.at[2], partner
            )
            partner_copy.start()
    for step in range(2):
        whole_block(2 * half + step)
    for step in range(8):
        index = 4 * (1 - half) + step if step < 4 else 4 * half + step - 4
        r.slot_f[index, 0:64, :] = r.wide[
            pl.ds(pl.multiple_of(512 + 64 * (1 - half if step < 4 else half), 64), 64),
            (step % 4) * 256 : (step % 4 + 1) * 256,
        ].astype(bf16)
        send_dq_f(index, True)

    arrived(r.do_c, r.do_c_sem)
    grads_c = joined(r.do_c, 0, 0, 64)
    spread_qc, spread_doc = set_tile(0, joined(r.slot_c, 4 * core, 0, 64), grads_c)
    delta_c = jnp.sum(grads_c.astype(f32) * r.att_c[0], axis=0, keepdims=True)
    dq_acc[0][...] = jnp.zeros((64, 1024), f32)

    def split_block(block):
        natural = r.natural_c[key_lines(block), :]
        probs, score_grad = back_block(
            natural, natural, spread_qc, spread_doc, 4 * block, lanes_c, r.mass_c[0], delta_c
        )
        dq_acc[0][...] += dot_nn(keys_t(r.slot_c, block), score_grad)
        return merged(score_grad, probs, 0)

    def split_theirs(step):
        turned = split_block(2 * (1 - core) + step).astype(bf16).T
        for u in range(2):
            r.c_send[2 * step + u] = turned[:, u * 256 : (u + 1) * 256]

    def split_mine(step):
        dkv_own[key_lines(step), :] = split_block(2 * core + step)

    for step in range(2):
        split_theirs(step)
    c_copy = remote(r.c_send, r.c_recv, r.c_send_sem, r.c_recv_sem, sibling)
    c_copy.start()
    for step in range(2):
        split_mine(step)

    arrived(r.c_recv, r.c_recv_sem)

    def send_g_c(start):
        for u in range(4):
            send_back(
                r.slot_c.at[4 * core + u],
                None,
                4 * core + u,
                g_recv.at[3 * chip + 2],
                r.gc_send.at[u],
                r.g_sem,
                start,
            )

    pass_c.wait_send()
    for u in range(4):
        r.slot_c[4 * core + u, 0:64, :] = dq_acc[0][:, u * 256 : (u + 1) * 256].astype(bf16)
        r.slot_c[4 * core + u, 64:192, :] = (
            dkv_own[u * 256 : (u + 1) * 256, :].T + r.c_recv[u].astype(f32)
        ).astype(bf16)
    send_g_c(True)

    adapter_sums(0, *kept, False)

    column48 = lax.broadcasted_iota(jnp.int32, (48, 16), 0) // 12
    lane16 = lax.broadcasted_iota(jnp.int32, (48, 16), 1)

    def kron_back(grad, left, right_wide, rules, transposed):
        left_grad = jnp.zeros((4, 192), f32)
        right_grad = jnp.zeros((4, 48), f32)
        rule_grad = jnp.zeros((4, 16), f32)
        for outer in range(4):
            block = grad[outer * 192 : (outer + 1) * 192, :]
            left_grad = left_grad + dot_nt(rules[outer] * right_wide, block, highest_p)
            contracted = dot_nn(left, block, highest_p)
            right_grad = right_grad + contracted * rules[outer]
            target = column48 * 4 + outer if transposed else outer * 4 + column48
            rule_grad = rule_grad + dot_nn(
                contracted * right_wide, (target == lane16).astype(f32), highest_p
            )
        return left_grad, dot_nt(right_grad, fold12, highest_p), rule_grad

    dl_grad, dr_grad, rule_down = kron_back(
        r.down_grad, r.down_left[...], down_right_wide, down_rules, False
    )
    ur_grad, ul_grad, rule_up = kron_back(
        r.up_grad, r.up_right[...], up_left_wide, up_rules, True
    )
    r.stats[...] = jnp.zeros_like(r.stats)
    r.stats[0:4, 0:192] = dl_grad
    r.stats[4:8, 0:192] = ur_grad
    r.stats[8:12, 0:12] = dr_grad
    r.stats[8:12, 128:140] = ul_grad
    r.stats[12:16, 0:16] = rule_down + rule_up
    r.stats[16:17, 0:48] = r.bias_grad[0:1, 0:48]
    for third in range(3):
        r.stats[17 + third : 18 + third, :] = r.bias_grad[1:2, third * 256 : (third + 1) * 256]

    def rows_copy(offset):
        return remote(
            r.stats,
            r.stats_rows.at[row_place],
            r.st_rows_send.at[offset - 1],
            r.st_rows_recv.at[offset - 1],
            (lax.rem(row_place + offset, rows_size), place),
        )

    for offset in range(1, rows_size):
        rows_copy(offset).start()
    r.stats_rows[row_place] = r.stats[...]

    part_send[1][...] = (
        project_back(near_other)
        + dot_nt(r.queries_b[:, their_half].T, r.w_query[:, my_heads])
    ).astype(bf16)
    near_copy = remote(
        part_send[1], r.part_recv.at[1], r.part_send_sem.at[1], r.part_recv_sem.at[1], sibling
    )
    near_copy.start()

    def finish_row(row, normed_grad):
        r.out_stage[1, row] = (
            r.hidden_grad[row] + norm_back(r.x_rows[row].astype(f32), gain_attn, normed_grad)
        ).astype(bf16)
        pltpu.make_async_copy(
            r.out_stage.at[1, row], r.grad_hbm.at[row], r.out_sem.at[2 + row]
        ).start()

    part_own[...] = project_back(my_block) + dot_nt(
        r.queries_b[:, my_half].T, r.w_query[:, my_heads]
    )

    my_lanes = pl.ds(pl.multiple_of(core * 128, 128), 128)
    other_lanes = pl.ds(pl.multiple_of((1 - core) * 128, 128), 128)
    for offset in range(1, rows_size):
        rows_copy(offset).wait()
    summed = r.stats_rows[0]
    for number in range(1, rows_size):
        summed = summed + r.stats_rows[number]
    r.stats_core[0] = summed
    core_copy = remote(
        r.stats_core.at[0, :, other_lanes],
        r.stats_core.at[1, :, other_lanes],
        r.st_core_send,
        r.st_core_recv,
        sibling,
    )
    core_copy.start()

    core_copy.wait_send()
    arrived(r.stats_core.at[1, :, my_lanes], r.st_core_recv)
    r.stats_z[chip] = r.stats_core[0, :, my_lanes] + r.stats_core[1, :, my_lanes]

    def z_copy(offset):
        return remote(
            r.stats_z.at[chip],
            r.stats_z.at[chip],
            r.st_z_send.at[offset - 1],
            r.st_z_recv.at[offset - 1],
            (row_place, lax.rem(chip + offset, 4) * 2 + core),
        )

    for offset in range(1, 4):
        z_copy(offset).start()

    arrived(r.part_recv.at[1], r.part_recv_sem.at[1])
    arrived(r.part_recv.at[2], r.part_recv_sem.at[2])
    finish_row(
        1, part_own[...] + r.part_recv[1].astype(f32) + r.part_recv[2].astype(f32)
    )

    for offset in range(1, 4):
        z_copy(offset).wait()
    r.stats_core[2, :, my_lanes] = (r.stats_z[0] + r.stats_z[1]) + (r.stats_z[2] + r.stats_z[3])
    last_copy = remote(
        r.stats_core.at[2, :, my_lanes],
        r.stats_core.at[2, :, my_lanes],
        r.st_last_send,
        r.st_last_recv,
        sibling,
    )
    last_copy.start()

    for copy in (do_to_sibling, c_copy, far_copy, near_copy, partner_copy):
        copy.wait_send()
    exchange_do(False)
    for tile in range(2):
        send_o_f(tile, False)
    send_o_c(False)
    for row in range(2):
        pltpu.make_async_copy(
            r.out_stage.at[0, row], r.out_hbm.at[row], r.out_sem.at[row]
        ).wait()
    arrived(g_recv, r.g_sem)
    turned_grad = jnp.zeros((768, LANES), f32)
    for part, weight in enumerate((r.w_query, r.w_key, r.w_value)):
        turned_grad = turned_grad + dot_nn(
            weight[...], g_recv[:, part * 64 : (part + 1) * 64, :].reshape(768, LANES)
        )
    finish_row(0, turned_grad.T)
    last_copy.wait_send()
    arrived(r.stats_core.at[2, :, other_lanes], r.st_last_recv)
    write_stats = pltpu.make_async_copy(r.stats_core.at[2], r.stats_out, r.stats_out_sem)
    write_stats.start()

    write_stats.wait()
    send_g_c(False)
    for index in range(8):
        send_g_f(index, False)
        send_dq_f(index, False)
    for row in range(2):
        pltpu.make_async_copy(
            r.out_stage.at[1, row], r.grad_hbm.at[row], r.out_sem.at[2 + row]
        ).wait()


def finish_kernel(
    doc_lengths,
    stats_from,
    out_from,
    grad_from,
    out_to,
    grad_to,
    rule_out,
    dl_out,
    dr_out,
    ul_out,
    ur_out,
    db_out,
    ub_out,
    stage,
    stats,
    rule_made,
    wide_made,
    narrow_made,
    db_made,
    ub_made,
    sem,
    stats_sem,
    small_sem,
):
    gets, puts = [], []
    first_single = doc_lengths[0, 1] == 0
    for number, (source, target) in enumerate(((grad_from, grad_to), (out_from, out_to))):
        for row in range(2):
            to_row = jnp.where(first_single, row, 1 - row)
            gets.append(
                pltpu.make_async_copy(
                    source.at[row], stage.at[number, row], sem.at[0, number, row]
                )
            )
            puts.append(
                pltpu.make_async_copy(
                    stage.at[number, row], target.at[to_row], sem.at[1, number, row]
                )
            )
    get_stats = pltpu.make_async_copy(stats_from, stats, stats_sem)
    get_stats.start()
    for get in gets:
        get.start()
    get_stats.wait()
    for outer in range(4):
        rule_made[:, outer, :] = stats[12:16, 4 * outer : 4 * outer + 4]
    wide_made[0] = stats[0:4, 0:192]
    wide_made[1] = stats[4:8, 0:192]
    narrow_made[0] = stats[8:12, 0:12]
    narrow_made[1] = stats[8:12, 128:140]
    db_made[...] = stats[16:17, 0:48].reshape(48)
    ub_made[...] = jnp.concatenate(
        [stats[17 + third : 18 + third, :] for third in range(3)], axis=1
    ).reshape(768)
    small = [
        pltpu.make_async_copy(source, target, small_sem.at[number])
        for number, (source, target) in enumerate(
            (
                (rule_made, rule_out),
                (wide_made.at[0], dl_out),
                (narrow_made.at[0], dr_out),
                (narrow_made.at[1], ul_out),
                (wide_made.at[1], ur_out),
                (db_made, db_out),
                (ub_made, ub_out),
            )
        )
    ]
    for copy in small:
        copy.start()
    for get, put in zip(gets, puts):
        get.wait()
        put.start()
    for copy in small + puts:
        copy.wait()


def layer_on_slice(rows_size, *arrays):
    (
        inputs,
        doc_lengths,
        w_query,
        w_key,
        w_value,
        w_out,
        w_in,
        w_ffout,
        rel_table,
        gain_attn,
        gain_ffn,
        phm_rule,
        down_left,
        down_right,
        up_left,
        up_right,
        down_bias,
        up_bias,
        cotangent,
    ) = arrays
    f32 = jnp.float32
    bf16 = jnp.bfloat16
    shape = jax.ShapeDtypeStruct
    vmem = pl.BlockSpec(memory_space=pltpu.VMEM)
    smem = pl.BlockSpec(memory_space=pltpu.SMEM)
    hbm = pl.BlockSpec(memory_space=pl.ANY)
    dma = pltpu.SemaphoreType.DMA
    results = pl.pallas_call(
        functools.partial(layer_kernel, rows_size),
        out_shape=[
            shape(inputs.shape, bf16),
            shape(inputs.shape, bf16),
            shape((24, 256), f32),
        ],
        in_specs=[smem] * 3 + [hbm] * 16,
        out_specs=[hbm] * 3,
        scratch_shapes=[
            pltpu.VMEM(tuple(rows_size if size is None else size for size in sizes), kind)
            for sizes, kind in SCRATCH
        ]
        + [dma(sizes) for sizes in SEMAPHORES],
        compiler_params=pltpu.CompilerParams(
            collective_id=0, has_side_effects=True, vmem_limit_bytes=56 * 1024 * 1024
        ),
        name="encoder_layer",
    )(
        doc_lengths,
        rel_table.T,
        phm_rule,
        gain_attn,
        gain_ffn,
        down_left,
        down_right,
        up_left,
        up_right,
        down_bias,
        up_bias,
        inputs,
        cotangent,
        w_query,
        w_key,
        w_value,
        w_out,
        w_in,
        w_ffout,
    )
    return pl.pallas_call(
        finish_kernel,
        out_shape=[
            shape(inputs.shape, bf16),
            shape(inputs.shape, bf16),
            shape(phm_rule.shape, f32),
            shape((4, 192), f32),
            shape((4, 12), f32),
            shape((4, 12), f32),
            shape((4, 192), f32),
            shape((48,), f32),
            shape((768,), f32),
        ],
        in_specs=[smem] + [hbm] * 3,
        out_specs=[hbm] * 9,
        scratch_shapes=[
            pltpu.VMEM((2, 2, LANES, 768), bf16),
            pltpu.VMEM((24, 256), f32),
            pltpu.VMEM((4, 4, 4), f32),
            pltpu.VMEM((2, 4, 192), f32),
            pltpu.VMEM((2, 4, 12), f32),
            pltpu.VMEM((48,), f32),
            pltpu.VMEM((768,), f32),
            dma((2, 2, 2)),
            dma(()),
            dma((7,)),
        ],
        name="finish",
    )(doc_lengths, results[2], results[0], results[1])


def pick(rows_size, seq_size, *arrays):
    inputs, doc_lengths = arrays[:2]
    fits = (
        seq_size == 8
        and inputs.shape == (2, LANES, 768)
        and doc_lengths.shape == (2, 2)
        and arrays[8].shape == (32, 12)
        and arrays[6].shape == (768, 3072)
    )
    return layer_on_slice(rows_size, *arrays) if fits else local(*arrays)


def solution(mesh):
    return jax.shard_map(
        functools.partial(pick, mesh.shape["rows"], mesh.shape["seq"]),
        mesh=mesh,
        in_specs=(
            P("rows", "seq", None),
            P("rows", None),
            P(),
            P(),
            P(),
            P(),
            P(),
            P(),
            P(),
            P(),
            P(),
            P(),
            P(),
            P(),
            P(),
            P(),
            P(),
            P(),
            P("rows", "seq", None),
        ),
        out_specs=(
            P("rows", "seq", None),
            P("rows", "seq", None),
            P(),
            P(),
            P(),
            P(),
            P(),
            P(),
            P(),
        ),
        check_vma=False,
    )
```
